32 devices in a mesh: slab: 4 (over x, core), mapx: 4 (over z), mapy: 2 (over y).
Axes of the slice: x: 2, y: 2, z: 4, core: 2. Of those that a mesh axis runs over, the one named last changes fastest.
Arguments:
- pressure: float32 [32, 384, 512], P('slab', 'mapx', 'mapy'), may hold values from -2 to 2
- porosity: float32 [32, 384, 512], P('slab', 'mapx', 'mapy'), may hold values from 0.1 to 0.5
- lithology: int32 [32, 384, 512], P('slab', 'mapx', 'mapy'), may hold values from 0 to 3
- layer_solid: float32 [32], P('slab'), may hold values from 0.05 to 0.15
Outputs:
- pressure_new: float32 [32, 384, 512], P('slab', 'mapx', 'mapy')
- porosity_new: float32 [32, 384, 512], P('slab', 'mapx', 'mapy')
- thickness_new: float32 [32, 384, 512], P('slab', 'mapx', 'mapy')
The draws below stay inside these ranges and needn't reach their ends.
All inputs are finite; a program needn't handle non-finite values.
Results may differ from the reference program's by a relative error of at most 0.00015.
Values sent between devices are 32-bit elements; how exact they have to be, the bound alone decides.
A program may use at most 64 MiB of HBM per device.

```python
import jax
import jax.numpy as jnp

NCLASS = 4
NZ = 32
NX = 384
NY = 512


def plant(entries, stream_key, least, top_value):
    extent = entries.shape
    index_at = [jax.random.randint(jax.random.fold_in(stream_key, axis), (), 0, extent[axis]) for axis in range(len(extent))]
    entries = entries.at[tuple(index_at)].set(least)
    longest = extent.index(max(extent))
    index_at[longest] = (index_at[longest] + 1) % extent[longest]
    return entries.at[tuple(index_at)].set(top_value)


def block_scale(key, dims, cuts, least, top_value):
    loudness = 1.0
    for dim, blocks in cuts:
        heights = jax.random.uniform(jax.random.fold_in(jax.random.fold_in(key, 6), dim), (blocks,), jnp.float32, least / len(cuts), top_value / len(cuts))
        loudness = loudness * jnp.repeat(jnp.exp(heights), dims[dim] // blocks).reshape((-1,) + (1,) * (len(dims) - 1 - dim))
    return loudness


def gaussian(key, shape, width, reach, cuts=(), kind=jnp.bfloat16):
    loudness = block_scale(key, shape, cuts, -0.22, 0.18) if cuts else 1.0
    array = jax.random.normal(key, shape, jnp.float32) * width * loudness
    return jnp.minimum(jnp.maximum(array, -reach), reach).astype(kind)


def setup_inputs(seed: int = 0) -> dict:
    streams_of = jax.random.split(jax.random.key(seed), 5)
    pressure = gaussian(streams_of[0], (NZ, NX, NY), 0.4, 2.0, ((0, 4), (1, 4), (2, 2)), jnp.float32)
    porosity = jnp.clip(0.1 + 0.4 * jax.random.uniform(streams_of[1], (NZ, NX, NY), jnp.float32) ** block_scale(streams_of[1], (NZ, NX, NY), ((0, 4), (1, 4), (2, 2)), -0.2, 0.2), 0.1, 0.5)
    lithology = plant(jax.random.randint(streams_of[2], (NZ, NX, NY), 0, NCLASS), jax.random.fold_in(streams_of[2], 1), 0, NCLASS - 1).astype(jnp.int32)
    layer_solid = jnp.clip(0.05 + 0.10000001 * jax.random.uniform(streams_of[3], (NZ,), jnp.float32) ** block_scale(streams_of[3], (NZ,), ((0, 4),), -0.2, 0.2), 0.05, 0.15)
    return {"pressure": pressure, "porosity": porosity, "lithology": lithology, "layer_solid": layer_solid}


PHI_SURFACE = (0.45, 0.55, 0.65, 0.40)
ATHY_RATE = (0.25, 0.45, 0.8, 0.35)
MOB_BASE = (1.0, 0.0, -1.5, -0.5)
MOB_SLOPE = (6.0, 5.0, 8.0, 4.0)
GRAIN_DENSITY = (2.65, 2.68, 2.72, 2.71)
WATER_DENSITY = 1.03
SPECTRUM_MID = 1.0
SPECTRUM_HALF = 0.95
SIGMA_RATIO = SPECTRUM_MID / SPECTRUM_HALF
RHO_FIRST = 1.0 / SIGMA_RATIO
RHO_SECOND = 1.0 / (2.0 * SIGMA_RATIO - RHO_FIRST)


def lookup(lithology, table):
    result = jnp.zeros(lithology.shape, jnp.float32)
    for index, entry in enumerate(table):
        result = result + jnp.where(lithology == index, jnp.float32(entry), jnp.float32(0.0))
    return result


def neighbours(padded):
    return [padded[2:, 1:-1, 1:-1], padded[:-2, 1:-1, 1:-1],
            padded[1:-1, 2:, 1:-1], padded[1:-1, :-2, 1:-1],
            padded[1:-1, 1:-1, 2:], padded[1:-1, 1:-1, :-2]]


def apply_operator(trans, field):
    result = field
    for weight, beside in zip(trans, neighbours(jnp.pad(field, 1))):
        result = result + weight * (field - beside)
    return result


def reference(pressure, porosity, lithology, layer_solid):
    mobility = jnp.exp(lookup(lithology, MOB_BASE) + lookup(lithology, MOB_SLOPE) * (porosity - 0.35))
    trans = [2.0 * mobility * other / (mobility + other) for other in neighbours(jnp.pad(mobility, 1))]
    diag = 1.0 + trans[0] + trans[1] + trans[2] + trans[3] + trans[4] + trans[5]
    first_res = pressure - apply_operator(trans, pressure)
    first_step = first_res / (SPECTRUM_MID * diag)
    middle = pressure + first_step
    second_res = pressure - apply_operator(trans, middle)
    second_step = RHO_SECOND * RHO_FIRST * first_step + (2.0 * RHO_SECOND / SPECTRUM_HALF) * second_res / diag
    pressure_new = middle + second_step
    solid = layer_solid[:, None, None]
    load = (lookup(lithology, GRAIN_DENSITY) + WATER_DENSITY * porosity / (1.0 - porosity)) * solid
    overburden = jnp.cumsum(load, axis=0) - 0.5 * load
    stress = jnp.maximum(overburden - pressure_new, 0.0)
    porosity_new = lookup(lithology, PHI_SURFACE) * jnp.exp(-lookup(lithology, ATHY_RATE) * stress)
    thickness_new = solid / (1.0 - porosity_new)
    return pressure_new, porosity_new, thickness_new
```

```python
import functools
import math

import jax
import jax.numpy as jnp
from jax import lax
from jax.experimental import pallas as pl
from jax.experimental.pallas import tpu as pltpu
from jax.sharding import PartitionSpec as P

PHI_SURFACE = (0.45, 0.55, 0.65, 0.4)
ATHY_RATE = (0.25, 0.45, 0.8, 0.35)
MOB_BASE = (1.0, 0.0, -1.5, -0.5)
MOB_SLOPE = (6.0, 5.0, 8.0, 4.0)
GRAIN_DENSITY = (2.65, 2.68, 2.72, 2.71)
WATER_DENSITY = 1.03
SPECTRUM_MID = 1.0
SPECTRUM_HALF = 0.95
SIGMA_RATIO = SPECTRUM_MID / SPECTRUM_HALF
RHO_FIRST = 1.0 / SIGMA_RATIO
RHO_SECOND = 1.0 / (2.0 * SIGMA_RATIO - RHO_FIRST)
STEP_KEEP = RHO_SECOND * RHO_FIRST
STEP_RES = 2.0 * RHO_SECOND / SPECTRUM_HALF

HALF_BASE = tuple(-(b - 0.35 * s) - math.log(2.0) for b, s in zip(MOB_BASE, MOB_SLOPE))
HALF_SLOPE = tuple(-s for s in MOB_SLOPE)
GRAIN_LESS = tuple(g - WATER_DENSITY for g in GRAIN_DENSITY)
ATHY_NEG = tuple(-a for a in ATHY_RATE)
OUTSIDE = 2.0e38

MESH = pl.DeviceIdType.MESH
PAD = 8
ROWS = 16
Z_P, Z_H, X_1, Y_1, Z_Q, X_Q, Y_Q, CHAIN = 0, 2, 4, 6, 8, 10, 12, 14
MESSAGES = 15


def rec(x):
    r = pl.reciprocal(x, approx=True)
    return r * (2.0 - x * r)


def classes(lith):
    return lith >= 2, (lith & 1) == 1


def pick(cls, table):
    high, odd = cls
    a, b, c, d = (jnp.float32(t) for t in table)
    return jnp.where(high, jnp.where(odd, d, c), jnp.where(odd, b, a))


def kernel(sizes, p_hbm, por_hbm, lit_hbm, solid, pn_out, phi_out, thick_out,
           pv, hv, qv, tz, tx, tym, typ, rd, ob, por, lit, col, col_send, above,
           xs, xr, ys, yr, xqs, xqr, yqs, yqr, load_sem, send_sem, recv_sem):
    nz, nx, ny = por.shape
    axes = ("slab", "mapx", "mapy")
    me = {a: lax.axis_index(a) for a in axes}
    has_lo = {a: me[a] > 0 for a in axes}
    has_hi = {a: me[a] < sizes[a] - 1 for a in axes}
    peers = sum(jnp.where(f, 1, 0) for flags in (has_lo, has_hi) for f in flags.values())
    inner = pl.ds(PAD, nx)

    loads = [
        pltpu.make_async_copy(por_hbm, por, load_sem.at[0]),
        pltpu.make_async_copy(lit_hbm, lit, load_sem.at[1]),
        pltpu.make_async_copy(p_hbm, pv.at[pl.ds(1, nz), inner, :], load_sem.at[2]),
    ]
    for c in loads:
        c.start()

    barrier = pltpu.get_barrier_semaphore()
    for a in axes:
        @pl.when(has_lo[a])
        def _():
            pl.semaphore_signal(barrier, inc=1, device_id={a: me[a] - 1}, device_id_type=MESH)

        @pl.when(has_hi[a])
        def _():
            pl.semaphore_signal(barrier, inc=1, device_id={a: me[a] + 1}, device_id_type=MESH)

    def message(k, axis, up, src, dst):
        target = me[axis] + 1 if up else me[axis] - 1
        return pltpu.make_async_remote_copy(
            src_ref=src, dst_ref=dst, send_sem=send_sem.at[k], recv_sem=recv_sem.at[k],
            device_id={axis: target}, device_id_type=MESH)

    def pair(k, axis, src_up, dst_up, src_down, dst_down):
        return [(k, axis, True, src_up, dst_up), (k + 1, axis, False, src_down, dst_down)]

    z_lo, z_hi = 0, nz + 1
    groups = {
        Z_P: pair(Z_P, "slab", p_hbm.at[nz - 1], pv.at[z_lo, inner, :],
                  p_hbm.at[0], pv.at[z_hi, inner, :]),
        Z_H: pair(Z_H, "slab", hv.at[nz, inner, :], hv.at[z_lo, inner, :],
                  hv.at[1, inner, :], hv.at[z_hi, inner, :]),
        X_1: pair(X_1, "mapx", xs.at[0], xr.at[0], xs.at[1], xr.at[1]),
        Y_1: pair(Y_1, "mapy", ys.at[0], yr.at[0], ys.at[1], yr.at[1]),
        Z_Q: pair(Z_Q, "slab", qv.at[nz, inner, :], qv.at[z_lo, inner, :],
                  qv.at[1, inner, :], qv.at[z_hi, inner, :]),
        X_Q: pair(X_Q, "mapx", xqs.at[0], xqr.at[0], xqs.at[1], xqr.at[1]),
        Y_Q: pair(Y_Q, "mapy", yqs.at[0], yqr.at[0], yqs.at[1], yqr.at[1]),
    }

    def start(group):
        for k, axis, up, src, dst in groups[group]:
            @pl.when(has_hi[axis] if up else has_lo[axis])
            def _():
                message(k, axis, up, src, dst).start()

    def arrived(group):
        for k, axis, up, src, dst in groups[group]:
            @pl.when(has_lo[axis] if up else has_hi[axis])
            def _():
                message(k, axis, up, src, dst).wait_recv()

    def sent(group):
        for k, axis, up, src, dst in groups[group]:
            @pl.when(has_hi[axis] if up else has_lo[axis])
            def _():
                message(k, axis, up, src, dst).wait_send()

    lane_y = lax.broadcasted_iota(jnp.int32, (nx, 128), 1)

    for axis, flags in (("lo", has_lo), ("hi", has_hi)):
        side = 0 if axis == "lo" else 1
        layer = z_lo if side == 0 else z_hi

        @pl.when(jnp.logical_not(flags["slab"]))
        def _():
            pv[layer, inner, :] = jnp.zeros((nx, ny), jnp.float32)
            qv[layer, inner, :] = jnp.zeros((nx, ny), jnp.float32)
            hv[layer, inner, :] = jnp.full((nx, ny), OUTSIDE, jnp.float32)
            if side == 0:
                above[...] = jnp.zeros((nx, ny), jnp.float32)

        @pl.when(jnp.logical_not(flags["mapx"]))
        def _():
            xr[side, pl.ds(0, nz), :] = jnp.zeros((nz, ny), jnp.float32)
            xr[side, pl.ds(nz, nz), :] = jnp.full((nz, ny), OUTSIDE, jnp.float32)
            xqr[side] = jnp.zeros((nz, ny), jnp.float32)

        @pl.when(jnp.logical_not(flags["mapy"]))
        def _():
            yr[side] = jnp.where(lane_y < nz, jnp.float32(0.0), jnp.float32(OUTSIDE))
            yqr[side] = jnp.zeros((nx, 128), jnp.float32)

    pl.semaphore_wait(barrier, peers)

    start(Z_P)
    loads[0].wait()
    loads[1].wait()

    def half_inverse(z):
        for r in range(0, nx, 32):
            rows = pl.ds(r, 32)
            cls = classes(lit[z, rows, :])
            hv[z + 1, pl.ds(PAD + r, 32), :] = jnp.exp(
                pick(cls, HALF_BASE) + pick(cls, HALF_SLOPE) * por[z, rows, :])

    half_inverse(0)
    half_inverse(nz - 1)
    start(Z_H)
    lax.fori_loop(1, nz - 1, lambda z, c: (half_inverse(z), c)[1], 0)
    loads[2].wait()

    def face_x(src, dst, offset):
        for side, row in ((0, PAD + nx - 1), (1, PAD)):
            for z in range(nz):
                dst[side, pl.ds(offset + z, 1), :] = src[z + 1, pl.ds(row, 1), :]

    def face_y(srcs, dst):
        for side in range(2):
            for r in range(0, nx, 32):
                acc = jnp.zeros((32, 128), jnp.float32)
                lane = lane_y[:32]
                for i, src in enumerate(srcs):
                    for z in range(nz):
                        k = i * nz + z
                        if side == 0:
                            col_ = src[z + 1, pl.ds(PAD + r, 32), pl.ds(ny - 128, 128)]
                            moved = pltpu.roll(col_, k + 1, 1)
                        else:
                            col_ = src[z + 1, pl.ds(PAD + r, 32), pl.ds(0, 128)]
                            moved = pltpu.roll(col_, k, 1) if k else col_
                        acc = jnp.where(lane == k, moved, acc)
                dst[side, pl.ds(r, 32), :] = acc

    face_x(pv, xs, 0)
    face_x(hv, xs, nz)
    start(X_1)
    face_y((pv, hv), ys)
    start(Y_1)

    for r in range(0, nx, 32):
        rows = pl.ds(r, 32)

        def add_layer(z, total):
            cls = classes(lit[z, rows, :])
            load = (pick(cls, GRAIN_LESS) + WATER_DENSITY * rec(1.0 - por[z, rows, :])) * solid[z]
            ob[z, rows, :] = total + 0.5 * load
            return total + load

        col[rows, :] = lax.fori_loop(0, nz, add_layer, jnp.zeros((32, ny), jnp.float32))

    def chain(src):
        return message(CHAIN, "slab", True, src, above)

    @pl.when(me["slab"] == 0)
    def _():
        col_send[...] = col[...]
        chain(col_send).start()

    def forward():
        chain(col_send).wait_recv()
        col_send[...] = col[...] + above[...]
        chain(col_send).start()

    @pl.when(me["slab"] == 1)
    def _():
        forward()

    def spread_x(src, offset, dst):
        for side, row in ((0, PAD - 1), (1, PAD + nx)):
            for z in range(nz):
                dst[z + 1, pl.ds(row, 1), :] = src[side, pl.ds(offset + z, 1), :]

    arrived(X_1)
    spread_x(xr, 0, pv)
    spread_x(xr, nz, hv)
    arrived(Y_1)
    arrived(Z_P)
    arrived(Z_H)

    lane = lax.broadcasted_iota(jnp.int32, (ROWS, ny), 1)

    def beside_y(value, halo, index, r):
        lo = pltpu.roll(halo[0, pl.ds(r, ROWS), :], lax.rem(128 - index, 128), 1)
        hi = pltpu.roll(halo[1, pl.ds(r, ROWS), :], 127 - index, 1)
        wide = lambda v: jnp.concatenate([v] * (ny // 128), axis=1)
        before = jnp.where(lane == 0, wide(lo), pltpu.roll(value, 1, 1))
        after = jnp.where(lane == ny - 1, wide(hi), pltpu.roll(value, ny - 1, 1))
        return before, after

    def first(z):
        for r in range(0, nx, ROWS):
            at = lambda ref, dz, dx: ref[z + 1 + dz, pl.ds(PAD + r + dx, ROWS), :]
            rows = pl.ds(r, ROWS)
            h, p = at(hv, 0, 0), at(pv, 0, 0)
            h_before, h_after = beside_y(h, yr, nz + z, r)
            p_before, p_after = beside_y(p, yr, z, r)
            t_zm, t_zp = rec(h + at(hv, -1, 0)), rec(h + at(hv, 1, 0))
            t_xm, t_xp = rec(h + at(hv, 0, -1)), rec(h + at(hv, 0, 1))
            t_ym, t_yp = rec(h + h_before), rec(h + h_after)
            diag = 1.0 + ((t_zm + t_zp) + (t_xm + t_xp) + (t_ym + t_yp))
            inv = rec(diag)
            total = (p + (t_zm * at(pv, -1, 0) + t_zp * at(pv, 1, 0))
                     + (t_xm * at(pv, 0, -1) + t_xp * at(pv, 0, 1))
                     + (t_ym * p_before + t_yp * p_after))
            tz[z, rows, :] = t_zm
            tz[z + 1, rows, :] = t_zp
            tx[z, rows, :] = t_xm
            if r + ROWS == nx:
                tx[z, pl.ds(nx, 1), :] = t_xp[ROWS - 1:, :]
            tym[z, rows, :] = t_ym
            typ[z, rows, :] = t_yp
            rd[z, rows, :] = inv
            qv[z + 1, pl.ds(PAD + r, ROWS), :] = total * inv

    first(0)
    first(nz - 1)
    start(Z_Q)
    lax.fori_loop(1, nz - 1, lambda z, c: (first(z), c)[1], 0)
    face_x(qv, xqs, 0)
    start(X_Q)
    face_y((qv,), yqs)
    start(Y_Q)

    @pl.when(me["slab"] == 2)
    def _():
        forward()

    @pl.when(me["slab"] == 3)
    def _():
        chain(col_send).wait_recv()

    arrived(X_Q)
    spread_x(xqr, 0, qv)
    arrived(Y_Q)
    arrived(Z_Q)

    def second(z, carry):
        for r in range(0, nx, ROWS):
            at = lambda ref, dz, dx: ref[z + 1 + dz, pl.ds(PAD + r + dx, ROWS), :]
            rows = pl.ds(r, ROWS)
            p, q = at(pv, 0, 0), at(qv, 0, 0)
            q_before, q_after = beside_y(q, yqr, z, r)
            total = (p + (tz[z, rows, :] * at(qv, -1, 0) + tz[z + 1, rows, :] * at(qv, 1, 0))
                     + (tx[z, rows, :] * at(qv, 0, -1) + tx[z, pl.ds(r + 1, ROWS), :] * at(qv, 0, 1))
                     + (tym[z, rows, :] * q_before + typ[z, rows, :] * q_after))
            pn = q + STEP_KEEP * (q - p) + STEP_RES * (total * rd[z, rows, :] - q)
            stress = jnp.maximum(above[rows, :] + ob[z, rows, :] - pn, 0.0)
            cls = classes(lit[z, rows, :])
            phi = pick(cls, PHI_SURFACE) * jnp.exp(pick(cls, ATHY_NEG) * stress)
            pn_out[z, rows, :] = pn
            phi_out[z, rows, :] = phi
            thick_out[z, rows, :] = solid[z] * rec(1.0 - phi)
        return carry

    lax.fori_loop(0, nz, second, 0)

    for group in groups:
        sent(group)

    @pl.when(has_hi["slab"])
    def _():
        chain(col_send).wait_send()


def body(sizes, pressure, porosity, lithology, layer_solid):
    nz, nx, ny = pressure.shape
    f32 = jnp.float32
    block = pltpu.VMEM((nz, nx, ny), f32)
    padded = pltpu.VMEM((nz + 2, nx + 2 * PAD, ny), f32)
    plane = pltpu.VMEM((nx, ny), f32)
    out = jax.ShapeDtypeStruct((nz, nx, ny), f32)
    vmem = pl.BlockSpec(memory_space=pltpu.VMEM)
    return pl.pallas_call(
        functools.partial(kernel, sizes),
        out_shape=(out, out, out),
        in_specs=[pl.BlockSpec(memory_space=pl.ANY)] * 3 + [pl.BlockSpec(memory_space=pltpu.SMEM)],
        out_specs=(vmem, vmem, vmem),
        scratch_shapes=[
            padded, padded, padded,
            pltpu.VMEM((nz + 1, nx, ny), f32), pltpu.VMEM((nz, nx + PAD, ny), f32),
            block, block, block, block, block, pltpu.VMEM((nz, nx, ny), jnp.int32),
            plane, plane, plane,
            pltpu.VMEM((2, 2 * nz, ny), f32), pltpu.VMEM((2, 2 * nz, ny), f32),
            pltpu.VMEM((2, nx, 128), f32), pltpu.VMEM((2, nx, 128), f32),
            pltpu.VMEM((2, nz, ny), f32), pltpu.VMEM((2, nz, ny), f32),
            pltpu.VMEM((2, nx, 128), f32), pltpu.VMEM((2, nx, 128), f32),
            pltpu.SemaphoreType.DMA((3,)),
            pltpu.SemaphoreType.DMA((MESSAGES,)),
            pltpu.SemaphoreType.DMA((MESSAGES,)),
        ],
        compiler_params=pltpu.CompilerParams(
            collective_id=0, has_side_effects=True, vmem_limit_bytes=32 * 2**20),
        name="basin",
    )(pressure, porosity, lithology, layer_solid)


def solution(mesh):
    sizes = dict(mesh.shape)
    spec = P("slab", "mapx", "mapy")
    return jax.shard_map(
        functools.partial(body, sizes), mesh=mesh,
        in_specs=(spec, spec, spec, P("slab")), out_specs=(spec, spec, spec), check_vma=False)
```

```python
import functools
import math

import jax
import jax.numpy as jnp
from jax import lax
from jax.experimental import pallas as pl
from jax.experimental.pallas import tpu as pltpu
from jax.sharding import PartitionSpec as P

PHI_SURFACE = (0.45, 0.55, 0.65, 0.4)
ATHY_RATE = (0.25, 0.45, 0.8, 0.35)
MOB_BASE = (1.0, 0.0, -1.5, -0.5)
MOB_SLOPE = (6.0, 5.0, 8.0, 4.0)
GRAIN_DENSITY = (2.65, 2.68, 2.72, 2.71)
WATER_DENSITY = 1.03
SPECTRUM_MID = 1.0
SPECTRUM_HALF = 0.95
SIGMA_RATIO = SPECTRUM_MID / SPECTRUM_HALF
RHO_FIRST = 1.0 / SIGMA_RATIO
RHO_SECOND = 1.0 / (2.0 * SIGMA_RATIO - RHO_FIRST)
STEP_KEEP = RHO_SECOND * RHO_FIRST
STEP_RES = 2.0 * RHO_SECOND / SPECTRUM_HALF

HALF_BASE = tuple(-(b - 0.35 * s) - math.log(2.0) for b, s in zip(MOB_BASE, MOB_SLOPE))
HALF_SLOPE = tuple(-s for s in MOB_SLOPE)
GRAIN_LESS = tuple(g - WATER_DENSITY for g in GRAIN_DENSITY)
ATHY_NEG = tuple(-a for a in ATHY_RATE)
OUTSIDE = 2.0e38

MESH = pl.DeviceIdType.MESH
PAD = 8
ROWS = 16
Z_P, Z_H, X_1, Y_1, Z_Q, X_Q, Y_Q, CHAIN = 0, 2, 4, 6, 8, 10, 12, 14
MESSAGES = 15


def rec(x):
    r = pl.reciprocal(x, approx=True)
    return r * (2.0 - x * r)


def classes(lith):
    return lith >= 2, (lith & 1) == 1


def pick(cls, table):
    high, odd = cls
    a, b, c, d = (jnp.float32(t) for t in table)
    return jnp.where(high, jnp.where(odd, d, c), jnp.where(odd, b, a))


def beside_y(value, halo, index, r):
    ny = value.shape[1]
    lane = lax.broadcasted_iota(jnp.int32, (ROWS, ny), 1)
    lo = pltpu.roll(halo[0, pl.ds(r, ROWS), :], lax.rem(128 - index, 128), 1)
    hi = pltpu.roll(halo[1, pl.ds(r, ROWS), :], 127 - index, 1)
    wide = lambda v: jnp.concatenate([v] * (ny // 128), axis=1)
    before = jnp.where(lane == 0, wide(lo), pltpu.roll(value, 1, 1))
    after = jnp.where(lane == ny - 1, wide(hi), pltpu.roll(value, ny - 1, 1))
    return before, after


def exchange(sizes, p_hbm, por_hbm, lit_hbm, solid_hbm,
             pv, qv, tz, tx, tym, typ, rd, ob, lit, above, yqr,
             hv, por, col, col_send, xs, xr, ys, yr, xqs, xqr, yqs,
             solid, load_sem, send_sem, recv_sem):
    nz, nx, ny = por.shape
    axes = ("slab", "mapx", "mapy")
    me = {a: lax.axis_index(a) for a in axes}
    has_lo = {a: me[a] > 0 for a in axes}
    has_hi = {a: me[a] < sizes[a] - 1 for a in axes}
    peers = sum(jnp.where(f, 1, 0) for flags in (has_lo, has_hi) for f in flags.values())
    inner = pl.ds(PAD, nx)

    loads = [
        pltpu.make_async_copy(por_hbm, por, load_sem.at[0]),
        pltpu.make_async_copy(lit_hbm, lit, load_sem.at[1]),
        pltpu.make_async_copy(p_hbm, pv.at[pl.ds(1, nz), inner, :], load_sem.at[2]),
        pltpu.make_async_copy(solid_hbm, solid, load_sem.at[3]),
    ]
    for c in loads:
        c.start()

    barrier = pltpu.get_barrier_semaphore()
    for a in axes:
        @pl.when(has_lo[a])
        def _():
            pl.semaphore_signal(barrier, inc=1, device_id={a: me[a] - 1}, device_id_type=MESH)

        @pl.when(has_hi[a])
        def _():
            pl.semaphore_signal(barrier, inc=1, device_id={a: me[a] + 1}, device_id_type=MESH)

    def message(k, axis, up, src, dst):
        target = me[axis] + 1 if up else me[axis] - 1
        return pltpu.make_async_remote_copy(
            src_ref=src, dst_ref=dst, send_sem=send_sem.at[k], recv_sem=recv_sem.at[k],
            device_id={axis: target}, device_id_type=MESH)

    def pair(k, axis, src_up, dst_up, src_down, dst_down):
        return [(k, axis, True, src_up, dst_up), (k + 1, axis, False, src_down, dst_down)]

    z_lo, z_hi = 0, nz + 1
    groups = {
        Z_P: pair(Z_P, "slab", p_hbm.at[nz - 1], pv.at[z_lo, inner, :],
                  p_hbm.at[0], pv.at[z_hi, inner, :]),
        Z_H: pair(Z_H, "slab", hv.at[nz, inner, :], hv.at[z_lo, inner, :],
                  hv.at[1, inner, :], hv.at[z_hi, inner, :]),
        X_1: pair(X_1, "mapx", xs.at[0], xr.at[0], xs.at[1], xr.at[1]),
        Y_1: pair(Y_1, "mapy", ys.at[0], yr.at[0], ys.at[1], yr.at[1]),
        Z_Q: pair(Z_Q, "slab", qv.at[nz, inner, :], qv.at[z_lo, inner, :],
                  qv.at[1, inner, :], qv.at[z_hi, inner, :]),
        X_Q: pair(X_Q, "mapx", xqs.at[0], xqr.at[0], xqs.at[1], xqr.at[1]),
        Y_Q: pair(Y_Q, "mapy", yqs.at[0], yqr.at[0], yqs.at[1], yqr.at[1]),
    }

    def start(group):
        for k, axis, up, src, dst in groups[group]:
            @pl.when(has_hi[axis] if up else has_lo[axis])
            def _():
                message(k, axis, up, src, dst).start()

    def arrived(group):
        for k, axis, up, src, dst in groups[group]:
            @pl.when(has_lo[axis] if up else has_hi[axis])
            def _():
                message(k, axis, up, src, dst).wait_recv()

    def sent(group):
        for k, axis, up, src, dst in groups[group]:
            @pl.when(has_hi[axis] if up else has_lo[axis])
            def _():
                message(k, axis, up, src, dst).wait_send()

    lane_y = lax.broadcasted_iota(jnp.int32, (nx, 128), 1)

    for axis, flags in (("lo", has_lo), ("hi", has_hi)):
        side = 0 if axis == "lo" else 1
        layer = z_lo if side == 0 else z_hi

        @pl.when(jnp.logical_not(flags["slab"]))
        def _():
            pv[layer, inner, :] = jnp.zeros((nx, ny), jnp.float32)
            qv[layer, inner, :] = jnp.zeros((nx, ny), jnp.float32)
            hv[layer, inner, :] = jnp.full((nx, ny), OUTSIDE, jnp.float32)
            if side == 0:
                above[...] = jnp.zeros((nx, ny), jnp.float32)

        @pl.when(jnp.logical_not(flags["mapx"]))
        def _():
            xr[side, pl.ds(0, nz), :] = jnp.zeros((nz, ny), jnp.float32)
            xr[side, pl.ds(nz, nz), :] = jnp.full((nz, ny), OUTSIDE, jnp.float32)
            xqr[side] = jnp.zeros((nz, ny), jnp.float32)

        @pl.when(jnp.logical_not(flags["mapy"]))
        def _():
            yr[side] = jnp.where(lane_y < nz, jnp.float32(0.0), jnp.float32(OUTSIDE))
            yqr[side] = jnp.zeros((nx, 128), jnp.float32)

    pl.semaphore_wait(barrier, peers)

    start(Z_P)
    loads[0].wait()
    loads[1].wait()

    def half_inverse(z):
        for r in range(0, nx, 32):
            rows = pl.ds(r, 32)
            cls = classes(lit[z, rows, :])
            hv[z + 1, pl.ds(PAD + r, 32), :] = jnp.exp(
                pick(cls, HALF_BASE) + pick(cls, HALF_SLOPE) * por[z, rows, :])

    half_inverse(0)
    half_inverse(nz - 1)
    start(Z_H)
    lax.fori_loop(1, nz - 1, lambda z, c: (half_inverse(z), c)[1], 0)
    loads[2].wait()

    def face_x(src, dst, offset):
        for side, row in ((0, PAD + nx - 1), (1, PAD)):
            for z in range(nz):
                dst[side, pl.ds(offset + z, 1), :] = src[z + 1, pl.ds(row, 1), :]

    def face_y(srcs, dst):
        for side in range(2):
            for r in range(0, nx, 32):
                acc = jnp.zeros((32, 128), jnp.float32)
                lane = lane_y[:32]
                for i, src in enumerate(srcs):
                    for z in range(nz):
                        k = i * nz + z
                        if side == 0:
                            col_ = src[z + 1, pl.ds(PAD + r, 32), pl.ds(ny - 128, 128)]
                            moved = pltpu.roll(col_, k + 1, 1)
                        else:
                            col_ = src[z + 1, pl.ds(PAD + r, 32), pl.ds(0, 128)]
                            moved = pltpu.roll(col_, k, 1) if k else col_
                        acc = jnp.where(lane == k, moved, acc)
                dst[side, pl.ds(r, 32), :] = acc

    face_x(pv, xs, 0)
    face_x(hv, xs, nz)
    start(X_1)
    face_y((pv, hv), ys)
    start(Y_1)

    loads[3].wait()
    for r in range(0, nx, 32):
        rows = pl.ds(r, 32)

        def add_layer(z, total):
            cls = classes(lit[z, rows, :])
            load = (pick(cls, GRAIN_LESS) + WATER_DENSITY * rec(1.0 - por[z, rows, :])) * solid[z]
            ob[z, rows, :] = total + 0.5 * load
            return total + load

        col[rows, :] = lax.fori_loop(0, nz, add_layer, jnp.zeros((32, ny), jnp.float32))

    def chain(src):
        return message(CHAIN, "slab", True, src, above)

    @pl.when(me["slab"] == 0)
    def _():
        col_send[...] = col[...]
        chain(col_send).start()

    def forward():
        chain(col_send).wait_recv()
        col_send[...] = col[...] + above[...]
        chain(col_send).start()

    @pl.when(me["slab"] == 1)
    def _():
        forward()

    def spread_x(src, offset, dst):
        for side, row in ((0, PAD - 1), (1, PAD + nx)):
            for z in range(nz):
                dst[z + 1, pl.ds(row, 1), :] = src[side, pl.ds(offset + z, 1), :]

    arrived(X_1)
    spread_x(xr, 0, pv)
    spread_x(xr, nz, hv)
    arrived(Y_1)
    arrived(Z_P)
    arrived(Z_H)

    def first(z):
        for r in range(0, nx, ROWS):
            at = lambda ref, dz, dx: ref[z + 1 + dz, pl.ds(PAD + r + dx, ROWS), :]
            rows = pl.ds(r, ROWS)
            h, p = at(hv, 0, 0), at(pv, 0, 0)
            h_before, h_after = beside_y(h, yr, nz + z, r)
            p_before, p_after = beside_y(p, yr, z, r)
            t_zm, t_zp = rec(h + at(hv, -1, 0)), rec(h + at(hv, 1, 0))
            t_xm, t_xp = rec(h + at(hv, 0, -1)), rec(h + at(hv, 0, 1))
            t_ym, t_yp = rec(h + h_before), rec(h + h_after)
            diag = 1.0 + ((t_zm + t_zp) + (t_xm + t_xp) + (t_ym + t_yp))
            inv = rec(diag)
            total = (p + (t_zm * at(pv, -1, 0) + t_zp * at(pv, 1, 0))
                     + (t_xm * at(pv, 0, -1) + t_xp * at(pv, 0, 1))
                     + (t_ym * p_before + t_yp * p_after))
            tz[z, rows, :] = t_zm
            tz[z + 1, rows, :] = t_zp
            tx[z, rows, :] = t_xm
            if r + ROWS == nx:
                tx[z, pl.ds(nx, 1), :] = t_xp[ROWS - 1:, :]
            tym[z, rows, :] = t_ym
            typ[z, rows, :] = t_yp
            rd[z, rows, :] = inv
            qv[z + 1, pl.ds(PAD + r, ROWS), :] = total * inv

    first(0)
    first(nz - 1)
    start(Z_Q)
    lax.fori_loop(1, nz - 1, lambda z, c: (first(z), c)[1], 0)
    face_x(qv, xqs, 0)
    start(X_Q)
    face_y((qv,), yqs)
    start(Y_Q)

    @pl.when(me["slab"] == 2)
    def _():
        forward()

    @pl.when(me["slab"] == 3)
    def _():
        chain(col_send).wait_recv()

    arrived(X_Q)
    spread_x(xqr, 0, qv)
    arrived(Y_Q)
    arrived(Z_Q)

    for group in groups:
        sent(group)

    @pl.when(has_hi["slab"])
    def _():
        chain(col_send).wait_send()


def finish(pv, qv, tz, tx, tym, typ, rd, ob, lit, above, yqr, solid_hbm,
           pn_out, phi_out, thick_out, buf, solid, load_sem, store_sem):
    nz, nx, ny = lit.shape
    load = pltpu.make_async_copy(solid_hbm, solid, load_sem)
    load.start()
    load.wait()
    outs = (pn_out, phi_out, thick_out)

    def store(i, z):
        return pltpu.make_async_copy(buf.at[i, z], outs[i].at[z], store_sem.at[i, z])

    def second(z, carry):
        for r in range(0, nx, ROWS):
            at = lambda ref, dz, dx: ref[z + 1 + dz, pl.ds(PAD + r + dx, ROWS), :]
            rows = pl.ds(r, ROWS)
            p, q = at(pv, 0, 0), at(qv, 0, 0)
            q_before, q_after = beside_y(q, yqr, z, r)
            total = (p + (tz[z, rows, :] * at(qv, -1, 0) + tz[z + 1, rows, :] * at(qv, 1, 0))
                     + (tx[z, rows, :] * at(qv, 0, -1) + tx[z, pl.ds(r + 1, ROWS), :] * at(qv, 0, 1))
                     + (tym[z, rows, :] * q_before + typ[z, rows, :] * q_after))
            pn = q + STEP_KEEP * (q - p) + STEP_RES * (total * rd[z, rows, :] - q)
            stress = jnp.maximum(above[rows, :] + ob[z, rows, :] - pn, 0.0)
            cls = classes(lit[z, rows, :])
            phi = pick(cls, PHI_SURFACE) * jnp.exp(pick(cls, ATHY_NEG) * stress)
            buf[0, z, rows, :] = pn
            buf[1, z, rows, :] = phi
            buf[2, z, rows, :] = solid[z] * rec(1.0 - phi)
        for i in range(3):
            store(i, z).start()
        return carry

    lax.fori_loop(0, nz, second, 0)

    def stored(z, carry):
        for i in range(3):
            store(i, z).wait()
        return carry

    lax.fori_loop(0, nz, stored, 0)


def body(sizes, pressure, porosity, lithology, layer_solid):
    nz, nx, ny = pressure.shape
    f32, i32 = jnp.float32, jnp.int32
    shaped = jax.ShapeDtypeStruct
    block, plane = (nz, nx, ny), (nx, ny)
    padded = (nz + 2, nx + 2 * PAD, ny)
    x_face, y_face = (2, nz, ny), (2, nx, 128)
    vmem = pl.BlockSpec(memory_space=pltpu.VMEM)
    hbm = pl.BlockSpec(memory_space=pltpu.HBM)
    held = [padded, padded, (nz + 1, nx, ny), (nz, nx + PAD, ny), block, block, block, block]
    held = [shaped(s, f32) for s in held]
    held += [shaped(block, i32), shaped(plane, f32), shaped(y_face, f32)]
    held = pl.pallas_call(
        functools.partial(exchange, sizes),
        out_shape=tuple(held),
        in_specs=[hbm] * 4,
        out_specs=(vmem,) * len(held),
        scratch_shapes=[
            pltpu.VMEM(padded, f32), pltpu.VMEM(block, f32), pltpu.VMEM(plane, f32),
            pltpu.VMEM(plane, f32),
            pltpu.VMEM((2, 2 * nz, ny), f32), pltpu.VMEM((2, 2 * nz, ny), f32),
            pltpu.VMEM(y_face, f32), pltpu.VMEM(y_face, f32),
            pltpu.VMEM(x_face, f32), pltpu.VMEM(x_face, f32), pltpu.VMEM(y_face, f32),
            pltpu.SMEM((nz,), f32),
            pltpu.SemaphoreType.DMA((4,)),
            pltpu.SemaphoreType.DMA((MESSAGES,)),
            pltpu.SemaphoreType.DMA((MESSAGES,)),
        ],
        compiler_params=pltpu.CompilerParams(
            collective_id=0, has_side_effects=True, vmem_limit_bytes=24 * 2**20),
        name="exchange",
    )(*(pltpu.with_memory_space_constraint(a, pltpu.HBM) for a in (pressure, porosity, lithology, layer_solid)))
    return pl.pallas_call(
        finish,
        out_shape=(shaped(block, f32),) * 3,
        in_specs=[vmem] * len(held) + [hbm],
        out_specs=(hbm,) * 3,
        scratch_shapes=[
            pltpu.VMEM((3,) + block, f32),
            pltpu.SMEM((nz,), f32),
            pltpu.SemaphoreType.DMA,
            pltpu.SemaphoreType.DMA((3, nz)),
        ],
        compiler_params=pltpu.CompilerParams(vmem_limit_bytes=24 * 2**20),
        name="finish",
    )(*held, layer_solid)


def solution(mesh):
    sizes = dict(mesh.shape)
    spec = P("slab", "mapx", "mapy")
    return jax.shard_map(
        functools.partial(body, sizes), mesh=mesh,
        in_specs=(spec, spec, spec, P("slab")), out_specs=(spec, spec, spec), check_vma=False)
```

```python
import functools
import math

import jax
import jax.numpy as jnp
from jax import lax
from jax.experimental import pallas as pl
from jax.experimental.pallas import tpu as pltpu
from jax.sharding import PartitionSpec as P

PHI_SURFACE = (0.45, 0.55, 0.65, 0.4)
ATHY_RATE = (0.25, 0.45, 0.8, 0.35)
MOB_BASE = (1.0, 0.0, -1.5, -0.5)
MOB_SLOPE = (6.0, 5.0, 8.0, 4.0)
GRAIN_DENSITY = (2.65, 2.68, 2.72, 2.71)
WATER_DENSITY = 1.03
SPECTRUM_MID = 1.0
SPECTRUM_HALF = 0.95
SIGMA_RATIO = SPECTRUM_MID / SPECTRUM_HALF
RHO_FIRST = 1.0 / SIGMA_RATIO
RHO_SECOND = 1.0 / (2.0 * SIGMA_RATIO - RHO_FIRST)
STEP_KEEP = RHO_SECOND * RHO_FIRST
STEP_RES = 2.0 * RHO_SECOND / SPECTRUM_HALF

HALF_BASE = tuple(-(b - 0.35 * s) - math.log(2.0) for b, s in zip(MOB_BASE, MOB_SLOPE))
HALF_SLOPE = tuple(-s for s in MOB_SLOPE)
GRAIN_LESS = tuple(g - WATER_DENSITY for g in GRAIN_DENSITY)
ATHY_NEG = tuple(-a for a in ATHY_RATE)
OUTSIDE = 2.0e38

MESH = pl.DeviceIdType.MESH
PAD = 8
ROWS = 16
Z_P, Z_H, X_1, Y_1, Z_Q, X_Q, Y_Q, CHAIN = 0, 2, 4, 6, 8, 10, 12, 14
MESSAGES = 15


def rec(x):
    return pl.reciprocal(x, approx=True)


def classes(lith):
    return lith >= 2, (lith & 1) == 1


def pick(cls, table):
    high, odd = cls
    a, b, c, d = (jnp.float32(t) for t in table)
    return jnp.where(high, jnp.where(odd, d, c), jnp.where(odd, b, a))


def beside_y(value, halo, index, r):
    ny = value.shape[1]
    lane = lax.broadcasted_iota(jnp.int32, (ROWS, ny), 1)
    lo = pltpu.roll(halo[0, pl.ds(r, ROWS), :], lax.rem(128 - index, 128), 1)
    hi = pltpu.roll(halo[1, pl.ds(r, ROWS), :], 127 - index, 1)
    wide = lambda v: jnp.concatenate([v] * (ny // 128), axis=1)
    before = jnp.where(lane == 0, wide(lo), pltpu.roll(value, 1, 1))
    after = jnp.where(lane == ny - 1, wide(hi), pltpu.roll(value, ny - 1, 1))
    return before, after


def exchange(sizes, p_hbm, por_hbm, lit_hbm, solid_hbm,
             part, ob, lit, above, y_term, solid_wide,
             pv, qv, hv, tz, tx, tym, typ, rd, por, col, col_send, xs, xr, ys, yr,
             zqr, xqs, xqr, yqs, yqr, edge, solid, load_sem, send_sem, recv_sem):
    nz, nx, ny = por.shape
    axes = ("slab", "mapx", "mapy")
    me = {a: lax.axis_index(a) for a in axes}
    has_lo = {a: me[a] > 0 for a in axes}
    has_hi = {a: me[a] < sizes[a] - 1 for a in axes}
    peers = sum(jnp.where(f, 1, 0) for flags in (has_lo, has_hi) for f in flags.values())
    inner = pl.ds(PAD, nx)

    loads = [
        pltpu.make_async_copy(por_hbm, por, load_sem.at[0]),
        pltpu.make_async_copy(lit_hbm, lit, load_sem.at[1]),
        pltpu.make_async_copy(p_hbm, pv.at[pl.ds(1, nz), inner, :], load_sem.at[2]),
        pltpu.make_async_copy(solid_hbm, solid, load_sem.at[3]),
    ]
    for c in loads:
        c.start()

    barrier = pltpu.get_barrier_semaphore()
    for a in axes:
        @pl.when(has_lo[a])
        def _():
            pl.semaphore_signal(barrier, inc=1, device_id={a: me[a] - 1}, device_id_type=MESH)

        @pl.when(has_hi[a])
        def _():
            pl.semaphore_signal(barrier, inc=1, device_id={a: me[a] + 1}, device_id_type=MESH)

    def message(k, axis, up, src, dst):
        target = me[axis] + 1 if up else me[axis] - 1
        return pltpu.make_async_remote_copy(
            src_ref=src, dst_ref=dst, send_sem=send_sem.at[k], recv_sem=recv_sem.at[k],
            device_id={axis: target}, device_id_type=MESH)

    def pair(k, axis, src_up, dst_up, src_down, dst_down):
        return [(k, axis, True, src_up, dst_up), (k + 1, axis, False, src_down, dst_down)]

    z_lo, z_hi = 0, nz + 1
    groups = {
        Z_P: pair(Z_P, "slab", p_hbm.at[nz - 1], pv.at[z_lo, inner, :],
                  p_hbm.at[0], pv.at[z_hi, inner, :]),
        Z_H: pair(Z_H, "slab", hv.at[nz, inner, :], hv.at[z_lo, inner, :],
                  hv.at[1, inner, :], hv.at[z_hi, inner, :]),
        X_1: pair(X_1, "mapx", xs.at[0], xr.at[0], xs.at[1], xr.at[1]),
        Y_1: pair(Y_1, "mapy", ys.at[0], yr.at[0], ys.at[1], yr.at[1]),
        Z_Q: pair(Z_Q, "slab", qv.at[nz, inner, :], zqr.at[0], qv.at[1, inner, :], zqr.at[1]),
        X_Q: pair(X_Q, "mapx", xqs.at[0], xqr.at[0], xqs.at[1], xqr.at[1]),
        Y_Q: pair(Y_Q, "mapy", yqs.at[0], yqr.at[0], yqs.at[1], yqr.at[1]),
    }

    def start(group):
        for k, axis, up, src, dst in groups[group]:
            @pl.when(has_hi[axis] if up else has_lo[axis])
            def _():
                message(k, axis, up, src, dst).start()

    def arrived(group):
        for k, axis, up, src, dst in groups[group]:
            @pl.when(has_lo[axis] if up else has_hi[axis])
            def _():
                message(k, axis, up, src, dst).wait_recv()

    def sent(group):
        for k, axis, up, src, dst in groups[group]:
            @pl.when(has_hi[axis] if up else has_lo[axis])
            def _():
                message(k, axis, up, src, dst).wait_send()

    lane_y = lax.broadcasted_iota(jnp.int32, (nx, 128), 1)

    for layer in (z_lo, z_hi):
        qv[layer, inner, :] = jnp.zeros((nx, ny), jnp.float32)
    for z in range(nz):
        for row in (PAD - 1, PAD + nx):
            qv[z + 1, pl.ds(row, 1), :] = jnp.zeros((1, ny), jnp.float32)

    for axis, flags in (("lo", has_lo), ("hi", has_hi)):
        side = 0 if axis == "lo" else 1
        layer = z_lo if side == 0 else z_hi

        @pl.when(jnp.logical_not(flags["slab"]))
        def _():
            pv[layer, inner, :] = jnp.zeros((nx, ny), jnp.float32)
            zqr[side] = jnp.zeros((nx, ny), jnp.float32)
            hv[layer, inner, :] = jnp.full((nx, ny), OUTSIDE, jnp.float32)
            if side == 0:
                above[...] = jnp.zeros((nx, ny), jnp.float32)

        @pl.when(jnp.logical_not(flags["mapx"]))
        def _():
            xr[side, pl.ds(0, nz), :] = jnp.zeros((nz, ny), jnp.float32)
            xr[side, pl.ds(nz, nz), :] = jnp.full((nz, ny), OUTSIDE, jnp.float32)
            xqr[side] = jnp.zeros((nz, ny), jnp.float32)

        @pl.when(jnp.logical_not(flags["mapy"]))
        def _():
            yr[side] = jnp.where(lane_y < nz, jnp.float32(0.0), jnp.float32(OUTSIDE))
            yqr[side] = jnp.zeros((nx, 128), jnp.float32)

    loads[0].wait()
    loads[1].wait()

    def half_inverse(z):
        for r in range(0, nx, 32):
            rows = pl.ds(r, 32)
            cls = classes(lit[z, rows, :])
            hv[z + 1, pl.ds(PAD + r, 32), :] = jnp.exp(
                pick(cls, HALF_BASE) + pick(cls, HALF_SLOPE) * por[z, rows, :])

    half_inverse(0)
    half_inverse(nz - 1)
    pl.semaphore_wait(barrier, peers)
    start(Z_H)
    start(Z_P)
    lax.fori_loop(1, nz - 1, lambda z, c: (half_inverse(z), c)[1], 0)
    loads[2].wait()

    def face_x(src, dst, offset):
        for side, row in ((0, PAD + nx - 1), (1, PAD)):
            for z in range(nz):
                dst[side, pl.ds(offset + z, 1), :] = src[z + 1, pl.ds(row, 1), :]

    def face_y(srcs, dst):
        for side in range(2):
            for r in range(0, nx, 32):
                acc = jnp.zeros((32, 128), jnp.float32)
                lane = lane_y[:32]
                for i, src in enumerate(srcs):
                    for z in range(nz):
                        k = i * nz + z
                        if side == 0:
                            col_ = src[z + 1, pl.ds(PAD + r, 32), pl.ds(ny - 128, 128)]
                            moved = pltpu.roll(col_, k + 1, 1)
                        else:
                            col_ = src[z + 1, pl.ds(PAD + r, 32), pl.ds(0, 128)]
                            moved = pltpu.roll(col_, k, 1) if k else col_
                        acc = jnp.where(lane == k, moved, acc)
                dst[side, pl.ds(r, 32), :] = acc

    face_x(pv, xs, 0)
    face_x(hv, xs, nz)
    start(X_1)
    face_y((pv, hv), ys)
    start(Y_1)

    loads[3].wait()
    for r in range(0, nx, 32):
        rows = pl.ds(r, 32)

        def add_layer(z, total):
            cls = classes(lit[z, rows, :])
            load = (pick(cls, GRAIN_LESS) + WATER_DENSITY * rec(1.0 - por[z, rows, :])) * solid[z]
            ob[z, rows, :] = total + 0.5 * load
            return total + load

        col[rows, :] = lax.fori_loop(0, nz, add_layer, jnp.zeros((32, ny), jnp.float32))

    def chain(src):
        return message(CHAIN, "slab", True, src, above)

    @pl.when(me["slab"] == 0)
    def _():
        col_send[...] = col[...]
        chain(col_send).start()

    def forward():
        chain(col_send).wait_recv()
        col_send[...] = col[...] + above[...]
        chain(col_send).start()

    @pl.when(me["slab"] == 1)
    def _():
        forward()

    def spread_x(src, offset, dst):
        for side, row in ((0, PAD - 1), (1, PAD + nx)):
            for z in range(nz):
                dst[z + 1, pl.ds(row, 1), :] = src[side, pl.ds(offset + z, 1), :]

    arrived(X_1)
    spread_x(xr, 0, pv)
    spread_x(xr, nz, hv)
    arrived(Y_1)
    arrived(Z_P)
    arrived(Z_H)

    def first(z, below_known=True):
        for r in range(0, nx, ROWS):
            at = lambda ref, dz, dx: ref[z + 1 + dz, pl.ds(PAD + r + dx, ROWS), :]
            rows = pl.ds(r, ROWS)
            h, p = at(hv, 0, 0), at(pv, 0, 0)
            h_before, h_after = beside_y(h, yr, nz + z, r)
            p_before, p_after = beside_y(p, yr, z, r)
            t_zm = tz[z, rows, :] if below_known else rec(h + at(hv, -1, 0))
            t_zp = rec(h + at(hv, 1, 0))
            t_xm, t_xp = rec(h + at(hv, 0, -1)), rec(h + at(hv, 0, 1))
            t_ym, t_yp = rec(h + h_before), rec(h + h_after)
            diag = 1.0 + ((t_zm + t_zp) + (t_xm + t_xp) + (t_ym + t_yp))
            inv = rec(diag)
            total = (p + (t_zm * at(pv, -1, 0) + t_zp * at(pv, 1, 0))
                     + (t_xm * at(pv, 0, -1) + t_xp * at(pv, 0, 1))
                     + (t_ym * p_before + t_yp * p_after))
            if not below_known:
                tz[z, rows, :] = t_zm
            tz[z + 1, rows, :] = t_zp
            tx[z, rows, :] = t_xm
            if r + ROWS == nx:
                tx[z, pl.ds(nx, 1), :] = t_xp[ROWS - 1:, :]
            tym[z, rows, :] = t_ym
            typ[z, rows, :] = t_yp
            rd[z, rows, :] = STEP_RES * inv
            qv[z + 1, pl.ds(PAD + r, ROWS), :] = total * inv

    first(0, False)
    first(nz - 1, False)
    start(Z_Q)
    lax.fori_loop(1, nz - 1, lambda z, c: (first(z), c)[1], 0)
    face_x(qv, xqs, 0)
    start(X_Q)
    face_y((qv,), yqs)
    start(Y_Q)

    for side in range(2):
        for r in range(0, nx, 32):
            rows, lane = pl.ds(r, 32), lane_y[:32]
            acc = jnp.zeros((32, 128), jnp.float32)
            for z in range(nz):
                if side == 0:
                    term = tym[z, rows, pl.ds(0, 128)] * rd[z, rows, pl.ds(0, 128)]
                    moved = pltpu.roll(term, z, 1) if z else term
                else:
                    lanes = pl.ds(ny - 128, 128)
                    term = typ[z, rows, lanes] * rd[z, rows, lanes]
                    moved = pltpu.roll(term, z + 1, 1)
                acc = jnp.where(lane == z, moved, acc)
            edge[side, rows, :] = acc

    @pl.when(me["slab"] == 2)
    def _():
        forward()

    lane = lax.broadcasted_iota(jnp.int32, (ROWS, ny), 1)

    def second(z, carry):
        for r in range(0, nx, ROWS):
            at = lambda ref, dz, dx: ref[z + 1 + dz, pl.ds(PAD + r + dx, ROWS), :]
            rows = pl.ds(r, ROWS)
            p, q = at(pv, 0, 0), at(qv, 0, 0)
            q_before = jnp.where(lane == 0, 0.0, pltpu.roll(q, 1, 1))
            q_after = jnp.where(lane == ny - 1, 0.0, pltpu.roll(q, ny - 1, 1))
            total = (p + (tz[z, rows, :] * at(qv, -1, 0) + tz[z + 1, rows, :] * at(qv, 1, 0))
                     + (tx[z, rows, :] * at(qv, 0, -1) + tx[z, pl.ds(r + 1, ROWS), :] * at(qv, 0, 1))
                     + (tym[z, rows, :] * q_before + typ[z, rows, :] * q_after))
            part[z, rows, :] = q + STEP_KEEP * (q - p) + (total * rd[z, rows, :] - STEP_RES * q)
        return carry

    lax.fori_loop(0, nz, second, 0)

    arrived(X_Q)
    for side, row in ((0, 0), (1, nx - 1)):
        for z in range(nz):
            one = pl.ds(row, 1)
            part[z, one, :] += rd[z, one, :] * tx[z, pl.ds(row + side, 1), :] * xqr[side, pl.ds(z, 1), :]
    arrived(Y_Q)
    for side in range(2):
        y_term[side] = edge[side] * yqr[side]
    arrived(Z_Q)
    for side, z in ((0, 0), (1, nz - 1)):
        for r in range(0, nx, 32):
            rows = pl.ds(r, 32)
            part[z, rows, :] += rd[z, rows, :] * tz[z + side, rows, :] * zqr[side, rows, :]
    for z in range(nz):
        solid_wide[z] = jnp.full((8, 128), solid[z], jnp.float32)

    @pl.when(me["slab"] == 3)
    def _():
        chain(col_send).wait_recv()

    for group in groups:
        sent(group)

    @pl.when(has_hi["slab"])
    def _():
        chain(col_send).wait_send()


def finish(part, ob, lit, above, y_term, solid_wide, pn_out, phi_out, thick_out, buf, store_sem):
    nz, nx, ny = lit.shape
    outs = (pn_out, phi_out, thick_out)
    lane = lax.broadcasted_iota(jnp.int32, (ROWS, 128), 1)

    def store(i, z):
        return pltpu.make_async_copy(buf.at[i, z], outs[i].at[z], store_sem.at[i, z])

    def layer(z, carry):
        solid = jnp.concatenate([solid_wide[z]] * (ny // 128), axis=1)
        solid = jnp.concatenate([solid] * (ROWS // 8), axis=0)
        for r in range(0, nx, ROWS):
            rows = pl.ds(r, ROWS)
            lo = pltpu.roll(y_term[0, rows, :], lax.rem(128 - z, 128), 1)
            hi = pltpu.roll(y_term[1, rows, :], 127 - z, 1)
            lo, hi = jnp.where(lane == 0, lo, 0.0), jnp.where(lane == 127, hi, 0.0)
            zeros = [jnp.zeros((ROWS, 128), jnp.float32)] * (ny // 128 - 2)
            pn = part[z, rows, :] + jnp.concatenate([lo] + zeros + [hi], axis=1)
            stress = jnp.maximum(above[rows, :] + ob[z, rows, :] - pn, 0.0)
            cls = classes(lit[z, rows, :])
            phi = pick(cls, PHI_SURFACE) * jnp.exp(pick(cls, ATHY_NEG) * stress)
            buf[0, z, rows, :] = pn
            buf[1, z, rows, :] = phi
            buf[2, z, rows, :] = solid * rec(1.0 - phi)
        for i in range(3):
            store(i, z).start()
        return carry

    lax.fori_loop(0, nz, layer, 0)

    def stored(z, carry):
        for i in range(3):
            store(i, z).wait()
        return carry

    lax.fori_loop(0, nz, stored, 0)


def body(sizes, pressure, porosity, lithology, layer_solid):
    nz, nx, ny = pressure.shape
    f32, i32 = jnp.float32, jnp.int32
    shaped = jax.ShapeDtypeStruct
    block, plane = (nz, nx, ny), (nx, ny)
    padded = (nz + 2, nx + 2 * PAD, ny)
    x_face, y_face = (2, nz, ny), (2, nx, 128)
    vmem = pl.BlockSpec(memory_space=pltpu.VMEM)
    hbm = pl.BlockSpec(memory_space=pltpu.HBM)
    held = (shaped(block, f32), shaped(block, f32), shaped(block, i32), shaped(plane, f32),
            shaped(y_face, f32), shaped((nz, 8, 128), f32))
    held = pl.pallas_call(
        functools.partial(exchange, sizes),
        out_shape=held,
        in_specs=[hbm] * 4,
        out_specs=(vmem,) * len(held),
        scratch_shapes=[pltpu.VMEM(shape, f32) for shape in (
            padded, padded, padded, (nz + 1, nx, ny), (nz, nx + PAD, ny),
            block, block, block, block, plane, plane,
            (2, 2 * nz, ny), (2, 2 * nz, ny), y_face, y_face,
            (2, nx, ny), x_face, x_face, y_face, y_face, y_face)] + [
            pltpu.SMEM((nz,), f32),
            pltpu.SemaphoreType.DMA((4,)),
            pltpu.SemaphoreType.DMA((MESSAGES,)),
            pltpu.SemaphoreType.DMA((MESSAGES,)),
        ],
        compiler_params=pltpu.CompilerParams(
            collective_id=0, has_side_effects=True, vmem_limit_bytes=24 * 2**20),
        name="exchange",
    )(*(pltpu.with_memory_space_constraint(a, pltpu.HBM) for a in (pressure, porosity, lithology, layer_solid)))
    return pl.pallas_call(
        finish,
        out_shape=(shaped(block, f32),) * 3,
        in_specs=[vmem] * len(held),
        out_specs=(hbm,) * 3,
        scratch_shapes=[
            pltpu.VMEM((3,) + block, f32),
            pltpu.SemaphoreType.DMA((3, nz)),
        ],
        compiler_params=pltpu.CompilerParams(vmem_limit_bytes=24 * 2**20),
        name="finish",
    )(*held)


def solution(mesh):
    sizes = dict(mesh.shape)
    spec = P("slab", "mapx", "mapy")
    return jax.shard_map(
        functools.partial(body, sizes), mesh=mesh,
        in_specs=(spec, spec, spec, P("slab")), out_specs=(spec, spec, spec), check_vma=False)
```

```python
import functools
import math

import jax
import jax.numpy as jnp
from jax import lax
from jax.experimental import pallas as pl
from jax.experimental.pallas import tpu as pltpu
from jax.sharding import PartitionSpec as P

PHI_SURFACE = (0.45, 0.55, 0.65, 0.4)
ATHY_RATE = (0.25, 0.45, 0.8, 0.35)
MOB_BASE = (1.0, 0.0, -1.5, -0.5)
MOB_SLOPE = (6.0, 5.0, 8.0, 4.0)
GRAIN_DENSITY = (2.65, 2.68, 2.72, 2.71)
WATER_DENSITY = 1.03
SPECTRUM_MID = 1.0
SPECTRUM_HALF = 0.95
SIGMA_RATIO = SPECTRUM_MID / SPECTRUM_HALF
RHO_FIRST = 1.0 / SIGMA_RATIO
RHO_SECOND = 1.0 / (2.0 * SIGMA_RATIO - RHO_FIRST)
STEP_KEEP = RHO_SECOND * RHO_FIRST
STEP_RES = 2.0 * RHO_SECOND / SPECTRUM_HALF

LOG2_E = 1.0 / math.log(2.0)

HALF_BASE = tuple(-(b - 0.35 * s) * LOG2_E - 1.0 for b, s in zip(MOB_BASE, MOB_SLOPE))
HALF_SLOPE = tuple(-s * LOG2_E for s in MOB_SLOPE)
GRAIN_LESS = tuple(g - WATER_DENSITY for g in GRAIN_DENSITY)
ATHY_NEG = tuple(-a * LOG2_E for a in ATHY_RATE)
OUTSIDE = 2.0e38

MESH = pl.DeviceIdType.MESH
PAD = 8
ROWS = 16
Z_P, Z_H, X_1, Y_1, Z_Q, X_Q, Y_Q, CHAIN = 0, 2, 4, 6, 8, 10, 12, 14
MESSAGES = 15


def rec(x):
    return pl.reciprocal(x, approx=True)


def classes(lith):
    return lith >= 2, (lith & 1) == 1


def pick(cls, table):
    high, odd = cls
    a, b, c, d = (jnp.float32(t) for t in table)
    return jnp.where(high, jnp.where(odd, d, c), jnp.where(odd, b, a))


def beside_y(value, lo, hi):
    rows, ny = value.shape
    lane = lax.broadcasted_iota(jnp.int32, (rows, 128), 1)
    parts = [value[:, y:y + 128] for y in range(0, ny, 128)]
    later = [pltpu.roll(v, 1, 1) for v in parts]
    earlier = [pltpu.roll(v, 127, 1) for v in parts]
    before = [jnp.where(lane == 0, a, b) for a, b in zip([lo] + later[:-1], later)]
    after = [jnp.where(lane == 127, a, b) for a, b in zip(earlier[1:] + [hi], earlier)]
    return jnp.concatenate(before, axis=1), jnp.concatenate(after, axis=1)


def unpacked(halo, index, rows):
    lo = pltpu.roll(halo[0, rows, :], lax.rem(128 - index, 128), 1)
    hi = pltpu.roll(halo[1, rows, :], 127 - index, 1)
    return lo, hi


def exchange(sizes, p_hbm, por_hbm, lit_hbm, solid_hbm,
             part, ob, lit, above, y_term, solid_wide,
             pv, qv, hv, tz, tx, tym, typ, rd, por, col, col_send, xs, xr, ys, yr,
             zqr, xqs, xqr, yqs, yqr, edge, solid, load_sem, send_sem, recv_sem):
    nz, nx, ny = por.shape
    axes = ("slab", "mapx", "mapy")
    me = {a: lax.axis_index(a) for a in axes}
    has_lo = {a: me[a] > 0 for a in axes}
    has_hi = {a: me[a] < sizes[a] - 1 for a in axes}
    peers = sum(jnp.where(f, 1, 0) for flags in (has_lo, has_hi) for f in flags.values())
    inner = pl.ds(PAD, nx)

    loads = [
        pltpu.make_async_copy(por_hbm, por, load_sem.at[0]),
        pltpu.make_async_copy(lit_hbm, lit, load_sem.at[1]),
        pltpu.make_async_copy(p_hbm, pv.at[pl.ds(1, nz), inner, :], load_sem.at[2]),
        pltpu.make_async_copy(solid_hbm, solid, load_sem.at[3]),
    ]
    for c in loads:
        c.start()

    barrier = pltpu.get_barrier_semaphore()
    for a in axes:
        @pl.when(has_lo[a])
        def _():
            pl.semaphore_signal(barrier, inc=1, device_id={a: me[a] - 1}, device_id_type=MESH)

        @pl.when(has_hi[a])
        def _():
            pl.semaphore_signal(barrier, inc=1, device_id={a: me[a] + 1}, device_id_type=MESH)

    def message(k, axis, up, src, dst):
        target = me[axis] + 1 if up else me[axis] - 1
        return pltpu.make_async_remote_copy(
            src_ref=src, dst_ref=dst, send_sem=send_sem.at[k], recv_sem=recv_sem.at[k],
            device_id={axis: target}, device_id_type=MESH)

    def pair(k, axis, src_up, dst_up, src_down, dst_down):
        return [(k, axis, True, src_up, dst_up), (k + 1, axis, False, src_down, dst_down)]

    z_lo, z_hi = 0, nz + 1
    groups = {
        Z_P: pair(Z_P, "slab", p_hbm.at[nz - 1], pv.at[z_lo, inner, :],
                  p_hbm.at[0], pv.at[z_hi, inner, :]),
        Z_H: pair(Z_H, "slab", hv.at[nz, inner, :], hv.at[z_lo, inner, :],
                  hv.at[1, inner, :], hv.at[z_hi, inner, :]),
        X_1: pair(X_1, "mapx", xs.at[0], xr.at[0], xs.at[1], xr.at[1]),
        Y_1: pair(Y_1, "mapy", ys.at[0], yr.at[0], ys.at[1], yr.at[1]),
        Z_Q: pair(Z_Q, "slab", qv.at[nz, inner, :], zqr.at[0], qv.at[1, inner, :], zqr.at[1]),
        X_Q: pair(X_Q, "mapx", xqs.at[0], xqr.at[0], xqs.at[1], xqr.at[1]),
        Y_Q: pair(Y_Q, "mapy", yqs.at[0], yqr.at[0], yqs.at[1], yqr.at[1]),
    }

    def start(group):
        for k, axis, up, src, dst in groups[group]:
            @pl.when(has_hi[axis] if up else has_lo[axis])
            def _():
                message(k, axis, up, src, dst).start()

    def arrived(group):
        for k, axis, up, src, dst in groups[group]:
            @pl.when(has_lo[axis] if up else has_hi[axis])
            def _():
                message(k, axis, up, src, dst).wait_recv()

    def sent(group):
        for k, axis, up, src, dst in groups[group]:
            @pl.when(has_hi[axis] if up else has_lo[axis])
            def _():
                message(k, axis, up, src, dst).wait_send()

    lane_y = lax.broadcasted_iota(jnp.int32, (nx, 128), 1)

    for layer in (z_lo, z_hi):
        qv[layer, inner, :] = jnp.zeros((nx, ny), jnp.float32)
    for z in range(nz):
        for row in (PAD - 1, PAD + nx):
            qv[z + 1, pl.ds(row, 1), :] = jnp.zeros((1, ny), jnp.float32)

    for axis, flags in (("lo", has_lo), ("hi", has_hi)):
        side = 0 if axis == "lo" else 1
        layer = z_lo if side == 0 else z_hi

        @pl.when(jnp.logical_not(flags["slab"]))
        def _():
            pv[layer, inner, :] = jnp.zeros((nx, ny), jnp.float32)
            zqr[side] = jnp.zeros((nx, ny), jnp.float32)
            hv[layer, inner, :] = jnp.full((nx, ny), OUTSIDE, jnp.float32)
            if side == 0:
                above[...] = jnp.zeros((nx, ny), jnp.float32)

        @pl.when(jnp.logical_not(flags["mapx"]))
        def _():
            xr[side, pl.ds(0, nz), :] = jnp.zeros((nz, ny), jnp.float32)
            xr[side, pl.ds(nz, nz), :] = jnp.full((nz, ny), OUTSIDE, jnp.float32)
            xqr[side] = jnp.zeros((nz, ny), jnp.float32)

        @pl.when(jnp.logical_not(flags["mapy"]))
        def _():
            yr[side] = jnp.where(lane_y < nz, jnp.float32(0.0), jnp.float32(OUTSIDE))
            yqr[side] = jnp.zeros((nx, 128), jnp.float32)

    loads[0].wait()
    loads[1].wait()

    def half_inverse(z):
        for r in range(0, nx, 32):
            rows = pl.ds(r, 32)
            cls = classes(lit[z, rows, :])
            hv[z + 1, pl.ds(PAD + r, 32), :] = jnp.exp2(
                pick(cls, HALF_BASE) + pick(cls, HALF_SLOPE) * por[z, rows, :])

    half_inverse(0)
    half_inverse(nz - 1)
    pl.semaphore_wait(barrier, peers)
    start(Z_H)
    start(Z_P)
    lax.fori_loop(1, nz - 1, lambda z, c: (half_inverse(z), c)[1], 0)
    loads[2].wait()

    def face_x(src, dst, offset):
        for side, row in ((0, PAD + nx - 1), (1, PAD)):
            for z in range(nz):
                dst[side, pl.ds(offset + z, 1), :] = src[z + 1, pl.ds(row, 1), :]

    def face_y(srcs, dst):
        for side in range(2):
            for r in range(0, nx, 32):
                acc = jnp.zeros((32, 128), jnp.float32)
                lane = lane_y[:32]
                for i, src in enumerate(srcs):
                    for z in range(nz):
                        k = i * nz + z
                        if side == 0:
                            col_ = src[z + 1, pl.ds(PAD + r, 32), pl.ds(ny - 128, 128)]
                            moved = pltpu.roll(col_, k + 1, 1)
                        else:
                            col_ = src[z + 1, pl.ds(PAD + r, 32), pl.ds(0, 128)]
                            moved = pltpu.roll(col_, k, 1) if k else col_
                        acc = jnp.where(lane == k, moved, acc)
                dst[side, pl.ds(r, 32), :] = acc

    face_x(pv, xs, 0)
    face_x(hv, xs, nz)
    start(X_1)
    face_y((pv, hv), ys)
    start(Y_1)

    loads[3].wait()
    for r in range(0, nx, 32):
        rows = pl.ds(r, 32)

        def add_layer(z, total):
            cls = classes(lit[z, rows, :])
            load = (pick(cls, GRAIN_LESS) + WATER_DENSITY * rec(1.0 - por[z, rows, :])) * solid[z]
            ob[z, rows, :] = total + 0.5 * load
            return total + load

        col[rows, :] = lax.fori_loop(0, nz, add_layer, jnp.zeros((32, ny), jnp.float32))

    def chain(src):
        return message(CHAIN, "slab", True, src, above)

    @pl.when(me["slab"] == 0)
    def _():
        col_send[...] = col[...]
        chain(col_send).start()

    def forward():
        chain(col_send).wait_recv()
        col_send[...] = col[...] + above[...]
        chain(col_send).start()

    def spread_x(src, offset, dst):
        for side, row in ((0, PAD - 1), (1, PAD + nx)):
            for z in range(nz):
                dst[z + 1, pl.ds(row, 1), :] = src[side, pl.ds(offset + z, 1), :]

    arrived(X_1)
    spread_x(xr, 0, pv)
    spread_x(xr, nz, hv)
    arrived(Y_1)

    def first(z, below=True, above_known=False):
        for r in range(0, nx, ROWS):
            at = lambda ref, dz, dx: ref[z + 1 + dz, pl.ds(PAD + r + dx, ROWS), :]
            rows = pl.ds(r, ROWS)
            h, p = at(hv, 0, 0), at(pv, 0, 0)
            h_before, h_after = beside_y(h, *unpacked(yr, nz + z, rows))
            p_before, p_after = beside_y(p, *unpacked(yr, z, rows))
            t_zm = tz[z, rows, :] if below else rec(h + at(hv, -1, 0))
            t_zp = tz[z + 1, rows, :] if above_known else rec(h + at(hv, 1, 0))
            t_xm, t_xp = rec(h + at(hv, 0, -1)), rec(h + at(hv, 0, 1))
            t_ym, t_yp = rec(h + h_before), rec(h + h_after)
            diag = 1.0 + ((t_zm + t_zp) + (t_xm + t_xp) + (t_ym + t_yp))
            inv = rec(diag)
            total = (p + (t_zm * at(pv, -1, 0) + t_zp * at(pv, 1, 0))
                     + (t_xm * at(pv, 0, -1) + t_xp * at(pv, 0, 1))
                     + (t_ym * p_before + t_yp * p_after))
            if not below:
                tz[z, rows, :] = t_zm
            if not above_known:
                tz[z + 1, rows, :] = t_zp
            tx[z, rows, :] = t_xm
            if r + ROWS == nx:
                tx[z, pl.ds(nx, 1), :] = t_xp[ROWS - 1:, :]
            tym[z, rows, :] = t_ym
            typ[z, rows, :] = t_yp
            rd[z, rows, :] = STEP_RES * inv
            qv[z + 1, pl.ds(PAD + r, ROWS), :] = total * inv

    first(1, below=False)
    lax.fori_loop(2, nz // 2, lambda z, c: (first(z), c)[1], 0)

    @pl.when(me["slab"] == 1)
    def _():
        forward()

    lax.fori_loop(nz // 2, nz - 1, lambda z, c: (first(z), c)[1], 0)
    arrived(Z_H)
    arrived(Z_P)
    first(0, below=False, above_known=True)
    first(nz - 1)
    start(Z_Q)
    face_x(qv, xqs, 0)
    start(X_Q)
    face_y((qv,), yqs)
    start(Y_Q)

    for side in range(2):
        for r in range(0, nx, 32):
            rows, lane = pl.ds(r, 32), lane_y[:32]
            acc = jnp.zeros((32, 128), jnp.float32)
            for z in range(nz):
                if side == 0:
                    term = tym[z, rows, pl.ds(0, 128)] * rd[z, rows, pl.ds(0, 128)]
                    moved = pltpu.roll(term, z, 1) if z else term
                else:
                    lanes = pl.ds(ny - 128, 128)
                    term = typ[z, rows, lanes] * rd[z, rows, lanes]
                    moved = pltpu.roll(term, z + 1, 1)
                acc = jnp.where(lane == z, moved, acc)
            edge[side, rows, :] = acc

    @pl.when(me["slab"] == 2)
    def _():
        forward()

    def second(z, carry):
        for r in range(0, nx, ROWS):
            at = lambda ref, dz, dx: ref[z + 1 + dz, pl.ds(PAD + r + dx, ROWS), :]
            rows = pl.ds(r, ROWS)
            p, q = at(pv, 0, 0), at(qv, 0, 0)
            q_before, q_after = beside_y(q, 0.0, 0.0)
            total = (p + (tz[z, rows, :] * at(qv, -1, 0) + tz[z + 1, rows, :] * at(qv, 1, 0))
                     + (tx[z, rows, :] * at(qv, 0, -1) + tx[z, pl.ds(r + 1, ROWS), :] * at(qv, 0, 1))
                     + (tym[z, rows, :] * q_before + typ[z, rows, :] * q_after))
            part[z, rows, :] = q + STEP_KEEP * (q - p) + (total * rd[z, rows, :] - STEP_RES * q)
        return carry

    lax.fori_loop(0, nz, second, 0)

    arrived(X_Q)
    for side, row in ((0, 0), (1, nx - 1)):
        for z in range(nz):
            one = pl.ds(row, 1)
            part[z, one, :] += rd[z, one, :] * tx[z, pl.ds(row + side, 1), :] * xqr[side, pl.ds(z, 1), :]
    arrived(Y_Q)
    for side in range(2):
        y_term[side] = edge[side] * yqr[side]
    arrived(Z_Q)
    for side, z in ((0, 0), (1, nz - 1)):
        for r in range(0, nx, 32):
            rows = pl.ds(r, 32)
            part[z, rows, :] += rd[z, rows, :] * tz[z + side, rows, :] * zqr[side, rows, :]
    for z in range(nz):
        solid_wide[z] = jnp.full((8, 128), solid[z], jnp.float32)

    @pl.when(me["slab"] == 3)
    def _():
        chain(col_send).wait_recv()

    for group in groups:
        sent(group)

    @pl.when(has_hi["slab"])
    def _():
        chain(col_send).wait_send()


def finish(part, ob, lit, above, y_term, solid_wide, pn_out, phi_out, thick_out, buf, store_sem):
    nz, nx, ny = lit.shape
    outs = (pn_out, phi_out, thick_out)
    lane = lax.broadcasted_iota(jnp.int32, (ROWS, 128), 1)

    def store(i, z):
        return pltpu.make_async_copy(buf.at[i, z], outs[i].at[z], store_sem.at[i, z])

    def layer(z, carry):
        solid = jnp.concatenate([solid_wide[z]] * (ny // 128), axis=1)
        solid = jnp.concatenate([solid] * (ROWS // 8), axis=0)
        for r in range(0, nx, ROWS):
            rows = pl.ds(r, ROWS)
            lo, hi = unpacked(y_term, z, rows)
            lo, hi = jnp.where(lane == 0, lo, 0.0), jnp.where(lane == 127, hi, 0.0)
            zeros = [jnp.zeros((ROWS, 128), jnp.float32)] * (ny // 128 - 2)
            pn = part[z, rows, :] + jnp.concatenate([lo] + zeros + [hi], axis=1)
            stress = jnp.maximum(above[rows, :] + ob[z, rows, :] - pn, 0.0)
            cls = classes(lit[z, rows, :])
            phi = pick(cls, PHI_SURFACE) * jnp.exp2(pick(cls, ATHY_NEG) * stress)
            buf[0, z, rows, :] = pn
            buf[1, z, rows, :] = phi
            buf[2, z, rows, :] = solid * rec(1.0 - phi)
        for i in range(3):
            store(i, z).start()
        return carry

    lax.fori_loop(0, nz, layer, 0)

    def stored(z, carry):
        for i in range(3):
            store(i, z).wait()
        return carry

    lax.fori_loop(0, nz, stored, 0)


def body(sizes, pressure, porosity, lithology, layer_solid):
    nz, nx, ny = pressure.shape
    f32, i32 = jnp.float32, jnp.int32
    shaped = jax.ShapeDtypeStruct
    block, plane = (nz, nx, ny), (nx, ny)
    padded = (nz + 2, nx + 2 * PAD, ny)
    x_face, y_face = (2, nz, ny), (2, nx, 128)
    vmem = pl.BlockSpec(memory_space=pltpu.VMEM)
    hbm = pl.BlockSpec(memory_space=pltpu.HBM)
    held = (shaped(block, f32), shaped(block, f32), shaped(block, i32), shaped(plane, f32),
            shaped(y_face, f32), shaped((nz, 8, 128), f32))
    held = pl.pallas_call(
        functools.partial(exchange, sizes),
        out_shape=held,
        in_specs=[hbm] * 4,
        out_specs=(vmem,) * len(held),
        scratch_shapes=[pltpu.VMEM(shape, f32) for shape in (
            padded, padded, padded, (nz + 1, nx, ny), (nz, nx + PAD, ny),
            block, block, block, block, plane, plane,
            (2, 2 * nz, ny), (2, 2 * nz, ny), y_face, y_face,
            (2, nx, ny), x_face, x_face, y_face, y_face, y_face)] + [
            pltpu.SMEM((nz,), f32),
            pltpu.SemaphoreType.DMA((4,)),
            pltpu.SemaphoreType.DMA((MESSAGES,)),
            pltpu.SemaphoreType.DMA((MESSAGES,)),
        ],
        compiler_params=pltpu.CompilerParams(
            collective_id=0, has_side_effects=True, vmem_limit_bytes=24 * 2**20),
        name="exchange",
    )(*(pltpu.with_memory_space_constraint(a, pltpu.HBM) for a in (pressure, porosity, lithology, layer_solid)))
    return pl.pallas_call(
        finish,
        out_shape=(shaped(block, f32),) * 3,
        in_specs=[vmem] * len(held),
        out_specs=(hbm,) * 3,
        scratch_shapes=[
            pltpu.VMEM((3,) + block, f32),
            pltpu.SemaphoreType.DMA((3, nz)),
        ],
        compiler_params=pltpu.CompilerParams(vmem_limit_bytes=24 * 2**20),
        name="finish",
    )(*held)


def solution(mesh):
    sizes = dict(mesh.shape)
    spec = P("slab", "mapx", "mapy")
    return jax.shard_map(
        functools.partial(body, sizes), mesh=mesh,
        in_specs=(spec, spec, spec, P("slab")), out_specs=(spec, spec, spec), check_vma=False)
```

```python
import functools
import math

import jax
import jax.numpy as jnp
from jax import lax
from jax.experimental import pallas as pl
from jax.experimental.pallas import tpu as pltpu
from jax.sharding import PartitionSpec as P

PHI_SURFACE = (0.45, 0.55, 0.65, 0.4)
ATHY_RATE = (0.25, 0.45, 0.8, 0.35)
MOB_BASE = (1.0, 0.0, -1.5, -0.5)
MOB_SLOPE = (6.0, 5.0, 8.0, 4.0)
GRAIN_DENSITY = (2.65, 2.68, 2.72, 2.71)
WATER_DENSITY = 1.03
SPECTRUM_MID = 1.0
SPECTRUM_HALF = 0.95
SIGMA_RATIO = SPECTRUM_MID / SPECTRUM_HALF
RHO_FIRST = 1.0 / SIGMA_RATIO
RHO_SECOND = 1.0 / (2.0 * SIGMA_RATIO - RHO_FIRST)
STEP_KEEP = RHO_SECOND * RHO_FIRST
STEP_RES = 2.0 * RHO_SECOND / SPECTRUM_HALF

LOG2_E = 1.0 / math.log(2.0)

HALF_BASE = tuple(-(b - 0.35 * s) * LOG2_E - 1.0 for b, s in zip(MOB_BASE, MOB_SLOPE))
HALF_SLOPE = tuple(-s * LOG2_E for s in MOB_SLOPE)
GRAIN_LESS = tuple(g - WATER_DENSITY for g in GRAIN_DENSITY)
ATHY_NEG = tuple(-a * LOG2_E for a in ATHY_RATE)
OUTSIDE = 2.0e38

MESH = pl.DeviceIdType.MESH
PAD = 8
ROWS = 16
Z_P, Z_H, X_1, Y_1, Z_Q, X_Q, Y_Q, CHAIN = 0, 2, 4, 6, 8, 10, 12, 14
MESSAGES = 15


def rec(x):
    return pl.reciprocal(x, approx=True)


def classes(lith):
    return lith >= 2, (lith & 1) == 1


def pick(cls, table):
    high, odd = cls
    a, b, c, d = (jnp.float32(t) for t in table)
    return jnp.where(high, jnp.where(odd, d, c), jnp.where(odd, b, a))


def shifted(value, up):
    rows, ny = value.shape
    lane = lax.broadcasted_iota(jnp.int32, (rows, 128), 1)
    parts = [pltpu.roll(value[:, y:y + 128], 1 if up else 127, 1) for y in range(0, ny, 128)]
    if up:
        joined = [jnp.where(lane == 0, a, b) for a, b in zip(parts[-1:] + parts[:-1], parts)]
    else:
        joined = [jnp.where(lane == 127, a, b) for a, b in zip(parts[1:] + parts[:1], parts)]
    return jnp.concatenate(joined, axis=1)


def at_edges(halo, index, rows, ny):
    lo = pltpu.roll(halo[0, rows, :], lax.rem(128 - index, 128), 1)
    hi = pltpu.roll(halo[1, rows, :], 127 - index, 1)
    lane = lax.broadcasted_iota(jnp.int32, lo.shape, 1)
    zeros = [jnp.zeros(lo.shape, jnp.float32)] * (ny // 128 - 2)
    ends = [jnp.where(lane == 0, lo, 0.0)] + zeros + [jnp.where(lane == 127, hi, 0.0)]
    return jnp.concatenate(ends, axis=1)


def exchange(sizes, p_hbm, por_hbm, lit_hbm, solid_hbm,
             part, ob, lit, above, y_term, solid_wide,
             pv, qv, hv, tz, tx, ty, rd, por, col, col_send, xs, xr, ys, yr,
             zpr, zhr, zqr, xqs, xqr, yqs, yqr, z_link, x_link, y_link, y_flow, edge,
             solid, load_sem, send_sem, recv_sem):
    nz, nx, ny = por.shape
    axes = ("slab", "mapx", "mapy")
    me = {a: lax.axis_index(a) for a in axes}
    has_lo = {a: me[a] > 0 for a in axes}
    has_hi = {a: me[a] < sizes[a] - 1 for a in axes}
    peers = sum(jnp.where(f, 1, 0) for flags in (has_lo, has_hi) for f in flags.values())
    inner = pl.ds(PAD, nx)

    loads = [
        pltpu.make_async_copy(por_hbm, por, load_sem.at[0]),
        pltpu.make_async_copy(lit_hbm, lit, load_sem.at[1]),
        pltpu.make_async_copy(p_hbm, pv.at[pl.ds(1, nz), inner, :], load_sem.at[2]),
        pltpu.make_async_copy(solid_hbm, solid, load_sem.at[3]),
    ]
    for c in loads:
        c.start()

    barrier = pltpu.get_barrier_semaphore()
    for a in axes:
        @pl.when(has_lo[a])
        def _():
            pl.semaphore_signal(barrier, inc=1, device_id={a: me[a] - 1}, device_id_type=MESH)

        @pl.when(has_hi[a])
        def _():
            pl.semaphore_signal(barrier, inc=1, device_id={a: me[a] + 1}, device_id_type=MESH)

    def message(k, axis, up, src, dst):
        target = me[axis] + 1 if up else me[axis] - 1
        return pltpu.make_async_remote_copy(
            src_ref=src, dst_ref=dst, send_sem=send_sem.at[k], recv_sem=recv_sem.at[k],
            device_id={axis: target}, device_id_type=MESH)

    def pair(k, axis, src_up, dst_up, src_down, dst_down):
        return [(k, axis, True, src_up, dst_up), (k + 1, axis, False, src_down, dst_down)]

    z_lo, z_hi = 0, nz + 1
    groups = {
        Z_P: pair(Z_P, "slab", p_hbm.at[nz - 1], zpr.at[0], p_hbm.at[0], zpr.at[1]),
        Z_H: pair(Z_H, "slab", hv.at[nz, inner, :], zhr.at[0], hv.at[1, inner, :], zhr.at[1]),
        X_1: pair(X_1, "mapx", xs.at[0], xr.at[0], xs.at[1], xr.at[1]),
        Y_1: pair(Y_1, "mapy", ys.at[0], yr.at[0], ys.at[1], yr.at[1]),
        Z_Q: pair(Z_Q, "slab", qv.at[nz, inner, :], zqr.at[0], qv.at[1, inner, :], zqr.at[1]),
        X_Q: pair(X_Q, "mapx", xqs.at[0], xqr.at[0], xqs.at[1], xqr.at[1]),
        Y_Q: pair(Y_Q, "mapy", yqs.at[0], yqr.at[0], yqs.at[1], yqr.at[1]),
    }

    def start(group):
        for k, axis, up, src, dst in groups[group]:
            @pl.when(has_hi[axis] if up else has_lo[axis])
            def _():
                message(k, axis, up, src, dst).start()

    def arrived(group):
        for k, axis, up, src, dst in groups[group]:
            @pl.when(has_lo[axis] if up else has_hi[axis])
            def _():
                message(k, axis, up, src, dst).wait_recv()

    def sent(group):
        for k, axis, up, src, dst in groups[group]:
            @pl.when(has_hi[axis] if up else has_lo[axis])
            def _():
                message(k, axis, up, src, dst).wait_send()

    lane_y = lax.broadcasted_iota(jnp.int32, (nx, 128), 1)

    for layer in (z_lo, z_hi):
        pv[layer, inner, :] = jnp.zeros((nx, ny), jnp.float32)
        qv[layer, inner, :] = jnp.zeros((nx, ny), jnp.float32)
        hv[layer, inner, :] = jnp.full((nx, ny), OUTSIDE, jnp.float32)
    tz[0] = jnp.zeros((nx, ny), jnp.float32)
    for z in range(nz):
        for row in (PAD - 1, PAD + nx):
            pv[z + 1, pl.ds(row, 1), :] = jnp.zeros((1, ny), jnp.float32)
            qv[z + 1, pl.ds(row, 1), :] = jnp.zeros((1, ny), jnp.float32)
            hv[z + 1, pl.ds(row, 1), :] = jnp.full((1, ny), OUTSIDE, jnp.float32)

    for side, flags in ((0, has_lo), (1, has_hi)):
        @pl.when(jnp.logical_not(flags["slab"]))
        def _():
            zpr[side] = jnp.zeros((nx, ny), jnp.float32)
            zqr[side] = jnp.zeros((nx, ny), jnp.float32)
            zhr[side] = jnp.full((nx, ny), OUTSIDE, jnp.float32)
            if side == 0:
                above[...] = jnp.zeros((nx, ny), jnp.float32)

        @pl.when(jnp.logical_not(flags["mapx"]))
        def _():
            xr[side, pl.ds(0, nz), :] = jnp.zeros((nz, ny), jnp.float32)
            xr[side, pl.ds(nz, nz), :] = jnp.full((nz, ny), OUTSIDE, jnp.float32)
            xqr[side] = jnp.zeros((nz, ny), jnp.float32)

        @pl.when(jnp.logical_not(flags["mapy"]))
        def _():
            yr[side] = jnp.where(lane_y < nz, jnp.float32(0.0), jnp.float32(OUTSIDE))
            yqr[side] = jnp.zeros((nx, 128), jnp.float32)

    loads[0].wait()
    loads[1].wait()

    def half_inverse(z):
        for r in range(0, nx, 32):
            rows = pl.ds(r, 32)
            cls = classes(lit[z, rows, :])
            hv[z + 1, pl.ds(PAD + r, 32), :] = jnp.exp2(
                pick(cls, HALF_BASE) + pick(cls, HALF_SLOPE) * por[z, rows, :])

    lax.fori_loop(0, nz, lambda z, c: (half_inverse(z), c)[1], 0)
    loads[2].wait()

    def face_x(src, dst, offset):
        for side, row in ((0, PAD + nx - 1), (1, PAD)):
            for z in range(nz):
                dst[side, pl.ds(offset + z, 1), :] = src[z + 1, pl.ds(row, 1), :]

    def face_y(srcs, dst, first_z=1, first_row=PAD):
        for side in range(2):
            for r in range(0, nx, 32):
                acc = jnp.zeros((32, 128), jnp.float32)
                lane = lane_y[:32]
                for i, src in enumerate(srcs):
                    for z in range(nz):
                        k = i * nz + z
                        lanes = pl.ds(0 if side else ny - 128, 128)
                        column = src[z + first_z, pl.ds(first_row + r, 32), lanes]
                        shift = k if side else k + 1
                        moved = pltpu.roll(column, shift, 1) if shift else column
                        acc = jnp.where(lane == k, moved, acc)
                dst[side, pl.ds(r, 32), :] = acc

    face_x(pv, xs, 0)
    face_x(hv, xs, nz)
    face_y((pv, hv), ys)
    pl.semaphore_wait(barrier, peers)
    for group in (X_1, Y_1, Z_H, Z_P):
        start(group)

    loads[3].wait()
    for r in range(0, nx, 32):
        rows = pl.ds(r, 32)

        def add_layer(z, total):
            cls = classes(lit[z, rows, :])
            load = (pick(cls, GRAIN_LESS) + WATER_DENSITY * rec(1.0 - por[z, rows, :])) * solid[z]
            ob[z, rows, :] = total + 0.5 * load
            return total + load

        col[rows, :] = lax.fori_loop(0, nz, add_layer, jnp.zeros((32, ny), jnp.float32))

    def chain(src):
        return message(CHAIN, "slab", True, src, above)

    @pl.when(me["slab"] == 0)
    def _():
        col_send[...] = col[...]
        chain(col_send).start()

    def forward():
        chain(col_send).wait_recv()
        col_send[...] = col[...] + above[...]
        chain(col_send).start()

    def first(z, carry):
        for r in range(0, nx, ROWS):
            at = lambda ref, dz, dx: ref[z + 1 + dz, pl.ds(PAD + r + dx, ROWS), :]
            rows = pl.ds(r, ROWS)
            h, p = at(hv, 0, 0), at(pv, 0, 0)
            t_zm, t_zp = tz[z, rows, :], rec(h + at(hv, 1, 0))
            t_xm, t_xp = rec(h + at(hv, 0, -1)), rec(h + at(hv, 0, 1))
            last = lax.broadcasted_iota(jnp.int32, h.shape, 1) == ny - 1
            t_yp = jnp.where(last, 0.0, rec(h + shifted(h, False)))
            t_ym = shifted(t_yp, True)
            tz[z + 1, rows, :] = t_zp
            tx[z, rows, :] = t_xm
            if r + ROWS == nx:
                tx[z, pl.ds(nx, 1), :] = t_xp[ROWS - 1:, :]
            ty[z, rows, :] = t_yp
            rd[z, rows, :] = 1.0 + ((t_zm + t_zp) + (t_xm + t_xp) + (t_ym + t_yp))
            part[z, rows, :] = (
                p + (t_zm * at(pv, -1, 0) + t_zp * at(pv, 1, 0))
                + (t_xm * at(pv, 0, -1) + t_xp * at(pv, 0, 1))
                + (shifted(t_yp * p, True) + t_yp * shifted(p, False)))
        return carry

    lax.fori_loop(0, nz // 2, first, 0)

    @pl.when(me["slab"] == 1)
    def _():
        forward()

    lax.fori_loop(nz // 2, nz, first, 0)

    x_rows = ((0, 0), (1, nx - 1))
    arrived(X_1)
    for side, row in x_rows:
        link = rec(xs[1 - side, pl.ds(nz, nz), :] + xr[side, pl.ds(nz, nz), :])
        x_link[side] = link
        flow = link * xr[side, pl.ds(0, nz), :]
        for z in range(nz):
            one = pl.ds(row, 1)
            rd[z, one, :] += link[z:z + 1, :]
            part[z, one, :] += flow[z:z + 1, :]
    arrived(Y_1)
    for side in range(2):
        link = pltpu.roll(rec(ys[1 - side] + yr[side]), 128 - nz, 1)
        link = jnp.where(lane_y < nz, link, 0.0)
        y_link[side] = link
        y_flow[side] = link * yr[side]
    arrived(Z_H)
    arrived(Z_P)
    for side, z in ((0, 0), (1, nz - 1)):
        for r in range(0, nx, 32):
            rows = pl.ds(r, 32)
            link = rec(hv[z + 1, pl.ds(PAD + r, 32), :] + zhr[side, rows, :])
            z_link[side, rows, :] = link
            rd[z, rows, :] += link
            part[z, rows, :] += link * zpr[side, rows, :]

    def divide(z):
        for r in range(0, nx, 32):
            rows = pl.ds(r, 32)
            inv = rec(rd[z, rows, :] + at_edges(y_link, z, rows, ny))
            rd[z, rows, :] = STEP_RES * inv
            qv[z + 1, pl.ds(PAD + r, 32), :] = inv * (
                part[z, rows, :] + at_edges(y_flow, z, rows, ny))

    divide(0)
    divide(nz - 1)
    start(Z_Q)
    lax.fori_loop(1, nz - 1, lambda z, c: (divide(z), c)[1], 0)
    face_x(qv, xqs, 0)
    start(X_Q)
    face_y((qv,), yqs)
    start(Y_Q)

    face_y((rd,), edge, 0, 0)
    for side in range(2):
        y_link[side] = y_link[side] * edge[1 - side]

    @pl.when(me["slab"] == 2)
    def _():
        forward()

    def second(z, carry):
        for r in range(0, nx, ROWS):
            at = lambda ref, dz, dx: ref[z + 1 + dz, pl.ds(PAD + r + dx, ROWS), :]
            rows = pl.ds(r, ROWS)
            p, q = at(pv, 0, 0), at(qv, 0, 0)
            t_yp = ty[z, rows, :]
            total = (p + (tz[z, rows, :] * at(qv, -1, 0) + tz[z + 1, rows, :] * at(qv, 1, 0))
                     + (tx[z, rows, :] * at(qv, 0, -1) + tx[z, pl.ds(r + 1, ROWS), :] * at(qv, 0, 1))
                     + (shifted(t_yp * q, True) + t_yp * shifted(q, False)))
            part[z, rows, :] = q + STEP_KEEP * (q - p) + (total * rd[z, rows, :] - STEP_RES * q)
        return carry

    lax.fori_loop(0, nz, second, 0)

    arrived(X_Q)
    for side, row in x_rows:
        flow = x_link[side] * xqr[side]
        for z in range(nz):
            one = pl.ds(row, 1)
            part[z, one, :] += rd[z, one, :] * flow[z:z + 1, :]
    arrived(Y_Q)
    for side in range(2):
        y_term[side] = y_link[side] * yqr[side]
    arrived(Z_Q)
    for side, z in ((0, 0), (1, nz - 1)):
        for r in range(0, nx, 32):
            rows = pl.ds(r, 32)
            part[z, rows, :] += rd[z, rows, :] * z_link[side, rows, :] * zqr[side, rows, :]
    for z in range(nz):
        solid_wide[z] = jnp.full((8, 128), solid[z], jnp.float32)

    @pl.when(me["slab"] == 3)
    def _():
        chain(col_send).wait_recv()

    for group in groups:
        sent(group)

    @pl.when(has_hi["slab"])
    def _():
        chain(col_send).wait_send()


def finish(part, ob, lit, above, y_term, solid_wide, pn_out, phi_out, thick_out, buf, store_sem):
    nz, nx, ny = lit.shape
    outs = (pn_out, phi_out, thick_out)

    def store(i, z):
        return pltpu.make_async_copy(buf.at[i, z], outs[i].at[z], store_sem.at[i, z])

    def layer(z, carry):
        solid = jnp.concatenate([solid_wide[z]] * (ny // 128), axis=1)
        solid = jnp.concatenate([solid] * (ROWS // 8), axis=0)
        for r in range(0, nx, ROWS):
            rows = pl.ds(r, ROWS)
            pn = part[z, rows, :] + at_edges(y_term, z, rows, ny)
            stress = jnp.maximum(above[rows, :] + ob[z, rows, :] - pn, 0.0)
            cls = classes(lit[z, rows, :])
            phi = pick(cls, PHI_SURFACE) * jnp.exp2(pick(cls, ATHY_NEG) * stress)
            buf[0, z, rows, :] = pn
            buf[1, z, rows, :] = phi
            buf[2, z, rows, :] = solid * rec(1.0 - phi)
        for i in range(3):
            store(i, z).start()
        return carry

    lax.fori_loop(0, nz, layer, 0)

    def stored(z, carry):
        for i in range(3):
            store(i, z).wait()
        return carry

    lax.fori_loop(0, nz, stored, 0)


def body(sizes, pressure, porosity, lithology, layer_solid):
    nz, nx, ny = pressure.shape
    f32, i32 = jnp.float32, jnp.int32
    shaped = jax.ShapeDtypeStruct
    block, plane = (nz, nx, ny), (nx, ny)
    padded = (nz + 2, nx + 2 * PAD, ny)
    z_face, x_face, y_face = (2, nx, ny), (2, nz, ny), (2, nx, 128)
    vmem = pl.BlockSpec(memory_space=pltpu.VMEM)
    hbm = pl.BlockSpec(memory_space=pltpu.HBM)
    held = (shaped(block, f32), shaped(block, f32), shaped(block, i32), shaped(plane, f32),
            shaped(y_face, f32), shaped((nz, 8, 128), f32))
    held = pl.pallas_call(
        functools.partial(exchange, sizes),
        out_shape=held,
        in_specs=[hbm] * 4,
        out_specs=(vmem,) * len(held),
        scratch_shapes=[pltpu.VMEM(shape, f32) for shape in (
            padded, padded, padded, (nz + 1, nx, ny), (nz, nx + PAD, ny),
            block, block, block, plane, plane,
            (2, 2 * nz, ny), (2, 2 * nz, ny), y_face, y_face, z_face, z_face, z_face,
            x_face, x_face, y_face, y_face, z_face, x_face, y_face, y_face, y_face)] + [
            pltpu.SMEM((nz,), f32),
            pltpu.SemaphoreType.DMA((4,)),
            pltpu.SemaphoreType.DMA((MESSAGES,)),
            pltpu.SemaphoreType.DMA((MESSAGES,)),
        ],
        compiler_params=pltpu.CompilerParams(
            collective_id=0, has_side_effects=True, vmem_limit_bytes=24 * 2**20),
        name="exchange",
    )(*(pltpu.with_memory_space_constraint(a, pltpu.HBM) for a in (pressure, porosity, lithology, layer_solid)))
    return pl.pallas_call(
        finish,
        out_shape=(shaped(block, f32),) * 3,
        in_specs=[vmem] * len(held),
        out_specs=(hbm,) * 3,
        scratch_shapes=[
            pltpu.VMEM((3,) + block, f32),
            pltpu.SemaphoreType.DMA((3, nz)),
        ],
        compiler_params=pltpu.CompilerParams(vmem_limit_bytes=24 * 2**20),
        name="finish",
    )(*held)


def solution(mesh):
    sizes = dict(mesh.shape)
    spec = P("slab", "mapx", "mapy")
    return jax.shard_map(
        functools.partial(body, sizes), mesh=mesh,
        in_specs=(spec, spec, spec, P("slab")), out_specs=(spec, spec, spec), check_vma=False)
```

```python
import functools
import math

import jax
import jax.numpy as jnp
from jax import lax
from jax.experimental import pallas as pl
from jax.experimental.pallas import tpu as pltpu
from jax.sharding import PartitionSpec as P

PHI_SURFACE = (0.45, 0.55, 0.65, 0.4)
ATHY_RATE = (0.25, 0.45, 0.8, 0.35)
MOB_BASE = (1.0, 0.0, -1.5, -0.5)
MOB_SLOPE = (6.0, 5.0, 8.0, 4.0)
GRAIN_DENSITY = (2.65, 2.68, 2.72, 2.71)
WATER_DENSITY = 1.03
SPECTRUM_MID = 1.0
SPECTRUM_HALF = 0.95
SIGMA_RATIO = SPECTRUM_MID / SPECTRUM_HALF
RHO_FIRST = 1.0 / SIGMA_RATIO
RHO_SECOND = 1.0 / (2.0 * SIGMA_RATIO - RHO_FIRST)
STEP_KEEP = RHO_SECOND * RHO_FIRST
STEP_RES = 2.0 * RHO_SECOND / SPECTRUM_HALF

LOG2_E = 1.0 / math.log(2.0)

HALF_BASE = tuple(-(b - 0.35 * s) * LOG2_E - 1.0 for b, s in zip(MOB_BASE, MOB_SLOPE))
HALF_SLOPE = tuple(-s * LOG2_E for s in MOB_SLOPE)
GRAIN_LESS = tuple(g - WATER_DENSITY for g in GRAIN_DENSITY)
ATHY_NEG = tuple(-a * LOG2_E for a in ATHY_RATE)
OUTSIDE = 2.0e38

MESH = pl.DeviceIdType.MESH
PAD = 8
ROWS = 16
FOLD = 4
Z_P, Z_H, X_1, Y_1, Z_Q, X_Q, Y_Q, CHAIN = 0, 2, 4, 6, 8, 10, 12, 14
MESSAGES = 15


def rec(x):
    return pl.reciprocal(x, approx=True)


def classes(lith):
    return lith >= 2, (lith & 1) == 1


def pick(cls, table):
    high, odd = cls
    a, b, c, d = (jnp.float32(t) for t in table)
    return jnp.where(high, jnp.where(odd, d, c), jnp.where(odd, b, a))


def shifted(value, up):
    rows, ny = value.shape
    lane = lax.broadcasted_iota(jnp.int32, (rows, 128), 1)
    parts = [pltpu.roll(value[:, y:y + 128], 1 if up else 127, 1) for y in range(0, ny, 128)]
    if up:
        joined = [jnp.where(lane == 0, a, b) for a, b in zip(parts[-1:] + parts[:-1], parts)]
    else:
        joined = [jnp.where(lane == 127, a, b) for a, b in zip(parts[1:] + parts[:1], parts)]
    return jnp.concatenate(joined, axis=1)


def at_edges(halo, index, rows, ny):
    lo = pltpu.roll(halo[0, rows, :], lax.rem(128 - index, 128), 1)
    hi = pltpu.roll(halo[1, rows, :], 127 - index, 1)
    lane = lax.broadcasted_iota(jnp.int32, lo.shape, 1)
    zeros = [jnp.zeros(lo.shape, jnp.float32)] * (ny // 128 - 2)
    ends = [jnp.where(lane == 0, lo, 0.0)] + zeros + [jnp.where(lane == 127, hi, 0.0)]
    return jnp.concatenate(ends, axis=1)


def exchange(sizes, p_hbm, por_hbm, lit_hbm, solid_hbm,
             part, ob, lit, above, y_term, solid_wide,
             pv, qv, hv, tz, tx, ty, rd, por, col, col_send, xs, xr, ys, yr,
             zpr, zhr, zqr, xqs, xqr, yqs, yqr, z_link, x_link, x_flow,
             y_link, y_flow, link_fold, edge,
             solid, load_sem, send_sem, recv_sem):
    nz, nx, ny = por.shape
    axes = ("slab", "mapx", "mapy")
    me = {a: lax.axis_index(a) for a in axes}
    has_lo = {a: me[a] > 0 for a in axes}
    has_hi = {a: me[a] < sizes[a] - 1 for a in axes}
    peers = sum(jnp.where(f, 1, 0) for flags in (has_lo, has_hi) for f in flags.values())
    inner = pl.ds(PAD, nx)

    spans = (pl.ds(0, 1), pl.ds(nz - 1, 1), pl.ds(1, nz - 2))
    loads = []
    for i, span in enumerate(spans):
        loads.append(pltpu.make_async_copy(por_hbm.at[span], por.at[span], load_sem.at[2 * i]))
        loads.append(pltpu.make_async_copy(lit_hbm.at[span], lit.at[span], load_sem.at[2 * i + 1]))
    load_p = pltpu.make_async_copy(p_hbm, pv.at[pl.ds(1, nz), inner, :], load_sem.at[6])
    load_solid = pltpu.make_async_copy(solid_hbm, solid, load_sem.at[7])
    for c in loads + [load_p, load_solid]:
        c.start()

    barrier = pltpu.get_barrier_semaphore()
    for a in axes:
        @pl.when(has_lo[a])
        def _():
            pl.semaphore_signal(barrier, inc=1, device_id={a: me[a] - 1}, device_id_type=MESH)

        @pl.when(has_hi[a])
        def _():
            pl.semaphore_signal(barrier, inc=1, device_id={a: me[a] + 1}, device_id_type=MESH)

    def message(k, axis, up, src, dst):
        target = me[axis] + 1 if up else me[axis] - 1
        return pltpu.make_async_remote_copy(
            src_ref=src, dst_ref=dst, send_sem=send_sem.at[k], recv_sem=recv_sem.at[k],
            device_id={axis: target}, device_id_type=MESH)

    def pair(k, axis, src_up, dst_up, src_down, dst_down):
        return [(k, axis, True, src_up, dst_up), (k + 1, axis, False, src_down, dst_down)]

    z_lo, z_hi = 0, nz + 1
    groups = {
        Z_P: pair(Z_P, "slab", p_hbm.at[nz - 1], zpr.at[0], p_hbm.at[0], zpr.at[1]),
        Z_H: pair(Z_H, "slab", hv.at[nz, inner, :], zhr.at[0], hv.at[1, inner, :], zhr.at[1]),
        X_1: pair(X_1, "mapx", xs.at[0], xr.at[0], xs.at[1], xr.at[1]),
        Y_1: pair(Y_1, "mapy", ys.at[0], yr.at[0], ys.at[1], yr.at[1]),
        Z_Q: pair(Z_Q, "slab", qv.at[nz, inner, :], zqr.at[0], qv.at[1, inner, :], zqr.at[1]),
        X_Q: pair(X_Q, "mapx", xqs.at[0], xqr.at[0], xqs.at[1], xqr.at[1]),
        Y_Q: pair(Y_Q, "mapy", yqs.at[0], yqr.at[0], yqs.at[1], yqr.at[1]),
    }

    def start(group):
        for k, axis, up, src, dst in groups[group]:
            @pl.when(has_hi[axis] if up else has_lo[axis])
            def _():
                message(k, axis, up, src, dst).start()

    def arrived(group):
        for k, axis, up, src, dst in groups[group]:
            @pl.when(has_lo[axis] if up else has_hi[axis])
            def _():
                message(k, axis, up, src, dst).wait_recv()

    def sent(group):
        for k, axis, up, src, dst in groups[group]:
            @pl.when(has_hi[axis] if up else has_lo[axis])
            def _():
                message(k, axis, up, src, dst).wait_send()

    lane_f = lax.broadcasted_iota(jnp.int32, (nx // FOLD, 128), 1)

    for layer in (z_lo, z_hi):
        pv[layer, inner, :] = jnp.zeros((nx, ny), jnp.float32)
        qv[layer, inner, :] = jnp.zeros((nx, ny), jnp.float32)
        hv[layer, inner, :] = jnp.full((nx, ny), OUTSIDE, jnp.float32)
    tz[0] = jnp.zeros((nx, ny), jnp.float32)
    for z in range(nz):
        for row in (PAD - 1, PAD + nx):
            pv[z + 1, pl.ds(row, 1), :] = jnp.zeros((1, ny), jnp.float32)
            qv[z + 1, pl.ds(row, 1), :] = jnp.zeros((1, ny), jnp.float32)
            hv[z + 1, pl.ds(row, 1), :] = jnp.full((1, ny), OUTSIDE, jnp.float32)

    for side, flags in ((0, has_lo), (1, has_hi)):
        @pl.when(jnp.logical_not(flags["slab"]))
        def _():
            zpr[side] = jnp.zeros((nx, ny), jnp.float32)
            zqr[side] = jnp.zeros((nx, ny), jnp.float32)
            zhr[side] = jnp.full((nx, ny), OUTSIDE, jnp.float32)
            if side == 0:
                above[...] = jnp.zeros((nx, ny), jnp.float32)

        @pl.when(jnp.logical_not(flags["mapx"]))
        def _():
            xr[side, pl.ds(0, nz), :] = jnp.zeros((nz, ny), jnp.float32)
            xr[side, pl.ds(nz, nz), :] = jnp.full((nz, ny), OUTSIDE, jnp.float32)
            xqr[side] = jnp.zeros((nz, ny), jnp.float32)

        @pl.when(jnp.logical_not(flags["mapy"]))
        def _():
            layer = lax.rem(lane_f, 2 * nz)
            yr[side] = jnp.where(layer < nz, jnp.float32(0.0), jnp.float32(OUTSIDE))
            yqr[side] = jnp.zeros(yqr.shape[1:], jnp.float32)


    def half_inverse(z):
        for r in range(0, nx, 32):
            rows = pl.ds(r, 32)
            cls = classes(lit[z, rows, :])
            hv[z + 1, pl.ds(PAD + r, 32), :] = jnp.exp2(
                pick(cls, HALF_BASE) + pick(cls, HALF_SLOPE) * por[z, rows, :])

    for i, z in enumerate((0, nz - 1)):
        loads[2 * i].wait()
        loads[2 * i + 1].wait()
        half_inverse(z)
    pl.semaphore_wait(barrier, peers)
    start(Z_H)
    start(Z_P)
    loads[4].wait()
    loads[5].wait()
    lax.fori_loop(1, nz - 1, lambda z, c: (half_inverse(z), c)[1], 0)
    load_p.wait()

    def face_x(src, dst, offset):
        for side, row in ((0, PAD + nx - 1), (1, PAD)):
            for z in range(nz):
                dst[side, pl.ds(offset + z, 1), :] = src[z + 1, pl.ds(row, 1), :]

    stride, part_rows = 2 * nz, nx // FOLD

    def face_y(srcs, dst, first_z=1, first_row=PAD):
        for side in range(2):
            acc = jnp.zeros((part_rows, 128), jnp.float32)
            for i in range(FOLD):
                for j, src in enumerate(srcs):
                    for z in range(nz):
                        k = i * stride + j * nz + z
                        lanes = pl.ds(0 if side else ny - 128, 128)
                        rows = pl.ds(first_row + i * part_rows, part_rows)
                        column = src[z + first_z, rows, lanes]
                        shift = k if side else k + 1
                        moved = pltpu.roll(column, shift, 1) if shift else column
                        acc = jnp.where(lane_f == k, moved, acc)
            dst[side] = acc

    def unfold(value, dst, side):
        for i in range(FOLD):
            moved = pltpu.roll(value, 128 - i * stride, 1) if i else value
            dst[side, pl.ds(i * part_rows, part_rows), :] = moved

    face_x(pv, xs, 0)
    face_x(hv, xs, nz)
    start(X_1)
    face_y((pv, hv), ys)
    start(Y_1)

    def first(z, carry):
        for r in range(0, nx, ROWS):
            at = lambda ref, dz, dx: ref[z + 1 + dz, pl.ds(PAD + r + dx, ROWS), :]
            rows = pl.ds(r, ROWS)
            h, p = at(hv, 0, 0), at(pv, 0, 0)
            t_zm, t_zp = rec(h + at(hv, -1, 0)), rec(h + at(hv, 1, 0))
            t_xm, t_xp = rec(h + at(hv, 0, -1)), rec(h + at(hv, 0, 1))
            last = lax.broadcasted_iota(jnp.int32, h.shape, 1) == ny - 1
            t_yp = jnp.where(last, 0.0, rec(h + shifted(h, False)))
            t_ym = shifted(t_yp, True)
            tz[z + 1, rows, :] = t_zp
            tx[z, rows, :] = t_xm
            if r + ROWS == nx:
                tx[z, pl.ds(nx, 1), :] = t_xp[ROWS - 1:, :]
            ty[z, rows, :] = t_yp
            rd[z, rows, :] = 1.0 + ((t_zm + t_zp) + (t_xm + t_xp) + (t_ym + t_yp))
            part[z, rows, :] = (
                p + (t_zm * at(pv, -1, 0) + t_zp * at(pv, 1, 0))
                + (t_xm * at(pv, 0, -1) + t_xp * at(pv, 0, 1))
                + (shifted(t_yp * p, True) + t_yp * shifted(p, False)))
        return carry

    first(0, 0)
    first(nz - 1, 0)

    load_solid.wait()
    for r in range(0, nx, 32):
        rows = pl.ds(r, 32)

        def add_layer(z, total):
            cls = classes(lit[z, rows, :])
            load = (pick(cls, GRAIN_LESS) + WATER_DENSITY * rec(1.0 - por[z, rows, :])) * solid[z]
            ob[z, rows, :] = total + 0.5 * load
            return total + load

        col[rows, :] = lax.fori_loop(0, nz, add_layer, jnp.zeros((32, ny), jnp.float32))

    def chain(src):
        return message(CHAIN, "slab", True, src, above)

    @pl.when(me["slab"] == 0)
    def _():
        col_send[...] = col[...]
        chain(col_send).start()

    def forward():
        chain(col_send).wait_recv()
        col_send[...] = col[...] + above[...]
        chain(col_send).start()

    x_rows = ((0, 0), (1, nx - 1))
    arrived(X_1)
    for side, row in x_rows:
        link = rec(xs[1 - side, pl.ds(nz, nz), :] + xr[side, pl.ds(nz, nz), :])
        x_link[side] = link
        x_flow[side] = link * xr[side, pl.ds(0, nz), :]

    def add_x(z):
        for side, row in x_rows:
            one = pl.ds(row, 1)
            rd[z, one, :] += x_link[side, pl.ds(z, 1), :]
            part[z, one, :] += x_flow[side, pl.ds(z, 1), :]

    arrived(Y_1)
    for side in range(2):
        link = pltpu.roll(rec(ys[1 - side] + yr[side]), 128 - nz, 1)
        link_fold[side] = link
        unfold(link, y_link, side)
        unfold(link * yr[side], y_flow, side)

    def divide(z):
        for r in range(0, nx, 32):
            rows = pl.ds(r, 32)
            inv = rec(rd[z, rows, :] + at_edges(y_link, z, rows, ny))
            rd[z, rows, :] = STEP_RES * inv
            qv[z + 1, pl.ds(PAD + r, 32), :] = inv * (
                part[z, rows, :] + at_edges(y_flow, z, rows, ny))

    add_x(0)
    add_x(nz - 1)
    arrived(Z_H)
    arrived(Z_P)
    for side, z in ((0, 0), (1, nz - 1)):
        for r in range(0, nx, 32):
            rows = pl.ds(r, 32)
            link = rec(hv[z + 1, pl.ds(PAD + r, 32), :] + zhr[side, rows, :])
            z_link[side, rows, :] = link
            rd[z, rows, :] += link
            part[z, rows, :] += link * zpr[side, rows, :]
        divide(z)
    start(Z_Q)

    lax.fori_loop(1, nz // 2, first, 0)

    @pl.when(me["slab"] == 1)
    def _():
        forward()

    lax.fori_loop(nz // 2, nz - 1, first, 0)
    for z in range(1, nz - 1):
        add_x(z)
    lax.fori_loop(1, nz - 1, lambda z, c: (divide(z), c)[1], 0)
    face_x(qv, xqs, 0)
    start(X_Q)
    face_y((qv,), yqs)
    start(Y_Q)

    face_y((rd,), edge, 0, 0)
    for side in range(2):
        link_fold[side] = link_fold[side] * edge[1 - side]

    @pl.when(me["slab"] == 2)
    def _():
        forward()

    def second(z, carry):
        for r in range(0, nx, ROWS):
            at = lambda ref, dz, dx: ref[z + 1 + dz, pl.ds(PAD + r + dx, ROWS), :]
            rows = pl.ds(r, ROWS)
            p, q = at(pv, 0, 0), at(qv, 0, 0)
            t_yp = ty[z, rows, :]
            total = (p + (tz[z, rows, :] * at(qv, -1, 0) + tz[z + 1, rows, :] * at(qv, 1, 0))
                     + (tx[z, rows, :] * at(qv, 0, -1) + tx[z, pl.ds(r + 1, ROWS), :] * at(qv, 0, 1))
                     + (shifted(t_yp * q, True) + t_yp * shifted(q, False)))
            part[z, rows, :] = q + STEP_KEEP * (q - p) + (total * rd[z, rows, :] - STEP_RES * q)
        return carry

    lax.fori_loop(0, nz, second, 0)

    arrived(X_Q)
    for side, row in x_rows:
        flow = x_link[side] * xqr[side]
        for z in range(nz):
            one = pl.ds(row, 1)
            part[z, one, :] += rd[z, one, :] * flow[z:z + 1, :]
    arrived(Y_Q)
    for side in range(2):
        unfold(link_fold[side] * yqr[side], y_term, side)
    arrived(Z_Q)
    for side, z in ((0, 0), (1, nz - 1)):
        for r in range(0, nx, 32):
            rows = pl.ds(r, 32)
            part[z, rows, :] += rd[z, rows, :] * z_link[side, rows, :] * zqr[side, rows, :]
    for z in range(nz):
        solid_wide[z] = jnp.full((8, 128), solid[z], jnp.float32)

    @pl.when(me["slab"] == 3)
    def _():
        chain(col_send).wait_recv()

    for group in groups:
        sent(group)

    @pl.when(has_hi["slab"])
    def _():
        chain(col_send).wait_send()


def finish(part, ob, lit, above, y_term, solid_wide, pn_out, phi_out, thick_out, buf, store_sem):
    nz, nx, ny = lit.shape
    outs = (pn_out, phi_out, thick_out)

    def store(i, z):
        return pltpu.make_async_copy(buf.at[i, z], outs[i].at[z], store_sem.at[i, z])

    def layer(z, carry):
        solid = jnp.concatenate([solid_wide[z]] * (ny // 128), axis=1)
        solid = jnp.concatenate([solid] * (ROWS // 8), axis=0)
        for r in range(0, nx, ROWS):
            rows = pl.ds(r, ROWS)
            pn = part[z, rows, :] + at_edges(y_term, z, rows, ny)
            stress = jnp.maximum(above[rows, :] + ob[z, rows, :] - pn, 0.0)
            cls = classes(lit[z, rows, :])
            phi = pick(cls, PHI_SURFACE) * jnp.exp2(pick(cls, ATHY_NEG) * stress)
            buf[0, z, rows, :] = pn
            buf[1, z, rows, :] = phi
            buf[2, z, rows, :] = solid * rec(1.0 - phi)
        for i in range(3):
            store(i, z).start()
        return carry

    lax.fori_loop(0, nz, layer, 0)

    def stored(z, carry):
        for i in range(3):
            store(i, z).wait()
        return carry

    lax.fori_loop(0, nz, stored, 0)


def body(sizes, pressure, porosity, lithology, layer_solid):
    nz, nx, ny = pressure.shape
    f32, i32 = jnp.float32, jnp.int32
    shaped = jax.ShapeDtypeStruct
    block, plane = (nz, nx, ny), (nx, ny)
    padded = (nz + 2, nx + 2 * PAD, ny)
    folded = (2, nx // FOLD, 128)
    z_face, x_face, y_face = (2, nx, ny), (2, nz, ny), (2, nx, 128)
    vmem = pl.BlockSpec(memory_space=pltpu.VMEM)
    hbm = pl.BlockSpec(memory_space=pltpu.HBM)
    held = (shaped(block, f32), shaped(block, f32), shaped(block, i32), shaped(plane, f32),
            shaped(y_face, f32), shaped((nz, 8, 128), f32))
    held = pl.pallas_call(
        functools.partial(exchange, sizes),
        out_shape=held,
        in_specs=[hbm] * 4,
        out_specs=(vmem,) * len(held),
        scratch_shapes=[pltpu.VMEM(shape, f32) for shape in (
            padded, padded, padded, (nz + 1, nx, ny), (nz, nx + PAD, ny),
            block, block, block, plane, plane,
            (2, 2 * nz, ny), (2, 2 * nz, ny), folded, folded, z_face, z_face, z_face,
            x_face, x_face, folded, folded, z_face, x_face, x_face,
            y_face, y_face, folded, folded)] + [
            pltpu.SMEM((nz,), f32),
            pltpu.SemaphoreType.DMA((8,)),
            pltpu.SemaphoreType.DMA((MESSAGES,)),
            pltpu.SemaphoreType.DMA((MESSAGES,)),
        ],
        compiler_params=pltpu.CompilerParams(
            collective_id=0, has_side_effects=True, vmem_limit_bytes=24 * 2**20),
        name="exchange",
    )(*(pltpu.with_memory_space_constraint(a, pltpu.HBM) for a in (pressure, porosity, lithology, layer_solid)))
    return pl.pallas_call(
        finish,
        out_shape=(shaped(block, f32),) * 3,
        in_specs=[vmem] * len(held),
        out_specs=(hbm,) * 3,
        scratch_shapes=[
            pltpu.VMEM((3,) + block, f32),
            pltpu.SemaphoreType.DMA((3, nz)),
        ],
        compiler_params=pltpu.CompilerParams(vmem_limit_bytes=24 * 2**20),
        name="finish",
    )(*held)


def solution(mesh):
    sizes = dict(mesh.shape)
    spec = P("slab", "mapx", "mapy")
    return jax.shard_map(
        functools.partial(body, sizes), mesh=mesh,
        in_specs=(spec, spec, spec, P("slab")), out_specs=(spec, spec, spec), check_vma=False)
```

```python
import functools
import math

import jax
import jax.numpy as jnp
from jax import lax
from jax.experimental import pallas as pl
from jax.experimental.pallas import tpu as pltpu
from jax.sharding import PartitionSpec as P

PHI_SURFACE = (0.45, 0.55, 0.65, 0.4)
ATHY_RATE = (0.25, 0.45, 0.8, 0.35)
MOB_BASE = (1.0, 0.0, -1.5, -0.5)
MOB_SLOPE = (6.0, 5.0, 8.0, 4.0)
GRAIN_DENSITY = (2.65, 2.68, 2.72, 2.71)
WATER_DENSITY = 1.03
SPECTRUM_MID = 1.0
SPECTRUM_HALF = 0.95
SIGMA_RATIO = SPECTRUM_MID / SPECTRUM_HALF
RHO_FIRST = 1.0 / SIGMA_RATIO
RHO_SECOND = 1.0 / (2.0 * SIGMA_RATIO - RHO_FIRST)
STEP_KEEP = RHO_SECOND * RHO_FIRST
STEP_RES = 2.0 * RHO_SECOND / SPECTRUM_HALF

LOG2_E = 1.0 / math.log(2.0)

HALF_BASE = tuple(-(b - 0.35 * s) * LOG2_E - 1.0 for b, s in zip(MOB_BASE, MOB_SLOPE))
HALF_SLOPE = tuple(-s * LOG2_E for s in MOB_SLOPE)
GRAIN_LESS = tuple(g - WATER_DENSITY for g in GRAIN_DENSITY)
ATHY_NEG = tuple(-a * LOG2_E for a in ATHY_RATE)
OUTSIDE = 2.0e38

MESH = pl.DeviceIdType.MESH
PAD = 8
ROWS = 16
FOLD = 4
Z_P, Z_H, X_1, Y_1, Z_Q, X_Q, Y_Q, CHAIN = 0, 2, 4, 6, 8, 10, 12, 14
MESSAGES = 15


def rec(x):
    return pl.reciprocal(x, approx=True)


def classes(lith):
    return lith >= 2, (lith & 1) == 1


def pick(cls, table):
    high, odd = cls
    a, b, c, d = (jnp.float32(t) for t in table)
    return jnp.where(high, jnp.where(odd, d, c), jnp.where(odd, b, a))


def shifted(value, up):
    rows, ny = value.shape
    lane = lax.broadcasted_iota(jnp.int32, (rows, 128), 1)
    parts = [pltpu.roll(value[:, y:y + 128], 1 if up else 127, 1) for y in range(0, ny, 128)]
    if up:
        joined = [jnp.where(lane == 0, a, b) for a, b in zip(parts[-1:] + parts[:-1], parts)]
    else:
        joined = [jnp.where(lane == 127, a, b) for a, b in zip(parts[1:] + parts[:1], parts)]
    return jnp.concatenate(joined, axis=1)


def at_edges(halo, index, rows, ny):
    lo = pltpu.roll(halo[0, rows, :], lax.rem(128 - index, 128), 1)
    hi = pltpu.roll(halo[1, rows, :], 127 - index, 1)
    lane = lax.broadcasted_iota(jnp.int32, lo.shape, 1)
    zeros = [jnp.zeros(lo.shape, jnp.float32)] * (ny // 128 - 2)
    ends = [jnp.where(lane == 0, lo, 0.0)] + zeros + [jnp.where(lane == 127, hi, 0.0)]
    return jnp.concatenate(ends, axis=1)


def exchange(sizes, p_hbm, por_hbm, lit_hbm, solid_hbm,
             part, ob, lit, above, y_term, solid_wide,
             pv, qv, hv, tz, tx, ty, rd, por, col, col_send, xs, xr, ys, yr,
             zpr, zhr, zqr, xqs, xqr, yqs, yqr, z_link, x_link, x_flow,
             y_link, y_flow, link_fold, edge,
             solid, load_sem, send_sem, recv_sem):
    nz, nx, ny = por.shape
    axes = ("slab", "mapx", "mapy")
    me = {a: lax.axis_index(a) for a in axes}
    has_lo = {a: me[a] > 0 for a in axes}
    has_hi = {a: me[a] < sizes[a] - 1 for a in axes}
    peers = sum(jnp.where(f, 1, 0) for flags in (has_lo, has_hi) for f in flags.values())
    inner = pl.ds(PAD, nx)

    spans = (pl.ds(0, 1), pl.ds(nz - 1, 1), pl.ds(1, nz - 2))
    loads = []
    for i, span in enumerate(spans):
        loads.append(pltpu.make_async_copy(por_hbm.at[span], por.at[span], load_sem.at[2 * i]))
        loads.append(pltpu.make_async_copy(lit_hbm.at[span], lit.at[span], load_sem.at[2 * i + 1]))
    load_p = pltpu.make_async_copy(p_hbm, pv.at[pl.ds(1, nz), inner, :], load_sem.at[6])
    load_solid = pltpu.make_async_copy(solid_hbm, solid, load_sem.at[7])
    for c in loads + [load_p, load_solid]:
        c.start()

    barrier = pltpu.get_barrier_semaphore()
    for a in axes:
        @pl.when(has_lo[a])
        def _():
            pl.semaphore_signal(barrier, inc=1, device_id={a: me[a] - 1}, device_id_type=MESH)

        @pl.when(has_hi[a])
        def _():
            pl.semaphore_signal(barrier, inc=1, device_id={a: me[a] + 1}, device_id_type=MESH)

    def message(k, axis, up, src, dst):
        target = me[axis] + 1 if up else me[axis] - 1
        return pltpu.make_async_remote_copy(
            src_ref=src, dst_ref=dst, send_sem=send_sem.at[k], recv_sem=recv_sem.at[k],
            device_id={axis: target}, device_id_type=MESH)

    def pair(k, axis, src_up, dst_up, src_down, dst_down):
        return [(k, axis, True, src_up, dst_up), (k + 1, axis, False, src_down, dst_down)]

    z_lo, z_hi = 0, nz + 1
    groups = {
        Z_P: pair(Z_P, "slab", p_hbm.at[nz - 1], zpr.at[0], p_hbm.at[0], zpr.at[1]),
        Z_H: pair(Z_H, "slab", hv.at[nz, inner, :], zhr.at[0], hv.at[1, inner, :], zhr.at[1]),
        X_1: pair(X_1, "mapx", xs.at[0], xr.at[0], xs.at[1], xr.at[1]),
        Y_1: pair(Y_1, "mapy", ys.at[0], yr.at[0], ys.at[1], yr.at[1]),
        Z_Q: pair(Z_Q, "slab", qv.at[nz, inner, :], zqr.at[0], qv.at[1, inner, :], zqr.at[1]),
        X_Q: pair(X_Q, "mapx", xqs.at[0], xqr.at[0], xqs.at[1], xqr.at[1]),
        Y_Q: pair(Y_Q, "mapy", yqs.at[0], yqr.at[0], yqs.at[1], yqr.at[1]),
    }

    def start(group):
        for k, axis, up, src, dst in groups[group]:
            @pl.when(has_hi[axis] if up else has_lo[axis])
            def _():
                message(k, axis, up, src, dst).start()

    def arrived(group):
        for k, axis, up, src, dst in groups[group]:
            @pl.when(has_lo[axis] if up else has_hi[axis])
            def _():
                message(k, axis, up, src, dst).wait_recv()

    def sent(group):
        for k, axis, up, src, dst in groups[group]:
            @pl.when(has_hi[axis] if up else has_lo[axis])
            def _():
                message(k, axis, up, src, dst).wait_send()

    lane_f = lax.broadcasted_iota(jnp.int32, (nx // FOLD, 128), 1)

    for layer in (z_lo, z_hi):
        pv[layer, inner, :] = jnp.zeros((nx, ny), jnp.float32)
        qv[layer, inner, :] = jnp.zeros((nx, ny), jnp.float32)
        hv[layer, inner, :] = jnp.full((nx, ny), OUTSIDE, jnp.float32)
    tz[0] = jnp.zeros((nx, ny), jnp.float32)
    for z in range(nz):
        for row in (PAD - 1, PAD + nx):
            pv[z + 1, pl.ds(row, 1), :] = jnp.zeros((1, ny), jnp.float32)
            qv[z + 1, pl.ds(row, 1), :] = jnp.zeros((1, ny), jnp.float32)
            hv[z + 1, pl.ds(row, 1), :] = jnp.full((1, ny), OUTSIDE, jnp.float32)

    for side, flags in ((0, has_lo), (1, has_hi)):
        @pl.when(jnp.logical_not(flags["slab"]))
        def _():
            zpr[side] = jnp.zeros((nx, ny), jnp.float32)
            zqr[side] = jnp.zeros((nx, ny), jnp.float32)
            zhr[side] = jnp.full((nx, ny), OUTSIDE, jnp.float32)
            if side == 0:
                above[...] = jnp.zeros((nx, ny), jnp.float32)

        @pl.when(jnp.logical_not(flags["mapx"]))
        def _():
            xr[side, pl.ds(0, nz), :] = jnp.zeros((nz, ny), jnp.float32)
            xr[side, pl.ds(nz, nz), :] = jnp.full((nz, ny), OUTSIDE, jnp.float32)
            xqr[side] = jnp.zeros((nz, ny), jnp.float32)

        @pl.when(jnp.logical_not(flags["mapy"]))
        def _():
            layer = lax.rem(lane_f, 2 * nz)
            yr[side] = jnp.where(layer < nz, jnp.float32(0.0), jnp.float32(OUTSIDE))
            yqr[side] = jnp.zeros(yqr.shape[1:], jnp.float32)


    def half_inverse(z):
        for r in range(0, nx, 32):
            rows = pl.ds(r, 32)
            cls = classes(lit[z, rows, :])
            hv[z + 1, pl.ds(PAD + r, 32), :] = jnp.exp2(
                pick(cls, HALF_BASE) + pick(cls, HALF_SLOPE) * por[z, rows, :])

    for load in loads[:4]:
        load.wait()
    lax.fori_loop(0, 2, lambda i, c: (half_inverse(i * (nz - 1)), c)[1], 0)
    pl.semaphore_wait(barrier, peers)
    start(Z_H)
    start(Z_P)
    loads[4].wait()
    loads[5].wait()
    lax.fori_loop(1, nz - 1, lambda z, c: (half_inverse(z), c)[1], 0)
    load_solid.wait()
    for r in range(0, nx, 32):
        rows = pl.ds(r, 32)

        def add_layer(z, total):
            cls = classes(lit[z, rows, :])
            load = (pick(cls, GRAIN_LESS) + WATER_DENSITY * rec(1.0 - por[z, rows, :])) * solid[z]
            ob[z, rows, :] = total + 0.5 * load
            return total + load

        col[rows, :] = lax.fori_loop(0, nz, add_layer, jnp.zeros((32, ny), jnp.float32))

    def chain(src):
        return message(CHAIN, "slab", True, src, above)

    @pl.when(me["slab"] == 0)
    def _():
        col_send[...] = col[...]
        chain(col_send).start()

    def forward():
        chain(col_send).wait_recv()
        col_send[...] = col[...] + above[...]
        chain(col_send).start()

    load_p.wait()

    def face_x(src, dst, offset):
        for side, row in ((0, PAD + nx - 1), (1, PAD)):
            for z in range(nz):
                dst[side, pl.ds(offset + z, 1), :] = src[z + 1, pl.ds(row, 1), :]

    stride, part_rows = 2 * nz, nx // FOLD

    def face_y(srcs, dst, first_z=1, first_row=PAD):
        def pack(z, faces):
            faces = list(faces)
            for side in range(2):
                lanes = pl.ds(0 if side else ny - 128, 128)
                for i in range(FOLD):
                    rows = pl.ds(first_row + i * part_rows, part_rows)
                    for j, src in enumerate(srcs):
                        k = i * stride + j * nz + z
                        moved = pltpu.roll(src[z + first_z, rows, lanes], k if side else k + 1, 1)
                        faces[side] = jnp.where(lane_f == k, moved, faces[side])
            return tuple(faces)

        empty = jnp.zeros((part_rows, 128), jnp.float32)
        for side, face in enumerate(lax.fori_loop(0, nz, pack, (empty, empty))):
            dst[side] = face

    def unfold(value, dst, side):
        for i in range(FOLD):
            moved = pltpu.roll(value, 128 - i * stride, 1) if i else value
            dst[side, pl.ds(i * part_rows, part_rows), :] = moved

    face_x(pv, xs, 0)
    face_x(hv, xs, nz)
    start(X_1)
    face_y((pv, hv), ys)
    start(Y_1)

    def first(z, carry):
        for r in range(0, nx, ROWS):
            at = lambda ref, dz, dx: ref[z + 1 + dz, pl.ds(PAD + r + dx, ROWS), :]
            rows = pl.ds(r, ROWS)
            h, p = at(hv, 0, 0), at(pv, 0, 0)
            t_zm, t_zp = rec(h + at(hv, -1, 0)), rec(h + at(hv, 1, 0))
            t_xm, t_xp = rec(h + at(hv, 0, -1)), rec(h + at(hv, 0, 1))
            last = lax.broadcasted_iota(jnp.int32, h.shape, 1) == ny - 1
            t_yp = jnp.where(last, 0.0, rec(h + shifted(h, False)))
            t_ym = shifted(t_yp, True)
            tz[z + 1, rows, :] = t_zp
            tx[z, rows, :] = t_xm
            if r + ROWS == nx:
                tx[z, pl.ds(nx, 1), :] = t_xp[ROWS - 1:, :]
            ty[z, rows, :] = t_yp
            rd[z, rows, :] = 1.0 + ((t_zm + t_zp) + (t_xm + t_xp) + (t_ym + t_yp))
            part[z, rows, :] = (
                p + (t_zm * at(pv, -1, 0) + t_zp * at(pv, 1, 0))
                + (t_xm * at(pv, 0, -1) + t_xp * at(pv, 0, 1))
                + (shifted(t_yp * p, True) + t_yp * shifted(p, False)))
        return carry

    lax.fori_loop(0, nz // 2 + 1, lambda k, c: first(lax.rem(k + nz - 1, nz), c), 0)

    @pl.when(me["slab"] == 1)
    def _():
        forward()

    x_rows = ((0, 0), (1, nx - 1))
    arrived(X_1)
    for side, row in x_rows:
        link = rec(xs[1 - side, pl.ds(nz, nz), :] + xr[side, pl.ds(nz, nz), :])
        x_link[side] = link
        x_flow[side] = link * xr[side, pl.ds(0, nz), :]

    def add_x(z):
        for side, row in x_rows:
            one = pl.ds(row, 1)
            rd[z, one, :] += x_link[side, pl.ds(z, 1), :]
            part[z, one, :] += x_flow[side, pl.ds(z, 1), :]

    arrived(Y_1)
    for side in range(2):
        link = pltpu.roll(rec(ys[1 - side] + yr[side]), 128 - nz, 1)
        link_fold[side] = link
        unfold(link, y_link, side)
        unfold(link * yr[side], y_flow, side)

    def divide(z):
        for r in range(0, nx, 32):
            rows = pl.ds(r, 32)
            inv = rec(rd[z, rows, :] + at_edges(y_link, z, rows, ny))
            rd[z, rows, :] = STEP_RES * inv
            qv[z + 1, pl.ds(PAD + r, 32), :] = inv * (
                part[z, rows, :] + at_edges(y_flow, z, rows, ny))

    add_x(0)
    add_x(nz - 1)
    arrived(Z_H)
    arrived(Z_P)
    for side, z in ((0, 0), (1, nz - 1)):
        for r in range(0, nx, 32):
            rows = pl.ds(r, 32)
            link = rec(hv[z + 1, pl.ds(PAD + r, 32), :] + zhr[side, rows, :])
            z_link[side, rows, :] = link
            rd[z, rows, :] += link
            part[z, rows, :] += link * zpr[side, rows, :]
    lax.fori_loop(0, 2, lambda i, c: (divide(i * (nz - 1)), c)[1], 0)
    start(Z_Q)

    lax.fori_loop(nz // 2, nz - 1, first, 0)

    @pl.when(me["slab"] == 2)
    def _():
        forward()

    for z in range(1, nz - 1):
        add_x(z)
    lax.fori_loop(1, nz - 1, lambda z, c: (divide(z), c)[1], 0)
    face_x(qv, xqs, 0)
    start(X_Q)
    face_y((qv,), yqs)
    start(Y_Q)

    face_y((rd,), edge, 0, 0)
    for side in range(2):
        link_fold[side] = link_fold[side] * edge[1 - side]

    def second(z, carry):
        for r in range(0, nx, ROWS):
            at = lambda ref, dz, dx: ref[z + 1 + dz, pl.ds(PAD + r + dx, ROWS), :]
            rows = pl.ds(r, ROWS)
            p, q = at(pv, 0, 0), at(qv, 0, 0)
            t_yp = ty[z, rows, :]
            total = (p + (tz[z, rows, :] * at(qv, -1, 0) + tz[z + 1, rows, :] * at(qv, 1, 0))
                     + (tx[z, rows, :] * at(qv, 0, -1) + tx[z, pl.ds(r + 1, ROWS), :] * at(qv, 0, 1))
                     + (shifted(t_yp * q, True) + t_yp * shifted(q, False)))
            part[z, rows, :] = q + STEP_KEEP * (q - p) + (total * rd[z, rows, :] - STEP_RES * q)
        return carry

    lax.fori_loop(0, nz, second, 0)

    arrived(X_Q)
    for side, row in x_rows:
        flow = x_link[side] * xqr[side]
        for z in range(nz):
            one = pl.ds(row, 1)
            part[z, one, :] += rd[z, one, :] * flow[z:z + 1, :]
    arrived(Y_Q)
    for side in range(2):
        unfold(link_fold[side] * yqr[side], y_term, side)
    arrived(Z_Q)
    for side, z in ((0, 0), (1, nz - 1)):
        for r in range(0, nx, 32):
            rows = pl.ds(r, 32)
            part[z, rows, :] += rd[z, rows, :] * z_link[side, rows, :] * zqr[side, rows, :]
    for z in range(nz):
        solid_wide[z] = jnp.full((8, 128), solid[z], jnp.float32)

    @pl.when(me["slab"] == 3)
    def _():
        chain(col_send).wait_recv()

    for group in groups:
        sent(group)

    @pl.when(has_hi["slab"])
    def _():
        chain(col_send).wait_send()


def finish(part, ob, lit, above, y_term, solid_wide, pn_out, phi_out, thick_out, buf, store_sem):
    nz, nx, ny = lit.shape
    outs = (pn_out, phi_out, thick_out)

    def store(i, z):
        return pltpu.make_async_copy(buf.at[i, z], outs[i].at[z], store_sem.at[i, z])

    def layer(z, carry):
        solid = jnp.concatenate([solid_wide[z]] * (ny // 128), axis=1)
        solid = jnp.concatenate([solid] * (ROWS // 8), axis=0)
        for r in range(0, nx, ROWS):
            rows = pl.ds(r, ROWS)
            pn = part[z, rows, :] + at_edges(y_term, z, rows, ny)
            stress = jnp.maximum(above[rows, :] + ob[z, rows, :] - pn, 0.0)
            cls = classes(lit[z, rows, :])
            phi = pick(cls, PHI_SURFACE) * jnp.exp2(pick(cls, ATHY_NEG) * stress)
            buf[0, z, rows, :] = pn
            buf[1, z, rows, :] = phi
            buf[2, z, rows, :] = solid * rec(1.0 - phi)
        for i in range(3):
            store(i, z).start()
        return carry

    lax.fori_loop(0, nz, layer, 0)

    def stored(z, carry):
        for i in range(3):
            store(i, z).wait()
        return carry

    lax.fori_loop(0, nz, stored, 0)


def body(sizes, pressure, porosity, lithology, layer_solid):
    nz, nx, ny = pressure.shape
    f32, i32 = jnp.float32, jnp.int32
    shaped = jax.ShapeDtypeStruct
    block, plane = (nz, nx, ny), (nx, ny)
    padded = (nz + 2, nx + 2 * PAD, ny)
    folded = (2, nx // FOLD, 128)
    z_face, x_face, y_face = (2, nx, ny), (2, nz, ny), (2, nx, 128)
    vmem = pl.BlockSpec(memory_space=pltpu.VMEM)
    hbm = pl.BlockSpec(memory_space=pltpu.HBM)
    held = (shaped(block, f32), shaped(block, f32), shaped(block, i32), shaped(plane, f32),
            shaped(y_face, f32), shaped((nz, 8, 128), f32))
    held = pl.pallas_call(
        functools.partial(exchange, sizes),
        out_shape=held,
        in_specs=[hbm] * 4,
        out_specs=(vmem,) * len(held),
        scratch_shapes=[pltpu.VMEM(shape, f32) for shape in (
            padded, padded, padded, (nz + 1, nx, ny), (nz, nx + PAD, ny),
            block, block, block, plane, plane,
            (2, 2 * nz, ny), (2, 2 * nz, ny), folded, folded, z_face, z_face, z_face,
            x_face, x_face, folded, folded, z_face, x_face, x_face,
            y_face, y_face, folded, folded)] + [
            pltpu.SMEM((nz,), f32),
            pltpu.SemaphoreType.DMA((8,)),
            pltpu.SemaphoreType.DMA((MESSAGES,)),
            pltpu.SemaphoreType.DMA((MESSAGES,)),
        ],
        compiler_params=pltpu.CompilerParams(
            collective_id=0, has_side_effects=True, vmem_limit_bytes=24 * 2**20),
        name="exchange",
    )(*(pltpu.with_memory_space_constraint(a, pltpu.HBM) for a in (pressure, porosity, lithology, layer_solid)))
    return pl.pallas_call(
        finish,
        out_shape=(shaped(block, f32),) * 3,
        in_specs=[vmem] * len(held),
        out_specs=(hbm,) * 3,
        scratch_shapes=[
            pltpu.VMEM((3,) + block, f32),
            pltpu.SemaphoreType.DMA((3, nz)),
        ],
        compiler_params=pltpu.CompilerParams(vmem_limit_bytes=24 * 2**20),
        name="finish",
    )(*held)


def solution(mesh):
    sizes = dict(mesh.shape)
    spec = P("slab", "mapx", "mapy")
    return jax.shard_map(
        functools.partial(body, sizes), mesh=mesh,
        in_specs=(spec, spec, spec, P("slab")), out_specs=(spec, spec, spec), check_vma=False)
```

```python
import functools
import math

import jax
import jax.numpy as jnp
from jax import lax
from jax.experimental import pallas as pl
from jax.experimental.pallas import tpu as pltpu
from jax.sharding import PartitionSpec as P

PHI_SURFACE = (0.45, 0.55, 0.65, 0.4)
ATHY_RATE = (0.25, 0.45, 0.8, 0.35)
MOB_BASE = (1.0, 0.0, -1.5, -0.5)
MOB_SLOPE = (6.0, 5.0, 8.0, 4.0)
GRAIN_DENSITY = (2.65, 2.68, 2.72, 2.71)
WATER_DENSITY = 1.03
SPECTRUM_MID = 1.0
SPECTRUM_HALF = 0.95
SIGMA_RATIO = SPECTRUM_MID / SPECTRUM_HALF
RHO_FIRST = 1.0 / SIGMA_RATIO
RHO_SECOND = 1.0 / (2.0 * SIGMA_RATIO - RHO_FIRST)
STEP_KEEP = RHO_SECOND * RHO_FIRST
STEP_RES = 2.0 * RHO_SECOND / SPECTRUM_HALF

LOG2_E = 1.0 / math.log(2.0)

HALF_BASE = tuple(-(b - 0.35 * s) * LOG2_E - 1.0 for b, s in zip(MOB_BASE, MOB_SLOPE))
HALF_SLOPE = tuple(-s * LOG2_E for s in MOB_SLOPE)
GRAIN_LESS = tuple(g - WATER_DENSITY for g in GRAIN_DENSITY)
ATHY_NEG = tuple(-a * LOG2_E for a in ATHY_RATE)
OUTSIDE = 2.0e38

MESH = pl.DeviceIdType.MESH
PAD = 8
ROWS = 16
SPLIT = 4
X_1, Y_1, X_Q, Y_Q = 0, 2, 4, 6
Z_P, Z_H, Z_Q, CHAIN = 8, 8 + 2 * SPLIT, 8 + 4 * SPLIT, 8 + 6 * SPLIT
MESSAGES = CHAIN + SPLIT


def rec(x):
    return pl.reciprocal(x, approx=True)


def classes(lith):
    return lith >= 2, (lith & 1) == 1


def pick(cls, table):
    high, odd = cls
    a, b, c, d = (jnp.float32(t) for t in table)
    return jnp.where(high, jnp.where(odd, d, c), jnp.where(odd, b, a))


def shifted(value, up):
    rows, ny = value.shape
    lane = lax.broadcasted_iota(jnp.int32, (rows, 128), 1)
    parts = [pltpu.roll(value[:, y:y + 128], 1 if up else 127, 1) for y in range(0, ny, 128)]
    if up:
        joined = [jnp.where(lane == 0, a, b) for a, b in zip(parts[-1:] + parts[:-1], parts)]
    else:
        joined = [jnp.where(lane == 127, a, b) for a, b in zip(parts[1:] + parts[:1], parts)]
    return jnp.concatenate(joined, axis=1)


def at_edges(halo, index, rows, ny):
    lo = pltpu.roll(halo[0, rows, :], lax.rem(128 - index, 128), 1)
    hi = pltpu.roll(halo[1, rows, :], 127 - index, 1)
    lane = lax.broadcasted_iota(jnp.int32, lo.shape, 1)
    zeros = [jnp.zeros(lo.shape, jnp.float32)] * (ny // 128 - 2)
    ends = [jnp.where(lane == 0, lo, 0.0)] + zeros + [jnp.where(lane == 127, hi, 0.0)]
    return jnp.concatenate(ends, axis=1)


def exchange(sizes, p_hbm, por_hbm, lit_hbm, solid_hbm,
             part, ob, lit, above, y_term, solid_wide,
             pv, qv, hv, tz, tx, ty, rd, por, col, col_send, xs, xr, ys, yr,
             zpr, zhr, zqr, xqs, xqr, yqs, yqr, z_link, x_link, y_link, y_flow, edge,
             solid, load_sem, send_sem, recv_sem):
    nz, nx, ny = por.shape
    axes = ("slab", "mapx", "mapy")
    me = {a: lax.axis_index(a) for a in axes}
    has_lo = {a: me[a] > 0 for a in axes}
    has_hi = {a: me[a] < sizes[a] - 1 for a in axes}
    peers = sum(jnp.where(f, 1, 0) for flags in (has_lo, has_hi) for f in flags.values())
    inner = pl.ds(PAD, nx)

    loads = [
        pltpu.make_async_copy(por_hbm, por, load_sem.at[0]),
        pltpu.make_async_copy(lit_hbm, lit, load_sem.at[1]),
        pltpu.make_async_copy(p_hbm, pv.at[pl.ds(1, nz), inner, :], load_sem.at[2]),
        pltpu.make_async_copy(solid_hbm, solid, load_sem.at[3]),
    ]
    for c in loads:
        c.start()

    barrier = pltpu.get_barrier_semaphore()
    for a in axes:
        @pl.when(has_lo[a])
        def _():
            pl.semaphore_signal(barrier, inc=1, device_id={a: me[a] - 1}, device_id_type=MESH)

        @pl.when(has_hi[a])
        def _():
            pl.semaphore_signal(barrier, inc=1, device_id={a: me[a] + 1}, device_id_type=MESH)

    def message(k, axis, up, src, dst):
        target = me[axis] + 1 if up else me[axis] - 1
        return pltpu.make_async_remote_copy(
            src_ref=src, dst_ref=dst, send_sem=send_sem.at[k], recv_sem=recv_sem.at[k],
            device_id={axis: target}, device_id_type=MESH)

    def pair(k, axis, src_up, dst_up, src_down, dst_down):
        return [(k, axis, True, src_up, dst_up), (k + 1, axis, False, src_down, dst_down)]

    cuts = [pl.ds(i * (nx // SPLIT), nx // SPLIT) for i in range(SPLIT)]

    def layers(k, layer, dst):
        copies = []
        for i, rows in enumerate(cuts):
            copies += pair(k + 2 * i, "slab", layer(nz, rows), dst.at[0, rows, :],
                           layer(1, rows), dst.at[1, rows, :])
        return copies

    def padded_layer(ref):
        return lambda z, rows: ref.at[z, pl.ds(PAD + rows.start, rows.size), :]

    z_lo, z_hi = 0, nz + 1
    groups = {
        Z_P: layers(Z_P, lambda z, rows: p_hbm.at[z - 1, rows, :], zpr),
        Z_H: layers(Z_H, padded_layer(hv), zhr),
        X_1: pair(X_1, "mapx", xs.at[0], xr.at[0], xs.at[1], xr.at[1]),
        Y_1: pair(Y_1, "mapy", ys.at[0], yr.at[0], ys.at[1], yr.at[1]),
        Z_Q: layers(Z_Q, padded_layer(qv), zqr),
        X_Q: pair(X_Q, "mapx", xqs.at[0], xqr.at[0], xqs.at[1], xqr.at[1]),
        Y_Q: pair(Y_Q, "mapy", yqs.at[0], yqr.at[0], yqs.at[1], yqr.at[1]),
    }

    def start(group):
        for k, axis, up, src, dst in groups[group]:
            @pl.when(has_hi[axis] if up else has_lo[axis])
            def _():
                message(k, axis, up, src, dst).start()

    def arrived(group):
        for k, axis, up, src, dst in groups[group]:
            @pl.when(has_lo[axis] if up else has_hi[axis])
            def _():
                message(k, axis, up, src, dst).wait_recv()

    def sent(group):
        for k, axis, up, src, dst in groups[group]:
            @pl.when(has_hi[axis] if up else has_lo[axis])
            def _():
                message(k, axis, up, src, dst).wait_send()

    lane_y = lax.broadcasted_iota(jnp.int32, (nx, 128), 1)

    for layer in (z_lo, z_hi):
        pv[layer, inner, :] = jnp.zeros((nx, ny), jnp.float32)
        qv[layer, inner, :] = jnp.zeros((nx, ny), jnp.float32)
        hv[layer, inner, :] = jnp.full((nx, ny), OUTSIDE, jnp.float32)
    tz[0] = jnp.zeros((nx, ny), jnp.float32)
    for z in range(nz):
        for row in (PAD - 1, PAD + nx):
            pv[z + 1, pl.ds(row, 1), :] = jnp.zeros((1, ny), jnp.float32)
            qv[z + 1, pl.ds(row, 1), :] = jnp.zeros((1, ny), jnp.float32)
            hv[z + 1, pl.ds(row, 1), :] = jnp.full((1, ny), OUTSIDE, jnp.float32)

    for side, flags in ((0, has_lo), (1, has_hi)):
        @pl.when(jnp.logical_not(flags["slab"]))
        def _():
            zpr[side] = jnp.zeros((nx, ny), jnp.float32)
            zqr[side] = jnp.zeros((nx, ny), jnp.float32)
            zhr[side] = jnp.full((nx, ny), OUTSIDE, jnp.float32)
            if side == 0:
                above[...] = jnp.zeros((nx, ny), jnp.float32)

        @pl.when(jnp.logical_not(flags["mapx"]))
        def _():
            xr[side, pl.ds(0, nz), :] = jnp.zeros((nz, ny), jnp.float32)
            xr[side, pl.ds(nz, nz), :] = jnp.full((nz, ny), OUTSIDE, jnp.float32)
            xqr[side] = jnp.zeros((nz, ny), jnp.float32)

        @pl.when(jnp.logical_not(flags["mapy"]))
        def _():
            yr[side] = jnp.where(lane_y < nz, jnp.float32(0.0), jnp.float32(OUTSIDE))
            yqr[side] = jnp.zeros((nx, 128), jnp.float32)

    loads[0].wait()
    loads[1].wait()

    def half_inverse(z):
        for r in range(0, nx, 32):
            rows = pl.ds(r, 32)
            cls = classes(lit[z, rows, :])
            hv[z + 1, pl.ds(PAD + r, 32), :] = jnp.exp2(
                pick(cls, HALF_BASE) + pick(cls, HALF_SLOPE) * por[z, rows, :])

    lax.fori_loop(0, nz, lambda z, c: (half_inverse(z), c)[1], 0)
    loads[2].wait()

    def face_x(src, dst, offset):
        for side, row in ((0, PAD + nx - 1), (1, PAD)):
            for z in range(nz):
                dst[side, pl.ds(offset + z, 1), :] = src[z + 1, pl.ds(row, 1), :]

    def face_y(srcs, dst, first_z=1, first_row=PAD):
        for side in range(2):
            for r in range(0, nx, 32):
                acc = jnp.zeros((32, 128), jnp.float32)
                lane = lane_y[:32]
                for i, src in enumerate(srcs):
                    for z in range(nz):
                        k = i * nz + z
                        lanes = pl.ds(0 if side else ny - 128, 128)
                        column = src[z + first_z, pl.ds(first_row + r, 32), lanes]
                        shift = k if side else k + 1
                        moved = pltpu.roll(column, shift, 1) if shift else column
                        acc = jnp.where(lane == k, moved, acc)
                dst[side, pl.ds(r, 32), :] = acc

    face_x(pv, xs, 0)
    face_x(hv, xs, nz)
    face_y((pv, hv), ys)
    pl.semaphore_wait(barrier, peers)
    for group in (X_1, Y_1, Z_H, Z_P):
        start(group)

    loads[3].wait()
    for r in range(0, nx, 32):
        rows = pl.ds(r, 32)

        def add_layer(z, total):
            cls = classes(lit[z, rows, :])
            load = (pick(cls, GRAIN_LESS) + WATER_DENSITY * rec(1.0 - por[z, rows, :])) * solid[z]
            ob[z, rows, :] = total + 0.5 * load
            return total + load

        col[rows, :] = lax.fori_loop(0, nz, add_layer, jnp.zeros((32, ny), jnp.float32))

    def chain():
        return [message(CHAIN + i, "slab", True, col_send.at[rows, :], above.at[rows, :])
                for i, rows in enumerate(cuts)]

    @pl.when(me["slab"] == 0)
    def _():
        col_send[...] = col[...]
        for copy in chain():
            copy.start()

    def forward():
        for copy in chain():
            copy.wait_recv()
        col_send[...] = col[...] + above[...]
        for copy in chain():
            copy.start()

    def first(z, carry):
        for r in range(0, nx, ROWS):
            at = lambda ref, dz, dx: ref[z + 1 + dz, pl.ds(PAD + r + dx, ROWS), :]
            rows = pl.ds(r, ROWS)
            h, p = at(hv, 0, 0), at(pv, 0, 0)
            t_zm, t_zp = tz[z, rows, :], rec(h + at(hv, 1, 0))
            t_xm, t_xp = rec(h + at(hv, 0, -1)), rec(h + at(hv, 0, 1))
            last = lax.broadcasted_iota(jnp.int32, h.shape, 1) == ny - 1
            t_yp = jnp.where(last, 0.0, rec(h + shifted(h, False)))
            t_ym = shifted(t_yp, True)
            tz[z + 1, rows, :] = t_zp
            tx[z, rows, :] = t_xm
            if r + ROWS == nx:
                tx[z, pl.ds(nx, 1), :] = t_xp[ROWS - 1:, :]
            ty[z, rows, :] = t_yp
            rd[z, rows, :] = 1.0 + ((t_zm + t_zp) + (t_xm + t_xp) + (t_ym + t_yp))
            part[z, rows, :] = (
                p + (t_zm * at(pv, -1, 0) + t_zp * at(pv, 1, 0))
                + (t_xm * at(pv, 0, -1) + t_xp * at(pv, 0, 1))
                + (shifted(t_yp * p, True) + t_yp * shifted(p, False)))
        return carry

    lax.fori_loop(0, nz // 2, first, 0)

    @pl.when(me["slab"] == 1)
    def _():
        forward()

    lax.fori_loop(nz // 2, nz, first, 0)

    x_rows = ((0, 0), (1, nx - 1))
    arrived(X_1)
    for side, row in x_rows:
        link = rec(xs[1 - side, pl.ds(nz, nz), :] + xr[side, pl.ds(nz, nz), :])
        x_link[side] = link
        flow = link * xr[side, pl.ds(0, nz), :]
        for z in range(nz):
            one = pl.ds(row, 1)
            rd[z, one, :] += link[z:z + 1, :]
            part[z, one, :] += flow[z:z + 1, :]
    arrived(Y_1)
    for side in range(2):
        link = pltpu.roll(rec(ys[1 - side] + yr[side]), 128 - nz, 1)
        link = jnp.where(lane_y < nz, link, 0.0)
        y_link[side] = link
        y_flow[side] = link * yr[side]
    arrived(Z_H)
    arrived(Z_P)
    for side, z in ((0, 0), (1, nz - 1)):
        for r in range(0, nx, 32):
            rows = pl.ds(r, 32)
            link = rec(hv[z + 1, pl.ds(PAD + r, 32), :] + zhr[side, rows, :])
            z_link[side, rows, :] = link
            rd[z, rows, :] += link
            part[z, rows, :] += link * zpr[side, rows, :]

    def divide(z):
        for r in range(0, nx, 32):
            rows = pl.ds(r, 32)
            inv = rec(rd[z, rows, :] + at_edges(y_link, z, rows, ny))
            rd[z, rows, :] = STEP_RES * inv
            qv[z + 1, pl.ds(PAD + r, 32), :] = inv * (
                part[z, rows, :] + at_edges(y_flow, z, rows, ny))

    divide(0)
    divide(nz - 1)
    start(Z_Q)
    lax.fori_loop(1, nz - 1, lambda z, c: (divide(z), c)[1], 0)
    face_x(qv, xqs, 0)
    start(X_Q)
    face_y((qv,), yqs)
    start(Y_Q)

    face_y((rd,), edge, 0, 0)
    for side in range(2):
        y_link[side] = y_link[side] * edge[1 - side]

    @pl.when(me["slab"] == 2)
    def _():
        forward()

    def second(z, carry):
        for r in range(0, nx, ROWS):
            at = lambda ref, dz, dx: ref[z + 1 + dz, pl.ds(PAD + r + dx, ROWS), :]
            rows = pl.ds(r, ROWS)
            p, q = at(pv, 0, 0), at(qv, 0, 0)
            t_yp = ty[z, rows, :]
            total = (p + (tz[z, rows, :] * at(qv, -1, 0) + tz[z + 1, rows, :] * at(qv, 1, 0))
                     + (tx[z, rows, :] * at(qv, 0, -1) + tx[z, pl.ds(r + 1, ROWS), :] * at(qv, 0, 1))
                     + (shifted(t_yp * q, True) + t_yp * shifted(q, False)))
            part[z, rows, :] = q + STEP_KEEP * (q - p) + (total * rd[z, rows, :] - STEP_RES * q)
        return carry

    lax.fori_loop(0, nz, second, 0)

    arrived(X_Q)
    for side, row in x_rows:
        flow = x_link[side] * xqr[side]
        for z in range(nz):
            one = pl.ds(row, 1)
            part[z, one, :] += rd[z, one, :] * flow[z:z + 1, :]
    arrived(Y_Q)
    for side in range(2):
        y_term[side] = y_link[side] * yqr[side]
    arrived(Z_Q)
    for side, z in ((0, 0), (1, nz - 1)):
        for r in range(0, nx, 32):
            rows = pl.ds(r, 32)
            part[z, rows, :] += rd[z, rows, :] * z_link[side, rows, :] * zqr[side, rows, :]
    for z in range(nz):
        solid_wide[z] = jnp.full((8, 128), solid[z], jnp.float32)

    @pl.when(me["slab"] == 3)
    def _():
        for copy in chain():
            copy.wait_recv()

    for group in groups:
        sent(group)

    @pl.when(has_hi["slab"])
    def _():
        for copy in chain():
            copy.wait_send()


def finish(part, ob, lit, above, y_term, solid_wide, pn_out, phi_out, thick_out, buf, store_sem):
    nz, nx, ny = lit.shape
    outs = (pn_out, phi_out, thick_out)

    def store(i, z):
        return pltpu.make_async_copy(buf.at[i, z], outs[i].at[z], store_sem.at[i, z])

    def layer(z, carry):
        solid = jnp.concatenate([solid_wide[z]] * (ny // 128), axis=1)
        solid = jnp.concatenate([solid] * (ROWS // 8), axis=0)
        for r in range(0, nx, ROWS):
            rows = pl.ds(r, ROWS)
            pn = part[z, rows, :] + at_edges(y_term, z, rows, ny)
            stress = jnp.maximum(above[rows, :] + ob[z, rows, :] - pn, 0.0)
            cls = classes(lit[z, rows, :])
            phi = pick(cls, PHI_SURFACE) * jnp.exp2(pick(cls, ATHY_NEG) * stress)
            buf[0, z, rows, :] = pn
            buf[1, z, rows, :] = phi
            buf[2, z, rows, :] = solid * rec(1.0 - phi)
        for i in range(3):
            store(i, z).start()
        return carry

    lax.fori_loop(0, nz, layer, 0)

    def stored(z, carry):
        for i in range(3):
            store(i, z).wait()
        return carry

    lax.fori_loop(0, nz, stored, 0)


def body(sizes, pressure, porosity, lithology, layer_solid):
    nz, nx, ny = pressure.shape
    f32, i32 = jnp.float32, jnp.int32
    shaped = jax.ShapeDtypeStruct
    block, plane = (nz, nx, ny), (nx, ny)
    padded = (nz + 2, nx + 2 * PAD, ny)
    z_face, x_face, y_face = (2, nx, ny), (2, nz, ny), (2, nx, 128)
    vmem = pl.BlockSpec(memory_space=pltpu.VMEM)
    hbm = pl.BlockSpec(memory_space=pltpu.HBM)
    held = (shaped(block, f32), shaped(block, f32), shaped(block, i32), shaped(plane, f32),
            shaped(y_face, f32), shaped((nz, 8, 128), f32))
    held = pl.pallas_call(
        functools.partial(exchange, sizes),
        out_shape=held,
        in_specs=[hbm] * 4,
        out_specs=(vmem,) * len(held),
        scratch_shapes=[pltpu.VMEM(shape, f32) for shape in (
            padded, padded, padded, (nz + 1, nx, ny), (nz, nx + PAD, ny),
            block, block, block, plane, plane,
            (2, 2 * nz, ny), (2, 2 * nz, ny), y_face, y_face, z_face, z_face, z_face,
            x_face, x_face, y_face, y_face, z_face, x_face, y_face, y_face, y_face)] + [
            pltpu.SMEM((nz,), f32),
            pltpu.SemaphoreType.DMA((4,)),
            pltpu.SemaphoreType.DMA((MESSAGES,)),
            pltpu.SemaphoreType.DMA((MESSAGES,)),
        ],
        compiler_params=pltpu.CompilerParams(
            collective_id=0, has_side_effects=True, vmem_limit_bytes=24 * 2**20),
        name="exchange",
    )(*(pltpu.with_memory_space_constraint(a, pltpu.HBM) for a in (pressure, porosity, lithology, layer_solid)))
    return pl.pallas_call(
        finish,
        out_shape=(shaped(block, f32),) * 3,
        in_specs=[vmem] * len(held),
        out_specs=(hbm,) * 3,
        scratch_shapes=[
            pltpu.VMEM((3,) + block, f32),
            pltpu.SemaphoreType.DMA((3, nz)),
        ],
        compiler_params=pltpu.CompilerParams(vmem_limit_bytes=24 * 2**20),
        name="finish",
    )(*held)


def solution(mesh):
    sizes = dict(mesh.shape)
    spec = P("slab", "mapx", "mapy")
    return jax.shard_map(
        functools.partial(body, sizes), mesh=mesh,
        in_specs=(spec, spec, spec, P("slab")), out_specs=(spec, spec, spec), check_vma=False)
```

```python
import functools
import math

import jax
import jax.numpy as jnp
from jax import lax
from jax.experimental import pallas as pl
from jax.experimental.pallas import tpu as pltpu
from jax.sharding import PartitionSpec as P

PHI_SURFACE = (0.45, 0.55, 0.65, 0.4)
ATHY_RATE = (0.25, 0.45, 0.8, 0.35)
MOB_BASE = (1.0, 0.0, -1.5, -0.5)
MOB_SLOPE = (6.0, 5.0, 8.0, 4.0)
GRAIN_DENSITY = (2.65, 2.68, 2.72, 2.71)
WATER_DENSITY = 1.03
SPECTRUM_MID = 1.0
SPECTRUM_HALF = 0.95
SIGMA_RATIO = SPECTRUM_MID / SPECTRUM_HALF
RHO_FIRST = 1.0 / SIGMA_RATIO
RHO_SECOND = 1.0 / (2.0 * SIGMA_RATIO - RHO_FIRST)
STEP_KEEP = RHO_SECOND * RHO_FIRST
STEP_RES = 2.0 * RHO_SECOND / SPECTRUM_HALF

LOG2_E = 1.0 / math.log(2.0)

HALF_BASE = tuple(-(b - 0.35 * s) * LOG2_E - 1.0 for b, s in zip(MOB_BASE, MOB_SLOPE))
HALF_SLOPE = tuple(-s * LOG2_E for s in MOB_SLOPE)
GRAIN_LESS = tuple(g - WATER_DENSITY for g in GRAIN_DENSITY)
ATHY_NEG = tuple(-a * LOG2_E for a in ATHY_RATE)
OUTSIDE = 2.0e38

MESH = pl.DeviceIdType.MESH
PAD = 8
ROWS = 16
Z_P, Z_H, X_1, Y_1, Z_Q, X_Q, Y_Q, CHAIN = 0, 2, 4, 6, 8, 10, 12, 14
MESSAGES = 15


def rec(x):
    return pl.reciprocal(x, approx=True)


def classes(lith):
    return lith >= 2, (lith & 1) == 1


def pick(cls, table):
    high, odd = cls
    a, b, c, d = (jnp.float32(t) for t in table)
    return jnp.where(high, jnp.where(odd, d, c), jnp.where(odd, b, a))


def shifted(value, up):
    rows, ny = value.shape
    lane = lax.broadcasted_iota(jnp.int32, (rows, 128), 1)
    parts = [pltpu.roll(value[:, y:y + 128], 1 if up else 127, 1) for y in range(0, ny, 128)]
    if up:
        joined = [jnp.where(lane == 0, a, b) for a, b in zip(parts[-1:] + parts[:-1], parts)]
    else:
        joined = [jnp.where(lane == 127, a, b) for a, b in zip(parts[1:] + parts[:1], parts)]
    return jnp.concatenate(joined, axis=1)


def at_edges(halo, index, rows, ny):
    lo = pltpu.roll(halo[0, rows, :], lax.rem(128 - index, 128), 1)
    hi = pltpu.roll(halo[1, rows, :], 127 - index, 1)
    lane = lax.broadcasted_iota(jnp.int32, lo.shape, 1)
    zeros = [jnp.zeros(lo.shape, jnp.float32)] * (ny // 128 - 2)
    ends = [jnp.where(lane == 0, lo, 0.0)] + zeros + [jnp.where(lane == 127, hi, 0.0)]
    return jnp.concatenate(ends, axis=1)


def exchange(sizes, p_hbm, por_hbm, lit_hbm, solid_hbm,
             part, ob, lit, above, y_term, solid_wide,
             pv, qv, hv, tz, tx, ty, rd, por, col, col_send, xs, xr, ys, yr,
             zpr, zhr, zqr, xqs, xqr, yqs, yqr, z_link, x_link, y_link, y_flow, edge,
             solid, load_sem, send_sem, recv_sem):
    nz, nx, ny = por.shape
    axes = ("slab", "mapx", "mapy")
    me = {a: lax.axis_index(a) for a in axes}
    has_lo = {a: me[a] > 0 for a in axes}
    has_hi = {a: me[a] < sizes[a] - 1 for a in axes}
    peers = sum(jnp.where(f, 1, 0) for flags in (has_lo, has_hi) for f in flags.values())
    inner = pl.ds(PAD, nx)

    loads = [
        pltpu.make_async_copy(por_hbm, por, load_sem.at[0]),
        pltpu.make_async_copy(lit_hbm, lit, load_sem.at[1]),
        pltpu.make_async_copy(p_hbm, pv.at[pl.ds(1, nz), inner, :], load_sem.at[2]),
        pltpu.make_async_copy(solid_hbm, solid, load_sem.at[3]),
    ]
    for c in loads:
        c.start()

    barrier = pltpu.get_barrier_semaphore()
    for a in axes:
        @pl.when(has_lo[a])
        def _():
            pl.semaphore_signal(barrier, inc=1, device_id={a: me[a] - 1}, device_id_type=MESH)

        @pl.when(has_hi[a])
        def _():
            pl.semaphore_signal(barrier, inc=1, device_id={a: me[a] + 1}, device_id_type=MESH)

    def message(k, axis, up, src, dst):
        target = me[axis] + 1 if up else me[axis] - 1
        return pltpu.make_async_remote_copy(
            src_ref=src, dst_ref=dst, send_sem=send_sem.at[k], recv_sem=recv_sem.at[k],
            device_id={axis: target}, device_id_type=MESH)

    def pair(k, axis, src_up, dst_up, src_down, dst_down):
        return [(k, axis, True, src_up, dst_up), (k + 1, axis, False, src_down, dst_down)]

    z_lo, z_hi = 0, nz + 1
    groups = {
        Z_P: pair(Z_P, "slab", p_hbm.at[nz - 1], zpr.at[0], p_hbm.at[0], zpr.at[1]),
        Z_H: pair(Z_H, "slab", hv.at[nz, inner, :], zhr.at[0], hv.at[1, inner, :], zhr.at[1]),
        X_1: pair(X_1, "mapx", xs.at[0], xr.at[0], xs.at[1], xr.at[1]),
        Y_1: pair(Y_1, "mapy", ys.at[0], yr.at[0], ys.at[1], yr.at[1]),
        Z_Q: pair(Z_Q, "slab", qv.at[nz, inner, :], zqr.at[0], qv.at[1, inner, :], zqr.at[1]),
        X_Q: pair(X_Q, "mapx", xqs.at[0], xqr.at[0], xqs.at[1], xqr.at[1]),
        Y_Q: pair(Y_Q, "mapy", yqs.at[0], yqr.at[0], yqs.at[1], yqr.at[1]),
    }

    def start(group):
        for k, axis, up, src, dst in groups[group]:
            @pl.when(has_hi[axis] if up else has_lo[axis])
            def _():
                message(k, axis, up, src, dst).start()

    def arrived(group):
        for k, axis, up, src, dst in groups[group]:
            @pl.when(has_lo[axis] if up else has_hi[axis])
            def _():
                message(k, axis, up, src, dst).wait_recv()

    def sent(group):
        for k, axis, up, src, dst in groups[group]:
            @pl.when(has_hi[axis] if up else has_lo[axis])
            def _():
                message(k, axis, up, src, dst).wait_send()

    lane_y = lax.broadcasted_iota(jnp.int32, (nx, 128), 1)

    for layer in (z_lo, z_hi):
        pv[layer, inner, :] = jnp.zeros((nx, ny), jnp.float32)
        qv[layer, inner, :] = jnp.zeros((nx, ny), jnp.float32)
        hv[layer, inner, :] = jnp.full((nx, ny), OUTSIDE, jnp.float32)
    tz[0] = jnp.zeros((nx, ny), jnp.float32)
    for z in range(nz):
        for row in (PAD - 1, PAD + nx):
            pv[z + 1, pl.ds(row, 1), :] = jnp.zeros((1, ny), jnp.float32)
            qv[z + 1, pl.ds(row, 1), :] = jnp.zeros((1, ny), jnp.float32)
            hv[z + 1, pl.ds(row, 1), :] = jnp.full((1, ny), OUTSIDE, jnp.float32)

    for side, flags in ((0, has_lo), (1, has_hi)):
        @pl.when(jnp.logical_not(flags["slab"]))
        def _():
            zpr[side] = jnp.zeros((nx, ny), jnp.float32)
            zqr[side] = jnp.zeros((nx, ny), jnp.float32)
            zhr[side] = jnp.full((nx, ny), OUTSIDE, jnp.float32)
            if side == 0:
                above[...] = jnp.zeros((nx, ny), jnp.float32)

        @pl.when(jnp.logical_not(flags["mapx"]))
        def _():
            xr[side, pl.ds(0, nz), :] = jnp.zeros((nz, ny), jnp.float32)
            xr[side, pl.ds(nz, nz), :] = jnp.full((nz, ny), OUTSIDE, jnp.float32)
            xqr[side] = jnp.zeros((nz, ny), jnp.float32)

        @pl.when(jnp.logical_not(flags["mapy"]))
        def _():
            yr[side] = jnp.where(lane_y < nz, jnp.float32(0.0), jnp.float32(OUTSIDE))
            yqr[side] = jnp.zeros((nx, 128), jnp.float32)

    loads[0].wait()
    loads[1].wait()

    def half_inverse(z):
        for r in range(0, nx, 32):
            rows = pl.ds(r, 32)
            cls = classes(lit[z, rows, :])
            hv[z + 1, pl.ds(PAD + r, 32), :] = jnp.exp2(
                pick(cls, HALF_BASE) + pick(cls, HALF_SLOPE) * por[z, rows, :])

    lax.fori_loop(0, nz, lambda z, c: (half_inverse(z), c)[1], 0)
    pl.semaphore_wait(barrier, peers)
    start(Z_H)
    start(Z_P)
    loads[2].wait()

    def face_x(src, dst, offset):
        for side, row in ((0, PAD + nx - 1), (1, PAD)):
            for z in range(nz):
                dst[side, pl.ds(offset + z, 1), :] = src[z + 1, pl.ds(row, 1), :]

    def face_y(srcs, dst, first_z=1, first_row=PAD):
        for side in range(2):
            for r in range(0, nx, 32):
                acc = jnp.zeros((32, 128), jnp.float32)
                lane = lane_y[:32]
                for i, src in enumerate(srcs):
                    for z in range(nz):
                        k = i * nz + z
                        lanes = pl.ds(0 if side else ny - 128, 128)
                        column = src[z + first_z, pl.ds(first_row + r, 32), lanes]
                        shift = k if side else k + 1
                        moved = pltpu.roll(column, shift, 1) if shift else column
                        acc = jnp.where(lane == k, moved, acc)
                dst[side, pl.ds(r, 32), :] = acc

    face_x(pv, xs, 0)
    face_x(hv, xs, nz)
    face_y((pv, hv), ys)
    start(X_1)
    start(Y_1)

    loads[3].wait()
    for r in range(0, nx, 32):
        rows = pl.ds(r, 32)

        def add_layer(z, total):
            cls = classes(lit[z, rows, :])
            load = (pick(cls, GRAIN_LESS) + WATER_DENSITY * rec(1.0 - por[z, rows, :])) * solid[z]
            ob[z, rows, :] = total + 0.5 * load
            return total + load

        col[rows, :] = lax.fori_loop(0, nz, add_layer, jnp.zeros((32, ny), jnp.float32))

    def chain(src):
        return message(CHAIN, "slab", True, src, above)

    @pl.when(me["slab"] == 0)
    def _():
        col_send[...] = col[...]
        chain(col_send).start()

    def forward():
        chain(col_send).wait_recv()
        col_send[...] = col[...] + above[...]
        chain(col_send).start()

    def first(z, carry):
        for r in range(0, nx, ROWS):
            at = lambda ref, dz, dx: ref[z + 1 + dz, pl.ds(PAD + r + dx, ROWS), :]
            rows = pl.ds(r, ROWS)
            h, p = at(hv, 0, 0), at(pv, 0, 0)
            t_zm, t_zp = tz[z, rows, :], rec(h + at(hv, 1, 0))
            t_xm, t_xp = rec(h + at(hv, 0, -1)), rec(h + at(hv, 0, 1))
            last = lax.broadcasted_iota(jnp.int32, h.shape, 1) == ny - 1
            t_yp = jnp.where(last, 0.0, rec(h + shifted(h, False)))
            t_ym = shifted(t_yp, True)
            tz[z + 1, rows, :] = t_zp
            tx[z, rows, :] = t_xm
            if r + ROWS == nx:
                tx[z, pl.ds(nx, 1), :] = t_xp[ROWS - 1:, :]
            ty[z, rows, :] = t_yp
            rd[z, rows, :] = 1.0 + ((t_zm + t_zp) + (t_xm + t_xp) + (t_ym + t_yp))
            part[z, rows, :] = (
                p + (t_zm * at(pv, -1, 0) + t_zp * at(pv, 1, 0))
                + (t_xm * at(pv, 0, -1) + t_xp * at(pv, 0, 1))
                + (shifted(t_yp * p, True) + t_yp * shifted(p, False)))
        return carry

    lax.fori_loop(0, nz // 2, first, 0)

    @pl.when(me["slab"] == 1)
    def _():
        forward()

    lax.fori_loop(nz // 2, nz, first, 0)

    x_rows = ((0, 0), (1, nx - 1))
    arrived(X_1)
    for side, row in x_rows:
        link = rec(xs[1 - side, pl.ds(nz, nz), :] + xr[side, pl.ds(nz, nz), :])
        x_link[side] = link
        flow = link * xr[side, pl.ds(0, nz), :]
        for z in range(nz):
            one = pl.ds(row, 1)
            rd[z, one, :] += link[z:z + 1, :]
            part[z, one, :] += flow[z:z + 1, :]
    arrived(Y_1)
    for side in range(2):
        link = pltpu.roll(rec(ys[1 - side] + yr[side]), 128 - nz, 1)
        link = jnp.where(lane_y < nz, link, 0.0)
        y_link[side] = link
        y_flow[side] = link * yr[side]
    arrived(Z_H)
    arrived(Z_P)
    for side, z in ((0, 0), (1, nz - 1)):
        for r in range(0, nx, 32):
            rows = pl.ds(r, 32)
            link = rec(hv[z + 1, pl.ds(PAD + r, 32), :] + zhr[side, rows, :])
            z_link[side, rows, :] = link
            rd[z, rows, :] += link
            part[z, rows, :] += link * zpr[side, rows, :]

    def divide(z):
        for r in range(0, nx, 32):
            rows = pl.ds(r, 32)
            inv = rec(rd[z, rows, :] + at_edges(y_link, z, rows, ny))
            rd[z, rows, :] = STEP_RES * inv
            qv[z + 1, pl.ds(PAD + r, 32), :] = inv * (
                part[z, rows, :] + at_edges(y_flow, z, rows, ny))

    divide(0)
    divide(nz - 1)
    start(Z_Q)
    lax.fori_loop(1, nz - 1, lambda z, c: (divide(z), c)[1], 0)
    face_x(qv, xqs, 0)
    start(X_Q)
    face_y((qv,), yqs)
    start(Y_Q)

    face_y((rd,), edge, 0, 0)
    for side in range(2):
        y_link[side] = y_link[side] * edge[1 - side]

    @pl.when(me["slab"] == 2)
    def _():
        forward()

    def second(z, carry):
        for r in range(0, nx, ROWS):
            at = lambda ref, dz, dx: ref[z + 1 + dz, pl.ds(PAD + r + dx, ROWS), :]
            rows = pl.ds(r, ROWS)
            p, q = at(pv, 0, 0), at(qv, 0, 0)
            t_yp = ty[z, rows, :]
            total = (p + (tz[z, rows, :] * at(qv, -1, 0) + tz[z + 1, rows, :] * at(qv, 1, 0))
                     + (tx[z, rows, :] * at(qv, 0, -1) + tx[z, pl.ds(r + 1, ROWS), :] * at(qv, 0, 1))
                     + (shifted(t_yp * q, True) + t_yp * shifted(q, False)))
            part[z, rows, :] = q + STEP_KEEP * (q - p) + (total * rd[z, rows, :] - STEP_RES * q)
        return carry

    lax.fori_loop(0, nz, second, 0)

    arrived(X_Q)
    for side, row in x_rows:
        flow = x_link[side] * xqr[side]
        for z in range(nz):
            one = pl.ds(row, 1)
            part[z, one, :] += rd[z, one, :] * flow[z:z + 1, :]
    arrived(Y_Q)
    for side in range(2):
        y_term[side] = y_link[side] * yqr[side]
    arrived(Z_Q)
    for side, z in ((0, 0), (1, nz - 1)):
        for r in range(0, nx, 32):
            rows = pl.ds(r, 32)
            part[z, rows, :] += rd[z, rows, :] * z_link[side, rows, :] * zqr[side, rows, :]
    for z in range(nz):
        solid_wide[z] = jnp.full((8, 128), solid[z], jnp.float32)

    @pl.when(me["slab"] == 3)
    def _():
        chain(col_send).wait_recv()

    for group in groups:
        sent(group)

    @pl.when(has_hi["slab"])
    def _():
        chain(col_send).wait_send()


def finish(part, ob, lit, above, y_term, solid_wide, pn_out, phi_out, thick_out, buf, store_sem):
    nz, nx, ny = lit.shape
    outs = (pn_out, phi_out, thick_out)

    def store(i, z):
        return pltpu.make_async_copy(buf.at[i, z], outs[i].at[z], store_sem.at[i, z])

    def layer(z, carry):
        solid = jnp.concatenate([solid_wide[z]] * (ny // 128), axis=1)
        solid = jnp.concatenate([solid] * (ROWS // 8), axis=0)
        for r in range(0, nx, ROWS):
            rows = pl.ds(r, ROWS)
            pn = part[z, rows, :] + at_edges(y_term, z, rows, ny)
            stress = jnp.maximum(above[rows, :] + ob[z, rows, :] - pn, 0.0)
            cls = classes(lit[z, rows, :])
            phi = pick(cls, PHI_SURFACE) * jnp.exp2(pick(cls, ATHY_NEG) * stress)
            buf[0, z, rows, :] = pn
            buf[1, z, rows, :] = phi
            buf[2, z, rows, :] = solid * rec(1.0 - phi)
        for i in range(3):
            store(i, z).start()
        return carry

    lax.fori_loop(0, nz, layer, 0)

    def stored(z, carry):
        for i in range(3):
            store(i, z).wait()
        return carry

    lax.fori_loop(0, nz, stored, 0)


def body(sizes, pressure, porosity, lithology, layer_solid):
    nz, nx, ny = pressure.shape
    f32, i32 = jnp.float32, jnp.int32
    shaped = jax.ShapeDtypeStruct
    block, plane = (nz, nx, ny), (nx, ny)
    padded = (nz + 2, nx + 2 * PAD, ny)
    z_face, x_face, y_face = (2, nx, ny), (2, nz, ny), (2, nx, 128)
    vmem = pl.BlockSpec(memory_space=pltpu.VMEM)
    hbm = pl.BlockSpec(memory_space=pltpu.HBM)
    held = (shaped(block, f32), shaped(block, f32), shaped(block, i32), shaped(plane, f32),
            shaped(y_face, f32), shaped((nz, 8, 128), f32))
    held = pl.pallas_call(
        functools.partial(exchange, sizes),
        out_shape=held,
        in_specs=[hbm] * 4,
        out_specs=(vmem,) * len(held),
        scratch_shapes=[pltpu.VMEM(shape, f32) for shape in (
            padded, padded, padded, (nz + 1, nx, ny), (nz, nx + PAD, ny),
            block, block, block, plane, plane,
            (2, 2 * nz, ny), (2, 2 * nz, ny), y_face, y_face, z_face, z_face, z_face,
            x_face, x_face, y_face, y_face, z_face, x_face, y_face, y_face, y_face)] + [
            pltpu.SMEM((nz,), f32),
            pltpu.SemaphoreType.DMA((4,)),
            pltpu.SemaphoreType.DMA((MESSAGES,)),
            pltpu.SemaphoreType.DMA((MESSAGES,)),
        ],
        compiler_params=pltpu.CompilerParams(
            collective_id=0, has_side_effects=True, vmem_limit_bytes=24 * 2**20),
        name="exchange",
    )(*(pltpu.with_memory_space_constraint(a, pltpu.HBM) for a in (pressure, porosity, lithology, layer_solid)))
    return pl.pallas_call(
        finish,
        out_shape=(shaped(block, f32),) * 3,
        in_specs=[vmem] * len(held),
        out_specs=(hbm,) * 3,
        scratch_shapes=[
            pltpu.VMEM((3,) + block, f32),
            pltpu.SemaphoreType.DMA((3, nz)),
        ],
        compiler_params=pltpu.CompilerParams(vmem_limit_bytes=24 * 2**20),
        name="finish",
    )(*held)


def solution(mesh):
    sizes = dict(mesh.shape)
    spec = P("slab", "mapx", "mapy")
    return jax.shard_map(
        functools.partial(body, sizes), mesh=mesh,
        in_specs=(spec, spec, spec, P("slab")), out_specs=(spec, spec, spec), check_vma=False)
```

```python
import functools
import math

import jax
import jax.numpy as jnp
from jax import lax
from jax.experimental import pallas as pl
from jax.experimental.pallas import tpu as pltpu
from jax.sharding import PartitionSpec as P

PHI_SURFACE = (0.45, 0.55, 0.65, 0.4)
ATHY_RATE = (0.25, 0.45, 0.8, 0.35)
MOB_BASE = (1.0, 0.0, -1.5, -0.5)
MOB_SLOPE = (6.0, 5.0, 8.0, 4.0)
GRAIN_DENSITY = (2.65, 2.68, 2.72, 2.71)
WATER_DENSITY = 1.03
SPECTRUM_MID = 1.0
SPECTRUM_HALF = 0.95
SIGMA_RATIO = SPECTRUM_MID / SPECTRUM_HALF
RHO_FIRST = 1.0 / SIGMA_RATIO
RHO_SECOND = 1.0 / (2.0 * SIGMA_RATIO - RHO_FIRST)
STEP_KEEP = RHO_SECOND * RHO_FIRST
STEP_RES = 2.0 * RHO_SECOND / SPECTRUM_HALF

LOG2_E = 1.0 / math.log(2.0)

HALF_BASE = tuple(-(b - 0.35 * s) * LOG2_E - 1.0 for b, s in zip(MOB_BASE, MOB_SLOPE))
HALF_SLOPE = tuple(-s * LOG2_E for s in MOB_SLOPE)
GRAIN_LESS = tuple(g - WATER_DENSITY for g in GRAIN_DENSITY)
ATHY_NEG = tuple(-a * LOG2_E for a in ATHY_RATE)
OUTSIDE = 2.0e38

MESH = pl.DeviceIdType.MESH
PAD = 8
ROWS = 16
Z_P, Z_H, X_1, Y_1, Z_Q, X_Q, Y_Q, CHAIN = 0, 2, 4, 6, 8, 10, 12, 14
MESSAGES = 15


def rec(x):
    return pl.reciprocal(x, approx=True)


def classes(lith):
    return lith >= 2, (lith & 1) == 1


def pick(cls, table):
    high, odd = cls
    a, b, c, d = (jnp.float32(t) for t in table)
    return jnp.where(high, jnp.where(odd, d, c), jnp.where(odd, b, a))


def shifted(value, up):
    rows, ny = value.shape
    lane = lax.broadcasted_iota(jnp.int32, (rows, 128), 1)
    parts = [pltpu.roll(value[:, y:y + 128], 1 if up else 127, 1) for y in range(0, ny, 128)]
    if up:
        joined = [jnp.where(lane == 0, a, b) for a, b in zip(parts[-1:] + parts[:-1], parts)]
    else:
        joined = [jnp.where(lane == 127, a, b) for a, b in zip(parts[1:] + parts[:1], parts)]
    return jnp.concatenate(joined, axis=1)


def at_edges(halo, index, rows, ny):
    lo = pltpu.roll(halo[0, rows, :], lax.rem(128 - index, 128), 1)
    hi = pltpu.roll(halo[1, rows, :], 127 - index, 1)
    lane = lax.broadcasted_iota(jnp.int32, lo.shape, 1)
    zeros = [jnp.zeros(lo.shape, jnp.float32)] * (ny // 128 - 2)
    ends = [jnp.where(lane == 0, lo, 0.0)] + zeros + [jnp.where(lane == 127, hi, 0.0)]
    return jnp.concatenate(ends, axis=1)


def exchange(sizes, p_hbm, por_hbm, lit_hbm, solid_hbm,
             part, ob, lit, above, y_term, solid_wide,
             pv, qv, hv, tz, tx, ty, rd, por, col, col_send, xs, xr, ys, yr,
             zpr, zhr, zqr, xqs, xqr, yqs, yqr, z_link, x_link, y_link, y_flow, edge,
             solid, load_sem, send_sem, recv_sem):
    nz, nx, ny = por.shape
    axes = ("slab", "mapx", "mapy")
    me = {a: lax.axis_index(a) for a in axes}
    has_lo = {a: me[a] > 0 for a in axes}
    has_hi = {a: me[a] < sizes[a] - 1 for a in axes}
    peers = sum(jnp.where(f, 1, 0) for flags in (has_lo, has_hi) for f in flags.values())
    inner = pl.ds(PAD, nx)

    loads = [
        pltpu.make_async_copy(por_hbm, por, load_sem.at[0]),
        pltpu.make_async_copy(lit_hbm, lit, load_sem.at[1]),
        pltpu.make_async_copy(p_hbm, pv.at[pl.ds(1, nz), inner, :], load_sem.at[2]),
        pltpu.make_async_copy(solid_hbm, solid, load_sem.at[3]),
    ]
    for c in loads:
        c.start()

    barrier = pltpu.get_barrier_semaphore()
    for a in axes:
        @pl.when(has_lo[a])
        def _():
            pl.semaphore_signal(barrier, inc=1, device_id={a: me[a] - 1}, device_id_type=MESH)

        @pl.when(has_hi[a])
        def _():
            pl.semaphore_signal(barrier, inc=1, device_id={a: me[a] + 1}, device_id_type=MESH)

    def message(k, axis, up, src, dst):
        target = me[axis] + 1 if up else me[axis] - 1
        return pltpu.make_async_remote_copy(
            src_ref=src, dst_ref=dst, send_sem=send_sem.at[k], recv_sem=recv_sem.at[k],
            device_id={axis: target}, device_id_type=MESH)

    def pair(k, axis, src_up, dst_up, src_down, dst_down):
        return [(k, axis, True, src_up, dst_up), (k + 1, axis, False, src_down, dst_down)]

    z_lo, z_hi = 0, nz + 1
    groups = {
        Z_P: pair(Z_P, "slab", p_hbm.at[nz - 1], zpr.at[0], p_hbm.at[0], zpr.at[1]),
        Z_H: pair(Z_H, "slab", hv.at[nz, inner, :], zhr.at[0], hv.at[1, inner, :], zhr.at[1]),
        X_1: pair(X_1, "mapx", xs.at[0], xr.at[0], xs.at[1], xr.at[1]),
        Y_1: pair(Y_1, "mapy", ys.at[0], yr.at[0], ys.at[1], yr.at[1]),
        Z_Q: pair(Z_Q, "slab", qv.at[nz, inner, :], zqr.at[0], qv.at[1, inner, :], zqr.at[1]),
        X_Q: pair(X_Q, "mapx", xqs.at[0], xqr.at[0], xqs.at[1], xqr.at[1]),
        Y_Q: pair(Y_Q, "mapy", yqs.at[0], yqr.at[0], yqs.at[1], yqr.at[1]),
    }

    def start(group):
        for k, axis, up, src, dst in groups[group]:
            @pl.when(has_hi[axis] if up else has_lo[axis])
            def _():
                message(k, axis, up, src, dst).start()

    def arrived(group):
        for k, axis, up, src, dst in groups[group]:
            @pl.when(has_lo[axis] if up else has_hi[axis])
            def _():
                message(k, axis, up, src, dst).wait_recv()

    def sent(group):
        for k, axis, up, src, dst in groups[group]:
            @pl.when(has_hi[axis] if up else has_lo[axis])
            def _():
                message(k, axis, up, src, dst).wait_send()

    lane_y = lax.broadcasted_iota(jnp.int32, (nx, 128), 1)

    for layer in (z_lo, z_hi):
        pv[layer, inner, :] = jnp.zeros((nx, ny), jnp.float32)
        qv[layer, inner, :] = jnp.zeros((nx, ny), jnp.float32)
        hv[layer, inner, :] = jnp.full((nx, ny), OUTSIDE, jnp.float32)
    tz[0] = jnp.zeros((nx, ny), jnp.float32)
    for z in range(nz):
        for row in (PAD - 1, PAD + nx):
            pv[z + 1, pl.ds(row, 1), :] = jnp.zeros((1, ny), jnp.float32)
            qv[z + 1, pl.ds(row, 1), :] = jnp.zeros((1, ny), jnp.float32)
            hv[z + 1, pl.ds(row, 1), :] = jnp.full((1, ny), OUTSIDE, jnp.float32)

    for side, flags in ((0, has_lo), (1, has_hi)):
        @pl.when(jnp.logical_not(flags["slab"]))
        def _():
            zpr[side] = jnp.zeros((nx, ny), jnp.float32)
            zqr[side] = jnp.zeros((nx, ny), jnp.float32)
            zhr[side] = jnp.full((nx, ny), OUTSIDE, jnp.float32)
            if side == 0:
                above[...] = jnp.zeros((nx, ny), jnp.float32)

        @pl.when(jnp.logical_not(flags["mapx"]))
        def _():
            xr[side, pl.ds(0, nz), :] = jnp.zeros((nz, ny), jnp.float32)
            xr[side, pl.ds(nz, nz), :] = jnp.full((nz, ny), OUTSIDE, jnp.float32)
            xqr[side] = jnp.zeros((nz, ny), jnp.float32)

        @pl.when(jnp.logical_not(flags["mapy"]))
        def _():
            yr[side] = jnp.where(lane_y < nz, jnp.float32(0.0), jnp.float32(OUTSIDE))
            yqr[side] = jnp.zeros((nx, 128), jnp.float32)

    loads[0].wait()
    loads[1].wait()

    def half_inverse(z):
        for r in range(0, nx, 32):
            rows = pl.ds(r, 32)
            cls = classes(lit[z, rows, :])
            hv[z + 1, pl.ds(PAD + r, 32), :] = jnp.exp2(
                pick(cls, HALF_BASE) + pick(cls, HALF_SLOPE) * por[z, rows, :])

    lax.fori_loop(0, nz, lambda z, c: (half_inverse(z), c)[1], 0)
    loads[2].wait()

    def face_x(src, dst, offset):
        for side, row in ((0, PAD + nx - 1), (1, PAD)):
            for z in range(nz):
                dst[side, pl.ds(offset + z, 1), :] = src[z + 1, pl.ds(row, 1), :]

    def face_y(srcs, dst, first_z=1, first_row=PAD):
        for side in range(2):
            for r in range(0, nx, 32):
                acc = jnp.zeros((32, 128), jnp.float32)
                lane = lane_y[:32]
                for i, src in enumerate(srcs):
                    for z in range(nz):
                        k = i * nz + z
                        lanes = pl.ds(0 if side else ny - 128, 128)
                        column = src[z + first_z, pl.ds(first_row + r, 32), lanes]
                        shift = k if side else k + 1
                        moved = pltpu.roll(column, shift, 1) if shift else column
                        acc = jnp.where(lane == k, moved, acc)
                dst[side, pl.ds(r, 32), :] = acc

    face_x(pv, xs, 0)
    face_x(hv, xs, nz)
    face_y((pv, hv), ys)
    pl.semaphore_wait(barrier, peers)
    for group in (X_1, Y_1, Z_H, Z_P):
        start(group)

    loads[3].wait()
    for r in range(0, nx, 32):
        rows = pl.ds(r, 32)

        def add_layer(z, total):
            cls = classes(lit[z, rows, :])
            load = (pick(cls, GRAIN_LESS) + WATER_DENSITY * rec(1.0 - por[z, rows, :])) * solid[z]
            ob[z, rows, :] = total + 0.5 * load
            return total + load

        col[rows, :] = lax.fori_loop(0, nz, add_layer, jnp.zeros((32, ny), jnp.float32))

    def chain(src):
        return message(CHAIN, "slab", True, src, above)

    @pl.when(me["slab"] == 0)
    def _():
        col_send[...] = col[...]
        chain(col_send).start()

    def forward():
        chain(col_send).wait_recv()
        col_send[...] = col[...] + above[...]
        chain(col_send).start()

    def first(z, carry):
        for r in range(0, nx, ROWS):
            at = lambda ref, dz, dx: ref[z + 1 + dz, pl.ds(PAD + r + dx, ROWS), :]
            rows = pl.ds(r, ROWS)
            h, p = at(hv, 0, 0), at(pv, 0, 0)
            t_zm, t_zp = tz[z, rows, :], rec(h + at(hv, 1, 0))
            t_xm, t_xp = rec(h + at(hv, 0, -1)), rec(h + at(hv, 0, 1))
            last = lax.broadcasted_iota(jnp.int32, h.shape, 1) == ny - 1
            t_yp = jnp.where(last, 0.0, rec(h + shifted(h, False)))
            t_ym = shifted(t_yp, True)
            tz[z + 1, rows, :] = t_zp
            tx[z, rows, :] = t_xm
            if r + ROWS == nx:
                tx[z, pl.ds(nx, 1), :] = t_xp[ROWS - 1:, :]
            ty[z, rows, :] = t_yp
            rd[z, rows, :] = 1.0 + ((t_zm + t_zp) + (t_xm + t_xp) + (t_ym + t_yp))
            part[z, rows, :] = (
                p + (t_zm * at(pv, -1, 0) + t_zp * at(pv, 1, 0))
                + (t_xm * at(pv, 0, -1) + t_xp * at(pv, 0, 1))
                + (shifted(t_yp * p, True) + t_yp * shifted(p, False)))
        return carry

    lax.fori_loop(0, nz // 2, first, 0)

    @pl.when(me["slab"] == 1)
    def _():
        forward()

    lax.fori_loop(nz // 2, nz, first, 0)

    x_rows = ((0, 0), (1, nx - 1))
    arrived(X_1)
    for side, row in x_rows:
        link = rec(xs[1 - side, pl.ds(nz, nz), :] + xr[side, pl.ds(nz, nz), :])
        x_link[side] = link
        flow = link * xr[side, pl.ds(0, nz), :]
        for z in range(nz):
            one = pl.ds(row, 1)
            rd[z, one, :] += link[z:z + 1, :]
            part[z, one, :] += flow[z:z + 1, :]
    arrived(Y_1)
    for side in range(2):
        link = pltpu.roll(rec(ys[1 - side] + yr[side]), 128 - nz, 1)
        link = jnp.where(lane_y < nz, link, 0.0)
        y_link[side] = link
        y_flow[side] = link * yr[side]
    def divide(z):
        for r in range(0, nx, 32):
            rows = pl.ds(r, 32)
            inv = rec(rd[z, rows, :] + at_edges(y_link, z, rows, ny))
            rd[z, rows, :] = STEP_RES * inv
            qv[z + 1, pl.ds(PAD + r, 32), :] = inv * (
                part[z, rows, :] + at_edges(y_flow, z, rows, ny))

    lax.fori_loop(1, nz - 1, lambda z, c: (divide(z), c)[1], 0)
    arrived(Z_H)
    arrived(Z_P)
    for side, z in ((0, 0), (1, nz - 1)):
        for r in range(0, nx, 32):
            rows = pl.ds(r, 32)
            link = rec(hv[z + 1, pl.ds(PAD + r, 32), :] + zhr[side, rows, :])
            z_link[side, rows, :] = link
            rd[z, rows, :] += link
            part[z, rows, :] += link * zpr[side, rows, :]

    divide(0)
    divide(nz - 1)
    start(Z_Q)
    face_x(qv, xqs, 0)
    start(X_Q)
    face_y((qv,), yqs)
    start(Y_Q)

    face_y((rd,), edge, 0, 0)
    for side in range(2):
        y_link[side] = y_link[side] * edge[1 - side]

    @pl.when(me["slab"] == 2)
    def _():
        forward()

    def second(z, carry):
        for r in range(0, nx, ROWS):
            at = lambda ref, dz, dx: ref[z + 1 + dz, pl.ds(PAD + r + dx, ROWS), :]
            rows = pl.ds(r, ROWS)
            p, q = at(pv, 0, 0), at(qv, 0, 0)
            t_yp = ty[z, rows, :]
            total = (p + (tz[z, rows, :] * at(qv, -1, 0) + tz[z + 1, rows, :] * at(qv, 1, 0))
                     + (tx[z, rows, :] * at(qv, 0, -1) + tx[z, pl.ds(r + 1, ROWS), :] * at(qv, 0, 1))
                     + (shifted(t_yp * q, True) + t_yp * shifted(q, False)))
            part[z, rows, :] = q + STEP_KEEP * (q - p) + (total * rd[z, rows, :] - STEP_RES * q)
        return carry

    lax.fori_loop(0, nz, second, 0)

    arrived(X_Q)
    for side, row in x_rows:
        flow = x_link[side] * xqr[side]
        for z in range(nz):
            one = pl.ds(row, 1)
            part[z, one, :] += rd[z, one, :] * flow[z:z + 1, :]
    arrived(Y_Q)
    for side in range(2):
        y_term[side] = y_link[side] * yqr[side]
    arrived(Z_Q)
    for side, z in ((0, 0), (1, nz - 1)):
        for r in range(0, nx, 32):
            rows = pl.ds(r, 32)
            part[z, rows, :] += rd[z, rows, :] * z_link[side, rows, :] * zqr[side, rows, :]
    for z in range(nz):
        solid_wide[z] = jnp.full((8, 128), solid[z], jnp.float32)

    @pl.when(me["slab"] == 3)
    def _():
        chain(col_send).wait_recv()

    for group in groups:
        sent(group)

    @pl.when(has_hi["slab"])
    def _():
        chain(col_send).wait_send()


def finish(part, ob, lit, above, y_term, solid_wide, pn_out, phi_out, thick_out, buf, store_sem):
    nz, nx, ny = lit.shape
    outs = (pn_out, phi_out, thick_out)

    def store(i, z):
        return pltpu.make_async_copy(buf.at[i, z], outs[i].at[z], store_sem.at[i, z])

    def layer(z, carry):
        solid = jnp.concatenate([solid_wide[z]] * (ny // 128), axis=1)
        solid = jnp.concatenate([solid] * (ROWS // 8), axis=0)
        for r in range(0, nx, ROWS):
            rows = pl.ds(r, ROWS)
            pn = part[z, rows, :] + at_edges(y_term, z, rows, ny)
            stress = jnp.maximum(above[rows, :] + ob[z, rows, :] - pn, 0.0)
            cls = classes(lit[z, rows, :])
            phi = pick(cls, PHI_SURFACE) * jnp.exp2(pick(cls, ATHY_NEG) * stress)
            buf[0, z, rows, :] = pn
            buf[1, z, rows, :] = phi
            buf[2, z, rows, :] = solid * rec(1.0 - phi)
        for i in range(3):
            store(i, z).start()
        return carry

    lax.fori_loop(0, nz, layer, 0)

    def stored(z, carry):
        for i in range(3):
            store(i, z).wait()
        return carry

    lax.fori_loop(0, nz, stored, 0)


def body(sizes, pressure, porosity, lithology, layer_solid):
    nz, nx, ny = pressure.shape
    f32, i32 = jnp.float32, jnp.int32
    shaped = jax.ShapeDtypeStruct
    block, plane = (nz, nx, ny), (nx, ny)
    padded = (nz + 2, nx + 2 * PAD, ny)
    z_face, x_face, y_face = (2, nx, ny), (2, nz, ny), (2, nx, 128)
    vmem = pl.BlockSpec(memory_space=pltpu.VMEM)
    hbm = pl.BlockSpec(memory_space=pltpu.HBM)
    held = (shaped(block, f32), shaped(block, f32), shaped(block, i32), shaped(plane, f32),
            shaped(y_face, f32), shaped((nz, 8, 128), f32))
    held = pl.pallas_call(
        functools.partial(exchange, sizes),
        out_shape=held,
        in_specs=[hbm] * 4,
        out_specs=(vmem,) * len(held),
        scratch_shapes=[pltpu.VMEM(shape, f32) for shape in (
            padded, padded, padded, (nz + 1, nx, ny), (nz, nx + PAD, ny),
            block, block, block, plane, plane,
            (2, 2 * nz, ny), (2, 2 * nz, ny), y_face, y_face, z_face, z_face, z_face,
            x_face, x_face, y_face, y_face, z_face, x_face, y_face, y_face, y_face)] + [
            pltpu.SMEM((nz,), f32),
            pltpu.SemaphoreType.DMA((4,)),
            pltpu.SemaphoreType.DMA((MESSAGES,)),
            pltpu.SemaphoreType.DMA((MESSAGES,)),
        ],
        compiler_params=pltpu.CompilerParams(
            collective_id=0, has_side_effects=True, vmem_limit_bytes=24 * 2**20),
        name="exchange",
    )(*(pltpu.with_memory_space_constraint(a, pltpu.HBM) for a in (pressure, porosity, lithology, layer_solid)))
    return pl.pallas_call(
        finish,
        out_shape=(shaped(block, f32),) * 3,
        in_specs=[vmem] * len(held),
        out_specs=(hbm,) * 3,
        scratch_shapes=[
            pltpu.VMEM((3,) + block, f32),
            pltpu.SemaphoreType.DMA((3, nz)),
        ],
        compiler_params=pltpu.CompilerParams(vmem_limit_bytes=24 * 2**20),
        name="finish",
    )(*held)


def solution(mesh):
    sizes = dict(mesh.shape)
    spec = P("slab", "mapx", "mapy")
    return jax.shard_map(
        functools.partial(body, sizes), mesh=mesh,
        in_specs=(spec, spec, spec, P("slab")), out_specs=(spec, spec, spec), check_vma=False)
```
